32 devices in a mesh: seq: 8 (over y, x, core), fsdp: 4 (over z).
Axes of the slice: x: 2, y: 2, z: 4, core: 2. Of those that a mesh axis runs over, the one named last changes fastest.
Arguments:
- tokens: bfloat16 [4096, 2048], P(('seq', 'fsdp')), may hold values from -6 to 6
- attn_qkv: bfloat16 [2048, 6144], P(('seq', 'fsdp')), may hold values from -0.125 to 0.125
- attn_out_t: bfloat16 [2048, 2048], P(('seq', 'fsdp')), may hold values from -4 to 4
- mlp_weight: bfloat16 [8192, 6144], P(('seq', 'fsdp')), may hold values from -0.125 to 0.125
- norm1: bfloat16 [2048], P(('seq', 'fsdp')), may hold values from 0.099609375 to 1.8984375
- norm2: bfloat16 [2048], P(('seq', 'fsdp')), may hold values from 0.099609375 to 1.8984375
- cotangent: bfloat16 [4096, 2048], P(('seq', 'fsdp')), may hold values from -6 to 6
Outputs:
- output: bfloat16 [4096, 2048], P(('seq', 'fsdp'))
- grad_tokens: float32 [4096, 2048], P(('seq', 'fsdp'))
- grad_attn_qkv: float32 [2048, 6144], P(('seq', 'fsdp'))
- grad_attn_out_t: float32 [2048, 2048], P(('seq', 'fsdp'))
- grad_mlp_weight: float32 [8192, 6144], P(('seq', 'fsdp'))
- grad_norm1: float32 [2048], P(('seq', 'fsdp'))
- grad_norm2: float32 [2048], P(('seq', 'fsdp'))
The draws below stay inside these ranges and needn't reach their ends.
All inputs are finite; a program needn't handle non-finite values.
Results may differ from the reference program's by a relative error of at most 0.015.
Values may be sent and summed in bfloat16 or wider, within the bound.
No kernel may reach another device: no remote copies, remote signals or barrier semaphores. Data moves between devices by JAX's collectives and lax.ppermute only.
A program may use at most 768 MiB of HBM per device.

```python
import jax
import jax.numpy as jnp
from jax import lax

D = 2048
HEADS = 32
FF = 8192
HEAD_DIM = 64
SEQ_LEN = 4096


def raised(drawn, rng, source, target, blocks, factor):
    owner, partner = [(jnp.arange(drawn.shape[position]) // (drawn.shape[position] // blocks)).reshape([-1 if axis == position else 1 for axis in range(drawn.ndim)]) for position in (source, target)]
    chosen = jax.random.permutation(rng, blocks)[partner]
    strong = (owner == chosen) | (owner == (partner + blocks // 2) % blocks)
    return jnp.where(strong, factor * drawn, drawn)


def steps_of(rng, shape, cuts, smallest, top_value):
    level, own = 1.0, jax.random.fold_in(rng, 6)
    for axis_at, parts in cuts:
        steps = jnp.exp(jax.random.uniform(jax.random.fold_in(own, axis_at), (parts,), jnp.float32, smallest / len(cuts), top_value / len(cuts)))
        level = level * jnp.repeat(steps, shape[axis_at] // parts).reshape([-1 if axis == axis_at else 1 for axis in range(len(shape))])
    return level


def scatter_about(key, extent, scale, limit, shards=(), kind=jnp.bfloat16):
    loudness = steps_of(key, extent, shards, -0.22, 0.18) if shards else 1.0
    values = jax.random.normal(key, extent, jnp.float32) * scale * loudness
    return jnp.minimum(jnp.maximum(values, -limit), limit).astype(kind)


def noise_with(stream_key, extent, deviation, bound, cuts, heavy, kind=jnp.bfloat16):
    array = deviation * jax.random.normal(stream_key, extent, jnp.float32)
    if cuts:
        array = array * steps_of(stream_key, extent, cuts, -0.22, 0.18)
    return jnp.clip(raised(array, jax.random.fold_in(stream_key, 3), *heavy), -bound, bound).astype(kind)


def setup_inputs(seed: int = 0) -> dict:
    seeds = jax.random.split(jax.random.key(seed), 8)
    return {
        "tokens": scatter_about(seeds[0], (SEQ_LEN, D), 1.0, 6.0, ((0, 32),)),
        "attn_qkv": scatter_about(seeds[1], (D, 3 * D), D ** -0.5, 0.125, ((0, 32),)),
        "attn_out_t": scatter_about(seeds[2], (D, D), (max(D // 1024, 1)) ** -0.5, 4.0, ((0, 32),)),
        "mlp_weight": scatter_about(seeds[3], (FF, 3 * D), D ** -0.5, 0.125, ((0, 32),)),
        "norm1": jnp.clip(1.0 + 0.18 * jax.random.normal(seeds[4], (D,), jnp.float32), 0.099609375, 1.8984375).astype(jnp.bfloat16),
        "norm2": jnp.clip(1.0 + 0.18 * jax.random.normal(seeds[5], (D,), jnp.float32), 0.099609375, 1.8984375).astype(jnp.bfloat16),
        "cotangent": noise_with(seeds[6], (SEQ_LEN, D), 1.0, 6.0, ((0, 32),), (0, 1, 32, 2.75)),
    }


epsilon = 1e-05
rope_base = 130000.0
highest = lax.Precision.HIGHEST

@jax.custom_vjp
def low(v):
    return lax.optimization_barrier(v.astype(jnp.bfloat16)).astype(jnp.float32)

@jax.custom_vjp
def low_back(v):
    return v

def low_keep(v):
    return (low(v), None)

def low_pass(kept, grad):
    return (grad,)

def back_keep(v):
    return (v, None)

def back_low(kept, grad):
    return (low(grad),)
low.defvjp(low_keep, low_pass)
low_back.defvjp(back_keep, back_low)

def matmul(left_side, right_side):
    return jnp.dot(left_side, right_side, precision=highest, preferred_element_type=jnp.float32)

def rms_norm(token_rows, gain_row):
    factor = lax.rsqrt(lax.optimization_barrier(jnp.mean(token_rows * token_rows, axis=-1, keepdims=True)) + epsilon)
    return token_rows * factor * gain_row

def rotary(vectors, positions):
    half_dim = HEAD_DIM // 2
    frequency = rope_base ** (-(jnp.arange(half_dim, dtype=jnp.float32) * 2.0) / HEAD_DIM)
    angles = positions.astype(jnp.float32)[:, None] * frequency[None, :]
    angles = jnp.concatenate([angles, angles], axis=1)
    cosine_table = jnp.cos(angles)[:, None, :]
    sine_table = jnp.sin(angles)[:, None, :]
    turned = jnp.concatenate([-vectors[..., half_dim:], vectors[..., :half_dim]], axis=-1)
    return vectors * cosine_table + turned * sine_table

def head_attention(pieces):
    query_head, key_head, value_head = pieces
    length = query_head.shape[0]
    block_rows = min(512, length)
    key_place = jnp.arange(length)

    def one_block(inputs):
        query_block, first_row = inputs
        scaled = low_back(matmul(query_block, key_head.T) * HEAD_DIM ** (-0.5))
        query_place = first_row + jnp.arange(block_rows)
        masked = jnp.where(key_place[None, :] <= query_place[:, None], scaled, -1e+30)
        probability = low(jax.nn.softmax(masked, axis=-1))
        return matmul(probability, value_head)
    starts = jnp.arange(length // block_rows) * block_rows
    blocks = lax.map(jax.checkpoint(one_block), (query_head.reshape(length // block_rows, block_rows, HEAD_DIM), starts))
    return blocks.reshape(length, HEAD_DIM)

def layer(token_rows, qkv_weight, out_weight, mlp_matrix, gain_one, gain_two):
    length = token_rows.shape[0]
    normed_one = low(rms_norm(token_rows, gain_one))
    qkv_raw = low_back(matmul(normed_one, qkv_weight)).reshape(length, 3, HEADS, HEAD_DIM)
    positions = jnp.arange(length)
    queries = low_back(low(rotary(qkv_raw[:, 0], positions)))
    key_rows = low_back(low(rotary(qkv_raw[:, 1], positions)))
    values = low_back(low(qkv_raw[:, 2]))
    heads_out = lax.map(jax.checkpoint(head_attention), (queries.transpose(1, 0, 2), key_rows.transpose(1, 0, 2), values.transpose(1, 0, 2)))
    attended = low_back(low(heads_out.transpose(1, 0, 2).reshape(length, D)))
    attn_branch = low_back(matmul(attended, out_weight.T))
    middle = token_rows + attn_branch
    normed_two = low(rms_norm(middle, gain_two))
    gate_part = low_back(matmul(normed_two, mlp_matrix[:, :D].T))
    up_part = low_back(matmul(normed_two, mlp_matrix[:, D:2 * D].T))
    activation = low(jax.nn.silu(gate_part) * up_part)
    mlp_branch = low_back(matmul(activation, mlp_matrix[:, 2 * D:]))
    return middle + mlp_branch

def reference(tokens, attn_qkv, attn_out_t, mlp_weight, norm1, norm2, cotangent):
    inputs = tuple((weight_array.astype(jnp.float32) for weight_array in (tokens, attn_qkv, attn_out_t, mlp_weight, norm1, norm2)))
    result, pullback = jax.vjp(layer, *inputs)
    gradients = pullback(cotangent.astype(jnp.float32))
    return (result.astype(jnp.bfloat16), gradients[0], gradients[1], gradients[2], gradients[3], gradients[4], gradients[5])
```

```python
import functools

import jax
import jax.numpy as jnp
from jax import lax
from jax.experimental import pallas as pl
from jax.experimental.pallas import tpu as pltpu
from jax.sharding import Mesh
from jax.sharding import PartitionSpec as P

HEADS = 32
epsilon = 1e-05
rope_base = 130000.0
f32 = jnp.float32
bf16 = jnp.bfloat16
ALL = ("r", "p", "c", "z")
GROUPS = ("r", "p")
TENSOR = ("c", "z")


def contract(left, right, left_dim, right_dim):
    return lax.dot_general(
        left, right, (((left_dim,), (right_dim,)), ((), ())), preferred_element_type=f32
    )


def causal(scores):
    keys = lax.broadcasted_iota(jnp.int32, scores.shape, 0)
    queries = lax.broadcasted_iota(jnp.int32, scores.shape, 1)
    return jnp.where(keys <= queries, scores, -1e30)


def forward_kernel(qkv_ref, out_ref, logsum_ref, keys, values_t, queries_t, *, block):
    chunks, rows = qkv_ref.shape[0], qkv_ref.shape[3]
    per_chunk = rows // block
    count = chunks * per_chunk
    head_dim = qkv_ref.shape[2]
    for number in range(count):
        chunk, part = divmod(number, per_chunk)
        span = slice(part * block, (part + 1) * block)
        queries_t[number] = qkv_ref[chunk, 0, :, span]
        keys[number] = qkv_ref[chunk, 1, :, span].T
        values_t[number] = qkv_ref[chunk, 2, :, span]

    def step(i, j, carry, diagonal):
        largest, total, result = carry
        scores = contract(keys[j], queries_t[i], 1, 0)
        if diagonal:
            scores = causal(scores)
        new_largest = jnp.maximum(largest, jnp.max(scores, axis=0, keepdims=True))
        shrink = jnp.exp(largest - new_largest)
        weights = jnp.exp(scores - new_largest)
        total = total * shrink + jnp.sum(weights, axis=0, keepdims=True)
        result = result * shrink + contract(values_t[j], weights.astype(bf16), 1, 0)
        return new_largest, total, result

    def query_block(i, _):
        carry = (
            jnp.full((1, block), -1e30, f32),
            jnp.zeros((1, block), f32),
            jnp.zeros((head_dim, block), f32),
        )
        carry = lax.fori_loop(0, i, lambda j, c: step(i, j, c, False), carry)
        largest, total, result = step(i, i, carry, True)
        out_ref[i] = (result / total).astype(bf16)
        logsum_ref[i] = largest + jnp.log(total)
        return 0

    lax.fori_loop(0, count, query_block, 0)


def backward_kernel(
    qkv_ref, grad_ref, out_ref, logsum_ref, result_ref,
    keys, queries, values, grads, keys_t, queries_t, grads_t, deltas, grad_queries,
    *, block, scale,
):
    chunks, rows = qkv_ref.shape[0], qkv_ref.shape[3]
    per_chunk = rows // block
    count = chunks * per_chunk
    head_dim = qkv_ref.shape[2]
    for number in range(count):
        chunk, part = divmod(number, per_chunk)
        span = slice(part * block, (part + 1) * block)
        queries_t[number] = qkv_ref[chunk, 0, :, span]
        keys_t[number] = qkv_ref[chunk, 1, :, span]
        queries[number] = qkv_ref[chunk, 0, :, span].T
        keys[number] = qkv_ref[chunk, 1, :, span].T
        values[number] = qkv_ref[chunk, 2, :, span].T
        grad = grad_ref[chunk, :, span]
        grads_t[number] = grad
        grads[number] = grad.T
        deltas[number] = jnp.sum(
            grad.astype(f32) * out_ref[number].astype(f32), axis=0, keepdims=True
        )
        grad_queries[number] = jnp.zeros((head_dim, block), f32)

    def step(i, j, carry, diagonal):
        grad_key, grad_value = carry
        scores = contract(keys[j], queries_t[i], 1, 0)
        if diagonal:
            scores = causal(scores)
        probs = jnp.exp(scores - logsum_ref[i])
        grad_value = grad_value + contract(probs.astype(bf16), grads[i], 1, 0)
        grad_probs = contract(values[j], grads_t[i], 1, 0)
        grad_scores = (probs * (grad_probs - deltas[i])).astype(bf16)
        grad_key = grad_key + contract(grad_scores, queries[i], 1, 0)
        grad_queries[i] = grad_queries[i] + contract(keys_t[j], grad_scores, 1, 0)
        return grad_key, grad_value

    for j in range(count):
        zero = jnp.zeros((block, head_dim), f32)
        carry = step(j, j, (zero, zero), True)
        grad_key, grad_value = lax.fori_loop(
            j + 1, count, lambda i, c, j=j: step(i, j, c, False), carry
        )
        chunk, part = divmod(j, per_chunk)
        span = slice(part * block, (part + 1) * block)
        result_ref[chunk, 1, :, span] = grad_key.T.astype(bf16)
        result_ref[chunk, 2, :, span] = grad_value.T.astype(bf16)
    for i in range(count):
        chunk, part = divmod(i, per_chunk)
        span = slice(part * block, (part + 1) * block)
        result_ref[chunk, 0, :, span] = (grad_queries[i] * scale).astype(bf16)


def attend_forward(qkv, block):
    chunks, _, head_dim, rows = qkv.shape
    count = chunks * rows // block
    pairs = count * (count + 1) // 2 * block * block
    in_vmem = pl.BlockSpec(memory_space=pltpu.VMEM)
    by_rows = pltpu.VMEM((count, block, head_dim), bf16)
    by_features = pltpu.VMEM((count, head_dim, block), bf16)
    return pl.pallas_call(
        functools.partial(forward_kernel, block=block),
        out_shape=(
            jax.ShapeDtypeStruct((count, head_dim, block), bf16),
            jax.ShapeDtypeStruct((count, 1, block), f32),
        ),
        in_specs=[in_vmem],
        out_specs=(in_vmem, in_vmem),
        scratch_shapes=[by_rows, by_features, by_features],
        compiler_params=pltpu.CompilerParams(vmem_limit_bytes=56 * 2**20),
        cost_estimate=pl.CostEstimate(
            flops=16 * pairs * head_dim, bytes_accessed=qkv.size * 3, transcendentals=pairs
        ),
        name="attend_forward",
    )(qkv)


def attend_backward(qkv, grad, out, logsum, block):
    chunks, _, head_dim, rows = qkv.shape
    count = chunks * rows // block
    pairs = count * (count + 1) // 2 * block * block
    in_vmem = pl.BlockSpec(memory_space=pltpu.VMEM)
    by_rows = pltpu.VMEM((count, block, head_dim), bf16)
    by_features = pltpu.VMEM((count, head_dim, block), bf16)
    return pl.pallas_call(
        functools.partial(backward_kernel, block=block, scale=head_dim**-0.5),
        out_shape=jax.ShapeDtypeStruct(qkv.shape, bf16),
        in_specs=[in_vmem] * 4,
        out_specs=in_vmem,
        scratch_shapes=[by_rows] * 4
        + [by_features] * 3
        + [pltpu.VMEM((count, 1, block), f32), pltpu.VMEM((count, head_dim, block), f32)],
        compiler_params=pltpu.CompilerParams(vmem_limit_bytes=60 * 2**20),
        cost_estimate=pl.CostEstimate(
            flops=32 * pairs * head_dim, bytes_accessed=qkv.size * 6, transcendentals=pairs
        ),
        name="attend_backward",
    )(qkv, grad, out, logsum)


def rotary_tables(positions, head_dim):
    half_dim = head_dim // 2
    frequency = rope_base ** (-(jnp.arange(half_dim, dtype=f32) * 2.0) / head_dim)
    angles = positions.astype(f32)[None, :] * frequency[:, None]
    return jnp.cos(angles), jnp.sin(angles)


def rotate(vectors, cosine, sine):
    half_dim = vectors.shape[-2] // 2
    first, second = vectors[..., :half_dim, :], vectors[..., half_dim:, :]
    return jnp.concatenate(
        [first * cosine - second * sine, second * cosine + first * sine], axis=-2
    )


def rotate_back(grads, cosine, sine):
    half_dim = grads.shape[-2] // 2
    first, second = grads[..., :half_dim, :], grads[..., half_dim:, :]
    return jnp.concatenate(
        [first * cosine + second * sine, second * cosine - first * sine], axis=-2
    )


def shards(tokens, attn_qkv, attn_out_t, mlp_weight, norm1, norm2, cotangent):
    rows, width = tokens.shape
    group_count, share_count = lax.axis_size("p"), lax.axis_size("r")
    tensor_count = lax.axis_size("c") * lax.axis_size("z")
    head_dim = width // HEADS
    heads_here = HEADS // tensor_count
    group_rows = rows * tensor_count
    features_here = heads_here * head_dim
    weight_rows = attn_qkv.shape[0]
    share = lax.axis_index("r")
    block = min(1024, group_rows)
    x = tokens.astype(f32)
    gain_one = norm1.astype(f32)[:, None]

    scaled_qkv = (attn_qkv.astype(f32) * gain_one).astype(bf16)
    qkv_cut = scaled_qkv.reshape(weight_rows, 3, tensor_count, features_here).transpose(2, 0, 1, 3)
    qkv_cut = qkv_cut.reshape(tensor_count, weight_rows, 3 * features_here)
    qkv_part = lax.all_to_all(qkv_cut, TENSOR, 0, 0).reshape(-1, 3 * features_here)
    qkv_weight = lax.all_gather(qkv_part, GROUPS, axis=0, tiled=True)
    x_group = lax.all_gather(tokens, TENSOR, axis=0, tiled=True).astype(f32)
    out_full = lax.all_gather(attn_out_t, ALL, axis=0, tiled=True)
    gain_two = lax.all_gather(norm2, ALL, axis=0, tiled=True).astype(f32)
    unit_weight = lax.all_gather(mlp_weight, GROUPS, axis=0, tiled=True)
    weight_gate = unit_weight[:, :width]
    weight_up = unit_weight[:, width : 2 * width]
    weight_down = unit_weight[:, 2 * width :]
    grad_out_group = lax.all_gather(cotangent, TENSOR, axis=0, tiled=True)

    factor_group = lax.rsqrt(jnp.mean(x_group * x_group, axis=-1, keepdims=True) + epsilon)
    unit_group = (x_group * factor_group).astype(bf16)
    group_index = share * group_count + lax.axis_index("p")
    positions = group_index * group_rows + jnp.arange(group_rows)
    cosine, sine = rotary_tables(positions, head_dim)
    projected = contract(qkv_weight, unit_group, 0, 1)
    projected = projected.reshape(3, heads_here, head_dim, group_rows)
    query_rows = rotate(projected[0], cosine, sine).astype(bf16) * bf16(head_dim**-0.5)
    key_rows = rotate(projected[1], cosine, sine).astype(bf16)
    stacked = jnp.stack([query_rows, key_rows, projected[2].astype(bf16)], axis=1)
    qkv = lax.all_to_all(stacked, "p", 0, 0)

    def over_shares(array):
        return lax.all_gather(array, "r", axis=0, tiled=True) if share_count > 1 else array

    def own_share(array):
        if share_count == 1:
            return array
        return lax.dynamic_slice_in_dim(array, share * group_count, group_count, 0)

    def by_chunk(blocks):
        blocks = blocks.reshape(share_count * group_count, -1, head_dim, block)
        return blocks.transpose(0, 2, 1, 3).reshape(-1, head_dim, group_rows)

    qkv = over_shares(qkv)
    attended, logsum = attend_forward(qkv, block)
    attended_head = own_share(by_chunk(attended))

    to_tokens = attended_head.reshape(group_count, head_dim, tensor_count, rows)
    to_tokens = to_tokens.transpose(0, 2, 1, 3).reshape(-1, head_dim, rows)
    attended_local = lax.all_to_all(to_tokens, ("p", "c", "z"), 0, 0)
    attended_local = attended_local.reshape(group_count, tensor_count, head_dim, rows)
    attended_local = attended_local.transpose(1, 0, 2, 3).reshape(width, rows)
    middle = x + contract(attended_local, out_full, 0, 1)
    attended_group = lax.all_to_all(attended_head, "p", 0, 0).reshape(features_here, group_rows)

    factor_two = lax.rsqrt(jnp.mean(middle * middle, axis=-1, keepdims=True) + epsilon)
    unit_two = middle * factor_two
    normed_two = (unit_two * gain_two).astype(bf16)
    normed_group = lax.all_gather(normed_two, TENSOR, axis=0, tiled=True)
    gate = contract(normed_group, weight_gate, 1, 1)
    up = contract(normed_group, weight_up, 1, 1)
    sigmoid = jax.nn.sigmoid(gate)
    silu = gate * sigmoid
    activation = (silu * up).astype(bf16)
    grad_act = contract(grad_out_group, weight_down, 1, 1)
    grad_gate = (grad_act * up * sigmoid * (1.0 + gate * (1.0 - sigmoid))).astype(bf16)
    grad_up = (grad_act * silu).astype(bf16)
    grad_normed_part = contract(grad_gate, weight_gate, 1, 0) + contract(grad_up, weight_up, 1, 0)
    grad_normed = lax.psum_scatter(
        grad_normed_part.astype(bf16), TENSOR, scatter_dimension=0, tiled=True
    ).astype(f32)
    branch_part = contract(activation, weight_down, 1, 0).astype(bf16)
    branch = lax.psum_scatter(branch_part, TENSOR, scatter_dimension=0, tiled=True)
    result = (middle + branch.astype(f32)).astype(bf16)
    weighted = grad_normed * gain_two
    grad_middle = (
        cotangent.astype(f32)
        + factor_two * weighted
        - middle * factor_two**3 * jnp.mean(weighted * middle, axis=-1, keepdims=True)
    )
    grad_norm_two = lax.psum_scatter(
        jnp.sum(grad_normed * unit_two, axis=0), ALL, scatter_dimension=0, tiled=True
    )
    unit_grads = jnp.concatenate(
        [
            contract(grad_gate, normed_group, 0, 0).astype(bf16),
            contract(grad_up, normed_group, 0, 0).astype(bf16),
            contract(activation, grad_out_group, 0, 0).astype(bf16),
        ],
        axis=1,
    )
    grad_mlp = lax.psum_scatter(unit_grads, GROUPS, scatter_dimension=0, tiled=True).astype(f32)

    grad_mid_low = grad_middle.astype(bf16)
    grad_attended = contract(out_full, grad_mid_low, 0, 1).astype(bf16)
    grad_attended = grad_attended.reshape(tensor_count, group_count, head_dim, rows)
    grad_attended = grad_attended.transpose(1, 0, 2, 3).reshape(-1, head_dim, rows)
    grad_head = lax.all_to_all(grad_attended, ("p", "c", "z"), 0, 0)
    grad_head = grad_head.reshape(group_count, tensor_count, head_dim, rows)
    grad_head = grad_head.transpose(0, 2, 1, 3).reshape(group_count, head_dim, group_rows)
    grad_qkv_head = attend_backward(qkv, over_shares(grad_head), attended, logsum, block)
    grad_qkv_head = own_share(grad_qkv_head)
    grad_mid_group = lax.all_gather(grad_mid_low, TENSOR, axis=0, tiled=True)

    def to_owners(part, columns):
        own = lax.psum_scatter(part.astype(bf16), GROUPS, scatter_dimension=0, tiled=True)
        own = lax.all_to_all(own.reshape(tensor_count, -1, columns), TENSOR, 0, 0)
        return own.astype(f32)

    out_term = contract(grad_mid_group, attended_group, 0, 1)
    grad_out_w = to_owners(out_term, features_here).transpose(1, 0, 2).reshape(-1, width)

    grad_qkv_rows = lax.all_to_all(grad_qkv_head, "p", 0, 0).astype(f32)
    grad_qkv_rows = jnp.stack(
        [
            rotate_back(grad_qkv_rows[:, 0], cosine, sine),
            rotate_back(grad_qkv_rows[:, 1], cosine, sine),
            grad_qkv_rows[:, 2],
        ]
    )
    grad_qkv_low = grad_qkv_rows.reshape(3 * features_here, group_rows).astype(bf16)
    weighted_part = contract(grad_qkv_low, qkv_weight, 0, 1)
    weighted_one = lax.psum_scatter(
        weighted_part.astype(bf16), TENSOR, scatter_dimension=0, tiled=True
    ).astype(f32)
    factor_one = lax.rsqrt(jnp.mean(x * x, axis=-1, keepdims=True) + epsilon)
    grad_tokens = (
        grad_middle
        + factor_one * weighted_one
        - x * factor_one**3 * jnp.mean(weighted_one * x, axis=-1, keepdims=True)
    )
    qkv_term = contract(unit_group, grad_qkv_low, 0, 1)
    qkv_sum = to_owners(qkv_term, 3 * features_here)
    qkv_sum = qkv_sum.reshape(tensor_count, weight_rows, 3, features_here)
    qkv_sum = qkv_sum.transpose(1, 2, 0, 3).reshape(weight_rows, 3 * width)
    grad_qkv = gain_one * qkv_sum
    grad_norm_one = jnp.sum(attn_qkv.astype(f32) * qkv_sum, axis=1)
    return (result, grad_tokens, grad_qkv, grad_out_w, grad_mlp, grad_norm_one, grad_norm_two)


def solution(mesh):
    seq_count, fsdp_count = mesh.shape["seq"], mesh.shape["fsdp"]
    groups = seq_count // 2
    heads_here = HEADS // (2 * fsdp_count)
    dealt = min(groups, heads_here)
    fine = Mesh(mesh.devices.reshape(groups // dealt, dealt, 2, fsdp_count), ALL)
    by_rows, by_items = P(ALL, None), P(ALL)
    in_specs = (by_rows, by_rows, by_rows, by_rows, by_items, by_items, by_rows)
    out_specs = (by_rows, by_rows, by_rows, by_rows, by_rows, by_items, by_items)
    return jax.shard_map(shards, mesh=fine, in_specs=in_specs, out_specs=out_specs, check_vma=False)
```

```python
import functools

import jax
import jax.numpy as jnp
from jax import lax
from jax.experimental import pallas as pl
from jax.experimental.pallas import tpu as pltpu
from jax.sharding import Mesh
from jax.sharding import PartitionSpec as P

HEADS = 32
epsilon = 1e-05
rope_base = 130000.0
f32 = jnp.float32
bf16 = jnp.bfloat16
SHORT = pl.CostEstimate(flops=1000, bytes_accessed=1000, transcendentals=0)
ALL = ("r", "p", "c", "z")
GROUPS = ("r", "p")
TENSOR = ("c", "z")


def contract(left, right, left_dim, right_dim):
    return lax.dot_general(
        left, right, (((left_dim,), (right_dim,)), ((), ())), preferred_element_type=f32
    )


def causal(scores):
    keys = lax.broadcasted_iota(jnp.int32, scores.shape, 0)
    queries = lax.broadcasted_iota(jnp.int32, scores.shape, 1)
    return jnp.where(keys <= queries, scores, -1e30)


def forward_kernel(qkv_ref, out_ref, logsum_ref, keys, values_t, queries_t, *, block):
    pieces, _, head_dim, rows = qkv_ref.shape
    per_block = block // rows
    count = pieces // per_block
    for piece in range(pieces):
        number, part = divmod(piece, per_block)
        span = slice(part * rows, (part + 1) * rows)
        queries_t[number, :, span] = qkv_ref[piece, 0]
        keys[number, span, :] = qkv_ref[piece, 1].T
        values_t[number, :, span] = qkv_ref[piece, 2]

    def step(i, j, carry, diagonal):
        largest, total, result = carry
        scores = contract(keys[j], queries_t[i], 1, 0)
        if diagonal:
            scores = causal(scores)
        new_largest = jnp.maximum(largest, jnp.max(scores, axis=0, keepdims=True))
        shrink = jnp.exp(largest - new_largest)
        weights = jnp.exp(scores - new_largest)
        total = total * shrink + jnp.sum(weights, axis=0, keepdims=True)
        result = result * shrink + contract(values_t[j], weights.astype(bf16), 1, 0)
        return new_largest, total, result

    def query_block(i, _):
        carry = (
            jnp.full((1, block), -1e30, f32),
            jnp.zeros((1, block), f32),
            jnp.zeros((head_dim, block), f32),
        )
        carry = lax.fori_loop(0, i, lambda j, c: step(i, j, c, False), carry)
        largest, total, result = step(i, i, carry, True)
        result = (result / total).astype(bf16)
        for part in range(per_block):
            out_ref[i * per_block + part] = result[:, part * rows : (part + 1) * rows]
        logsum_ref[i] = largest + jnp.log(total)
        return 0

    lax.fori_loop(0, count, query_block, 0)


def backward_kernel(
    qkv_ref, grad_ref, out_ref, logsum_ref, result_ref,
    keys, queries, values, grads, keys_t, queries_t, grads_t, deltas, grad_queries,
    *, block, scale,
):
    pieces, _, head_dim, rows = qkv_ref.shape
    per_block = block // rows
    count = pieces // per_block
    for piece in range(pieces):
        number, part = divmod(piece, per_block)
        span = slice(part * rows, (part + 1) * rows)
        queries_t[number, :, span] = qkv_ref[piece, 0]
        keys_t[number, :, span] = qkv_ref[piece, 1]
        queries[number, span, :] = qkv_ref[piece, 0].T
        keys[number, span, :] = qkv_ref[piece, 1].T
        values[number, span, :] = qkv_ref[piece, 2].T
        grad = grad_ref[piece]
        grads_t[number, :, span] = grad
        grads[number, span, :] = grad.T
        deltas[number, :, span] = jnp.sum(
            grad.astype(f32) * out_ref[piece].astype(f32), axis=0, keepdims=True
        )
    for number in range(count):
        grad_queries[number] = jnp.zeros((head_dim, block), f32)

    def step(i, j, carry, diagonal):
        grad_key, grad_value = carry
        scores = contract(keys[j], queries_t[i], 1, 0)
        if diagonal:
            scores = causal(scores)
        probs = jnp.exp(scores - logsum_ref[i])
        grad_value = grad_value + contract(probs.astype(bf16), grads[i], 1, 0)
        grad_probs = contract(values[j], grads_t[i], 1, 0)
        grad_scores = (probs * (grad_probs - deltas[i])).astype(bf16)
        grad_key = grad_key + contract(grad_scores, queries[i], 1, 0)
        grad_queries[i] = grad_queries[i] + contract(keys_t[j], grad_scores, 1, 0)
        return grad_key, grad_value

    for j in range(count):
        zero = jnp.zeros((block, head_dim), f32)
        carry = step(j, j, (zero, zero), True)
        grad_key, grad_value = lax.fori_loop(
            j + 1, count, lambda i, c, j=j: step(i, j, c, False), carry
        )
        for part in range(per_block):
            span = slice(part * rows, (part + 1) * rows)
            result_ref[j * per_block + part, 1] = grad_key[span].T.astype(bf16)
            result_ref[j * per_block + part, 2] = grad_value[span].T.astype(bf16)
    for piece in range(pieces):
        number, part = divmod(piece, per_block)
        span = slice(part * rows, (part + 1) * rows)
        result_ref[piece, 0] = (grad_queries[number, :, span] * scale).astype(bf16)


def attend_forward(qkv, block):
    pieces, _, head_dim, rows = qkv.shape
    count = pieces * rows // block
    pairs = count * (count + 1) // 2 * block * block
    in_vmem = pl.BlockSpec(memory_space=pltpu.VMEM)
    by_rows = pltpu.VMEM((count, block, head_dim), bf16)
    by_features = pltpu.VMEM((count, head_dim, block), bf16)
    return pl.pallas_call(
        functools.partial(forward_kernel, block=block),
        out_shape=(
            jax.ShapeDtypeStruct((pieces, head_dim, rows), bf16),
            jax.ShapeDtypeStruct((count, 1, block), f32),
        ),
        in_specs=[in_vmem],
        out_specs=(in_vmem, in_vmem),
        scratch_shapes=[by_rows, by_features, by_features],
        compiler_params=pltpu.CompilerParams(vmem_limit_bytes=56 * 2**20),
        cost_estimate=SHORT,
        name="attend_forward",
    )(qkv)


def attend_backward(qkv, grad, out, logsum, block):
    pieces, _, head_dim, rows = qkv.shape
    count = pieces * rows // block
    pairs = count * (count + 1) // 2 * block * block
    in_vmem = pl.BlockSpec(memory_space=pltpu.VMEM)
    by_rows = pltpu.VMEM((count, block, head_dim), bf16)
    by_features = pltpu.VMEM((count, head_dim, block), bf16)
    return pl.pallas_call(
        functools.partial(backward_kernel, block=block, scale=head_dim**-0.5),
        out_shape=jax.ShapeDtypeStruct(qkv.shape, bf16),
        in_specs=[in_vmem] * 4,
        out_specs=in_vmem,
        scratch_shapes=[by_rows] * 4
        + [by_features] * 3
        + [pltpu.VMEM((count, 1, block), f32), pltpu.VMEM((count, head_dim, block), f32)],
        compiler_params=pltpu.CompilerParams(vmem_limit_bytes=60 * 2**20),
        cost_estimate=SHORT,
        name="attend_backward",
    )(qkv, grad, out, logsum)


def start_pieces(refs, table, starts_ref, whole, semaphores):
    copies = []
    for number, (which, first, rows) in enumerate(table):
        start = pl.multiple_of(starts_ref[number], rows)
        copy = pltpu.make_async_copy(
            refs[which].at[pl.ds(first, rows), pl.ds(0, whole.shape[1])],
            whole.at[pl.ds(start, rows), :],
            semaphores.at[number],
        )
        copy.start()
        copies.append(copy)
    return copies


def qkv_kernel(count, table, starts_ref, x_ref, cosine_ref, sine_ref, *refs):
    pieces, (unit_ref, out_ref), (weight, weight_t, semaphores) = refs[:count], refs[-5:-3], refs[-3:]
    heads, blocks, _, head_dim, rows = out_ref.shape
    half = head_dim // 2
    copies = start_pieces(pieces, table, starts_ref, weight, semaphores)
    for number in range(blocks):
        span = slice(number * rows, (number + 1) * rows)
        x = x_ref[span].astype(f32)
        factor = lax.rsqrt(jnp.mean(x * x, axis=-1, keepdims=True) + epsilon)
        unit_ref[span] = (x * factor).astype(bf16)
    for copy in copies:
        copy.wait()
    weight_t[...] = weight[...].T
    step = 2
    for first in range(0, blocks, step):
        span = slice(first * rows, (first + step) * rows)
        made = contract(weight_t[...], unit_ref[span], 1, 1)
        cosine, sine = cosine_ref[:, span], sine_ref[:, span]
        for kind in range(3):
            for head in range(heads):
                at = (kind * heads + head) * head_dim
                upper, lower = made[at : at + half], made[at + half : at + head_dim]
                if kind < 2:
                    upper, lower = upper * cosine - lower * sine, lower * cosine + upper * sine
                upper, lower = upper.astype(bf16), lower.astype(bf16)
                if kind == 0:
                    upper, lower = upper * bf16(head_dim**-0.5), lower * bf16(head_dim**-0.5)
                for part in range(step):
                    lanes = slice(part * rows, (part + 1) * rows)
                    out_ref[head, first + part, kind, :half] = upper[:, lanes]
                    out_ref[head, first + part, kind, half:] = lower[:, lanes]


IN_VMEM = pl.BlockSpec(memory_space=pltpu.VMEM)
IN_SMEM = pl.BlockSpec(memory_space=pltpu.SMEM)
ANYWHERE = pl.BlockSpec(memory_space=pl.ANY)


def project(x_group, cosine, sine, pieces, table, starts, heads, head_dim, rows):
    tokens, width = x_group.shape
    columns = pieces[0].shape[1]
    return pl.pallas_call(
        functools.partial(qkv_kernel, len(pieces), table),
        out_shape=(
            jax.ShapeDtypeStruct((tokens, width), bf16),
            jax.ShapeDtypeStruct((heads, tokens // rows, 3, head_dim, rows), bf16),
        ),
        in_specs=[IN_SMEM] + [IN_VMEM] * 3 + [ANYWHERE] * len(pieces),
        out_specs=(IN_VMEM, IN_VMEM),
        scratch_shapes=[
            pltpu.VMEM((width, columns), bf16),
            pltpu.VMEM((columns, width), bf16),
            pltpu.SemaphoreType.DMA((len(table),)),
        ],
        compiler_params=pltpu.CompilerParams(vmem_limit_bytes=48 * 2**20),
        cost_estimate=SHORT,
        name="project",
    )(starts, x_group, cosine, sine, *pieces)


def mid_kernel(count, table, groups, starts_ref, x_ref, attended_ref, *refs):
    pieces, (mid_ref, normed_ref, gain_ref) = refs[:count], refs[-6:-3]
    weight, attended, semaphores = refs[-3:]
    copies = start_pieces(pieces, table, starts_ref, weight, semaphores)
    _, head_dim, rows = attended_ref.shape
    width = x_ref.shape[1]
    tensor = HEADS // groups
    pair = 128 // head_dim
    for first in range(0, HEADS, pair):
        features = jnp.concatenate(
            [
                attended_ref[head % groups * tensor + head // groups]
                for head in range(first, first + pair)
            ]
        )
        attended[:, first * head_dim : (first + pair) * head_dim] = features.T
    for copy in copies:
        copy.wait()
    cut = min(512, width)
    for start in range(0, width, cut):
        span = slice(start, start + cut)
        gain_ref[:, span] = weight[span, width:].astype(f32).T[:1]
        mid_ref[:, span] = x_ref[:, span].astype(f32) + contract(
            attended[...], weight[span, :width], 1, 1
        )
    mid = mid_ref[...]
    factor = lax.rsqrt(jnp.mean(mid * mid, axis=-1, keepdims=True) + epsilon)
    normed_ref[...] = (mid * factor * gain_ref[...]).astype(bf16)


def finish_attention(x, attended, pieces, table, starts, groups):
    rows, width = x.shape
    return pl.pallas_call(
        functools.partial(mid_kernel, len(pieces), table, groups),
        out_shape=(
            jax.ShapeDtypeStruct((rows, width), f32),
            jax.ShapeDtypeStruct((rows, width), bf16),
            jax.ShapeDtypeStruct((1, width), f32),
        ),
        in_specs=[IN_SMEM] + [IN_VMEM] * 2 + [ANYWHERE] * len(pieces),
        out_specs=(IN_VMEM,) * 3,
        scratch_shapes=[
            pltpu.VMEM((width, pieces[0].shape[1]), bf16),
            pltpu.VMEM((rows, width), bf16),
            pltpu.SemaphoreType.DMA((len(table),)),
        ],
        compiler_params=pltpu.CompilerParams(vmem_limit_bytes=48 * 2**20),
        cost_estimate=SHORT,
        name="finish_attention",
    )(starts, x, attended, *pieces)


def grad_mid_kernel(count, table, groups, starts_ref, mid_ref, grad_ref, cotangent_ref, gain_ref, *refs):
    pieces, (grad_mid_ref, low_ref, gain_part_ref, out_ref) = refs[:count], refs[-6:-2]
    weight, semaphores = refs[-2:]
    copies = start_pieces(pieces, table, starts_ref, weight, semaphores)
    _, head_dim, rows = out_ref.shape
    width = mid_ref.shape[1]
    tensor = HEADS // groups
    pair = 128 // head_dim
    mid, grad = mid_ref[...], grad_ref[...]
    factor = lax.rsqrt(jnp.mean(mid * mid, axis=-1, keepdims=True) + epsilon)
    weighted = grad * gain_ref[...]
    inner = jnp.mean(weighted * mid, axis=-1, keepdims=True)
    grad_mid = (
        cotangent_ref[...].astype(f32) + factor * weighted - mid * (factor * factor * factor * inner)
    )
    grad_mid_ref[...] = grad_mid
    low_ref[...] = grad_mid.astype(bf16)
    gain_part_ref[...] = jnp.sum(grad * (mid * factor), axis=0, keepdims=True)
    for copy in copies:
        copy.wait()
    cut = min(512, width)
    for start in range(0, width, cut):
        made = contract(low_ref[...], weight[:, start : start + cut], 1, 0).astype(bf16)
        for at in range(0, cut, pair * head_dim):
            features = made[:, at : at + pair * head_dim].T
            for part in range(pair):
                head = (start + at) // head_dim + part
                out_ref[head % groups * tensor + head // groups] = features[
                    part * head_dim : (part + 1) * head_dim
                ]


def back_to_attention(mid, grad, cotangent, gain, pieces, table, starts, groups, head_dim):
    rows, width = mid.shape
    return pl.pallas_call(
        functools.partial(grad_mid_kernel, len(pieces), table, groups),
        out_shape=(
            jax.ShapeDtypeStruct((rows, width), f32),
            jax.ShapeDtypeStruct((rows, width), bf16),
            jax.ShapeDtypeStruct((1, width), f32),
            jax.ShapeDtypeStruct((HEADS, head_dim, rows), bf16),
        ),
        in_specs=[IN_SMEM] + [IN_VMEM] * 4 + [ANYWHERE] * len(pieces),
        out_specs=(IN_VMEM,) * 4,
        scratch_shapes=[
            pltpu.VMEM((width, width), bf16),
            pltpu.SemaphoreType.DMA((len(table),)),
        ],
        compiler_params=pltpu.CompilerParams(vmem_limit_bytes=48 * 2**20),
        cost_estimate=SHORT,
        name="back_to_attention",
    )(starts, mid, grad, cotangent, gain, *pieces)


def grads_kernel(count, table, starts_ref, spots_ref, grad_ref, cosine_ref, sine_ref, *refs):
    pieces, (low_ref, keep_ref, send_ref) = refs[:count], refs[-6:-3]
    weight, by_tokens, semaphores = refs[-3:]
    copies = start_pieces(pieces, table, starts_ref, weight, semaphores)
    heads, blocks, _, head_dim, rows = grad_ref.shape
    half = head_dim // 2
    for block in range(blocks):
        span = slice(block * rows, (block + 1) * rows)
        cosine, sine = cosine_ref[:, span], sine_ref[:, span]
        for kind in range(3):
            for head in range(heads):
                at = (kind * heads + head) * head_dim
                grad = grad_ref[head, block, kind]
                if kind < 2:
                    grad = grad.astype(f32)
                    upper, lower = grad[:half], grad[half:]
                    grad = jnp.concatenate(
                        [upper * cosine + lower * sine, lower * cosine - upper * sine]
                    ).astype(bf16)
                low_ref[at : at + head_dim, span] = grad
        by_tokens[block] = low_ref[:, span].T
    for copy in copies:
        copy.wait()
    width = weight.shape[0]
    cut = min(1024, width)
    for step in range(keep_ref.shape[0]):
        tokens = jnp.concatenate(
            [by_tokens[spots_ref[2 * step]], by_tokens[spots_ref[2 * step + 1]]]
        )
        for start in range(0, width, cut):
            part = contract(tokens, weight[start : start + cut], 1, 1)
            keep_ref[step, :, start : start + cut] = part[:rows]
            send_ref[step, :, start : start + cut] = part[rows:].astype(bf16)


def back_to_norm(grad, cosine, sine, pieces, table, starts, spots):
    heads, blocks, _, head_dim, rows = grad.shape
    columns = pieces[0].shape[1]
    width = HEADS * head_dim
    steps = spots.shape[0] // 2
    return pl.pallas_call(
        functools.partial(grads_kernel, len(pieces), table),
        out_shape=(
            jax.ShapeDtypeStruct((columns, blocks * rows), bf16),
            jax.ShapeDtypeStruct((steps, rows, width), f32),
            jax.ShapeDtypeStruct((steps, rows, width), bf16),
        ),
        in_specs=[IN_SMEM] * 2 + [IN_VMEM] * 3 + [ANYWHERE] * len(pieces),
        out_specs=(IN_VMEM,) * 3,
        scratch_shapes=[
            pltpu.VMEM((width, columns), bf16),
            pltpu.VMEM((blocks, rows, columns), bf16),
            pltpu.SemaphoreType.DMA((len(table),)),
        ],
        compiler_params=pltpu.CompilerParams(vmem_limit_bytes=48 * 2**20),
        cost_estimate=SHORT,
        name="back_to_norm",
    )(starts, spots, grad, cosine, sine, *pieces)


def units_kernel(counts, tables, own_ref, other_ref, grad_own_ref, grad_other_ref, *refs):
    starts_refs, refs = refs[:3], refs[3:]
    pieces = (refs[: counts[0]], refs[counts[0] : sum(counts[:2])], refs[sum(counts[:2]) : sum(counts)])
    outs, weights, semaphores = refs[-15:-6], refs[-6:-3], refs[-3:]
    act_ref, grad_gate_ref, grad_up_ref, normed_ref, grads_ref = outs[:5]
    keep_ref, send_ref, branch_keep_ref, branch_send_ref = outs[5:]
    rows, width = own_ref.shape
    copies = [
        start_pieces(*each) for each in zip(pieces, tables, starts_refs, weights, semaphores)
    ]
    gate_w, up_w, down_w = weights

    def arrived(which):
        for copy in copies[which]:
            copy.wait()

    normed_ref[0, :rows] = own_ref[...]
    normed_ref[0, rows:] = other_ref[...]
    grads_ref[0, :rows] = grad_own_ref[...]
    grads_ref[0, rows:] = grad_other_ref[...]
    arrived(0)
    gate = contract(normed_ref[0], gate_w[...], 1, 1)
    sigmoid = 1.0 / (1.0 + jnp.exp(-gate))
    silu = gate * sigmoid
    arrived(1)
    up = contract(normed_ref[0], up_w[...], 1, 1)
    act_ref[0] = (silu * up).astype(bf16)
    arrived(2)
    grad_act = contract(grads_ref[0], down_w[...], 1, 1)
    grad_gate_ref[0] = (grad_act * up * sigmoid * (1.0 + gate * (1.0 - sigmoid))).astype(bf16)
    grad_up_ref[0] = (grad_act * silu).astype(bf16)
    cut = min(512, width)
    for start in range(0, width, cut):
        span = slice(start, start + cut)
        part = contract(grad_gate_ref[0], gate_w[:, span], 1, 0)
        part = part + contract(grad_up_ref[0], up_w[:, span], 1, 0)
        keep_ref[:, span] = part[:rows]
        send_ref[:, span] = part[rows:].astype(bf16)
    for start in range(0, width, cut):
        span = slice(start, start + cut)
        part = contract(act_ref[0], down_w[:, span], 1, 0)
        branch_keep_ref[:, span] = part[:rows]
        branch_send_ref[:, span] = part[rows:].astype(bf16)


def units_chunk(step, count, own, other, grad_own, grad_other, weights, held):
    rows, width = own.shape
    arrays = [array for pieces, _, _ in weights for array in pieces]
    counts = tuple(len(pieces) for pieces, _, _ in weights)
    tables = tuple(table for _, table, _ in weights)
    units = sum(taken for _, _, taken in tables[0])
    whole = pl.BlockSpec((rows, width), lambda i: (0, 0))
    kept_units = pl.BlockSpec((1, 2 * rows, units), lambda i: (step, 0, 0))
    kept_rows = pl.BlockSpec((1, 2 * rows, width), lambda i: (step, 0, 0))
    by_units = jax.ShapeDtypeStruct((count, 2 * rows, units), bf16)
    by_rows = jax.ShapeDtypeStruct((count, 2 * rows, width), bf16)
    sums = (jax.ShapeDtypeStruct((rows, width), f32), jax.ShapeDtypeStruct((rows, width), bf16))
    return pl.pallas_call(
        functools.partial(units_kernel, counts, tables),
        grid=(1,),
        out_shape=(by_units,) * 3 + (by_rows,) * 2 + sums * 2,
        in_specs=[whole] * 4 + [IN_SMEM] * 3 + [ANYWHERE] * (len(arrays) + len(held)),
        out_specs=(kept_units,) * 3 + (kept_rows,) * 2 + (whole,) * 4,
        scratch_shapes=[pltpu.VMEM((units, width), bf16)] * 3
        + [pltpu.SemaphoreType.DMA((len(table),)) for table in tables],
        input_output_aliases={7 + len(arrays) + i: i for i in range(len(held))},
        compiler_params=pltpu.CompilerParams(vmem_limit_bytes=56 * 2**20),
        cost_estimate=SHORT,
        name="units_chunk",
    )(own, other, grad_own, grad_other, *[starts for _, _, starts in weights], *arrays, *held)


def transposed_product_kernel(left_ref, right_ref, out_ref):
    out_ref[...] = contract(left_ref[...], right_ref[...], 0, 0).astype(bf16)


def transposed_product(left, right):
    depth, units = left.shape
    width = right.shape[1]
    cut = min(256, units)
    return pl.pallas_call(
        transposed_product_kernel,
        grid=(units // cut,),
        out_shape=jax.ShapeDtypeStruct((units, width), bf16),
        in_specs=[
            pl.BlockSpec((depth, cut), lambda i: (0, i)),
            pl.BlockSpec((depth, width), lambda i: (0, 0)),
        ],
        out_specs=pl.BlockSpec((cut, width), lambda i: (i, 0)),
        compiler_params=pltpu.CompilerParams(vmem_limit_bytes=48 * 2**20),
        cost_estimate=SHORT,
        name="transposed_product",
    )(left, right)


def rotary_tables(positions, head_dim):
    half_dim = head_dim // 2
    frequency = rope_base ** (-(jnp.arange(half_dim, dtype=f32) * 2.0) / head_dim)
    angles = positions.astype(f32)[None, :] * frequency[:, None]
    return jnp.cos(angles), jnp.sin(angles)


def after(array, *others):
    return lax.optimization_barrier((array, *others))[0]


def swap_cores(array):
    return lax.ppermute(array, "c", [(0, 1), (1, 0)])


def from_next(array):
    count = lax.axis_size("z")
    return lax.ppermute(array, "z", [(i, (i - 1) % count) for i in range(count)])


def from_flipped(array, bit):
    return lax.ppermute(array, "p", [(i, i ^ bit) for i in range(4)])


def square_groups():
    return lax.axis_size("p") == 4 and lax.axis_size("r") == 1


def gather_chunks(block):
    count = lax.axis_size("z")
    chunks = []
    for step in range(count):
        later = from_next(block) if step < count - 1 else None
        chunks.append((block, swap_cores(block)))
        block = later
    return chunks


def add_over_line(parts, starts=(), fills=()):
    count = lax.axis_size("z")
    total = parts[1 % count]
    for step in range(2, count + 1):
        send = total.astype(bf16)
        if step - 2 < len(starts):
            send = after(send, starts[step - 2])
        came = from_next(send)
        if step - 2 < len(fills):
            came = after(came, fills[step - 2])
        total = came.astype(f32) + parts[step % count]
    return total


def add_over_cores(keep, send):
    return keep + swap_cores(send.astype(bf16)).astype(f32)


def group_pieces(block, before_corner=()):
    if not square_groups():
        whole = lax.all_gather(block, GROUPS, axis=0)
        return [(whole[group], group, 0) for group in range(whole.shape[0])]
    half = block.shape[0] // 2
    place = lax.axis_index("p")
    beside, across = from_flipped(block, 1), from_flipped(block, 2)
    near = [(block, place, 0), (beside, place ^ 1, 0), (across, place ^ 2, 0)]
    top, low = after((beside[:half], across[half:]), before_corner)
    top, low = from_flipped(top, 2), from_flipped(low, 1)
    return [*near, (top, place ^ 3, 0), (low, place ^ 3, half)]


def placed(pieces, rows):
    table = tuple((which, 0, piece[0].shape[0]) for which, piece in enumerate(pieces))
    starts = [jnp.int32(group) * rows + first for _, group, first in pieces]
    return [array for array, _, _ in pieces], table, jnp.stack(starts).astype(jnp.int32)


def scatter_groups(parts):
    if not square_groups():
        flat = parts.reshape(-1, parts.shape[-1])
        return lax.psum_scatter(flat, GROUPS, scatter_dimension=0, tiled=True).astype(f32)
    half = parts.shape[1] // 2
    place = lax.axis_index("p")
    own, beside, across, corner = (
        lax.dynamic_index_in_dim(parts, place ^ bits, 0, keepdims=False) for bits in range(4)
    )
    to_across = from_flipped(corner[:half], 1)
    to_beside = from_flipped(corner[half:], 2)
    total_top = from_flipped(beside[:half], 1).astype(f32)
    total_low = from_flipped(across[half:], 2).astype(f32)
    beside_low = (beside[half:].astype(f32) + to_beside.astype(f32)).astype(bf16)
    across_top = (across[:half].astype(f32) + to_across.astype(f32)).astype(bf16)
    total_low = total_low + from_flipped(beside_low, 1).astype(f32)
    total_top = total_top + from_flipped(across_top, 2).astype(f32)
    return own.astype(f32) + jnp.concatenate([total_top, total_low])


def ring(block, starts=()):
    blocks = [block]
    for step in range(lax.axis_size("z") - 1):
        send = after(blocks[-1], starts[step]) if step < len(starts) else blocks[-1]
        blocks.append(from_next(send))
    return blocks


def shards(tokens, attn_qkv, attn_out_t, mlp_weight, norm1, norm2, cotangent):
    rows, width = tokens.shape
    group_count, share_count = lax.axis_size("p"), lax.axis_size("r")
    line_count = lax.axis_size("z")
    tensor_count = lax.axis_size("c") * line_count
    head_dim = width // HEADS
    heads_here = HEADS // tensor_count
    group_rows = rows * tensor_count
    features_here = heads_here * head_dim
    weight_rows = attn_qkv.shape[0]
    share, place, core = lax.axis_index("r"), lax.axis_index("z"), lax.axis_index("c")
    block = min(1024, group_rows)
    x = tokens.astype(f32)
    gain_one = norm1.astype(f32)[:, None]
    device_index = (share * group_count + lax.axis_index("p")) * tensor_count

    def chunk_places(step):
        along = lax.rem(place + step, line_count)
        return core * line_count + along, (1 - core) * line_count + along

    x_group = lax.all_gather(tokens, TENSOR, axis=0, tiled=True)
    scaled_qkv = (attn_qkv.astype(f32) * gain_one).astype(bf16)
    qkv_cut = scaled_qkv.reshape(weight_rows, 3, tensor_count, features_here).transpose(2, 0, 1, 3)
    qkv_cut = qkv_cut.reshape(tensor_count, weight_rows, 3 * features_here)
    qkv_part = lax.all_to_all(qkv_cut, TENSOR, 0, 0).reshape(-1, 3 * features_here)
    qkv_rows = qkv_part.shape[0]
    qkv_arrays, qkv_table, qkv_starts = placed(group_pieces(qkv_part), qkv_rows)
    gain_columns = jnp.pad(norm2[:, None], ((0, 0), (0, 127)))
    out_pieces = group_pieces(jnp.concatenate([attn_out_t, gain_columns], axis=1), qkv_part)
    unit_rows = mlp_weight.shape[0]
    gate_weight = placed(group_pieces(mlp_weight[:, :width], qkv_arrays), unit_rows)
    down_weight = placed(group_pieces(mlp_weight[:, 2 * width :], qkv_arrays), unit_rows)
    up_whole = lax.all_gather(
        after(mlp_weight[:, width : 2 * width], qkv_arrays), GROUPS, axis=0, tiled=True
    )
    up_weight = ([up_whole], ((0, 0, up_whole.shape[0]),), jnp.zeros((1,), jnp.int32))

    positions = device_index * rows + jnp.arange(group_rows)
    cosine, sine = rotary_tables(positions, head_dim)
    unit_group, stacked = project(
        x_group, cosine, sine, qkv_arrays, qkv_table, qkv_starts, heads_here, head_dim, rows
    )
    qkv = lax.all_to_all(stacked, "p", 0, 0)
    qkv = qkv.reshape(-1, 3, head_dim, rows)

    def over_shares(array):
        return lax.all_gather(array, "r", axis=0, tiled=True) if share_count > 1 else array

    def own_share(array):
        if share_count == 1:
            return array
        pieces = group_count * tensor_count
        return lax.dynamic_slice_in_dim(array, share * pieces, pieces, 0)

    qkv = over_shares(qkv)
    attended, logsum = attend_forward(qkv, block)
    attended_head = own_share(attended)

    out_plane = jnp.concatenate([array for array, _, _ in out_pieces])
    grad_out_ring = ring(cotangent, (x_group,))[:2]
    out_ring = ring(out_plane, (grad_out_ring[-1], stacked, qkv))
    out_arrays = out_ring + [swap_cores(array) for array in out_ring[:-1]]
    out_arrays.append(swap_cores(after(out_ring[-1], attended)))
    out_table, out_starts = [], []
    for which in range(2 * line_count):
        side = core if which < line_count else 1 - core
        along = lax.rem(place + which % line_count, line_count)
        first = 0
        for array, group, offset in out_pieces:
            out_table.append((which, first, array.shape[0]))
            spot = (jnp.int32(group) * 2 + side) * line_count + along
            out_starts.append(spot * weight_rows + offset)
            first += array.shape[0]
    out_table, out_starts = tuple(out_table), jnp.stack(out_starts).astype(jnp.int32)
    grad_out_ring += ring(after(grad_out_ring[-1], out_ring[-1]), ((),))[1 : line_count - 1]
    grad_out_chunks = [(block, swap_cores(block)) for block in grad_out_ring]

    attended_local = lax.all_to_all(attended_head, ("p", "c", "z"), 0, 0)
    middle, normed_two, gain_two = finish_attention(
        tokens, attended_local, out_arrays, out_table, out_starts, HEADS // tensor_count
    )
    attended_group = attended_head.reshape(group_count, tensor_count, head_dim, rows)
    attended_group = lax.all_to_all(after(attended_group, normed_two), "p", 0, 0)

    held, normed_parts, branch_parts = (), [], []
    normed = normed_two
    for step in range(line_count):
        later = from_next(normed) if step < line_count - 1 else None
        *held, keep, send, branch_keep, branch_send = units_chunk(
            step, line_count, normed, swap_cores(normed), *grad_out_chunks[step],
            (gate_weight, up_weight, down_weight), held,
        )
        normed_parts.append(add_over_cores(keep, send))
        branch_parts.append((branch_keep, branch_send))
        if later is not None:
            normed = after(later, keep)
    activation, gate_grads, up_grads, normed_group, grad_out_group = (
        array.reshape(group_rows, -1) for array in held
    )

    def over_groups(part):
        return lax.psum_scatter(part, GROUPS, scatter_dimension=0, tiled=True)

    gate_term = transposed_product(gate_grads, normed_group)
    grad_normed = add_over_line(normed_parts, fills=((), (), gate_term))
    grad_middle, grad_mid_low, norm_two_part, grad_attended = back_to_attention(
        middle, grad_normed, cotangent, gain_two, out_arrays, out_table, out_starts,
        HEADS // tensor_count, head_dim,
    )
    grad_head = lax.all_to_all(grad_attended, ("p", "c", "z"), 0, 0)
    up_grads, activation = after((up_grads, activation), grad_attended)
    up_term = transposed_product(up_grads, normed_group)
    down_term = transposed_product(activation, grad_out_group)
    grad_head = after(grad_head, up_term, down_term)

    grad_qkv_head = attend_backward(qkv, over_shares(grad_head), attended, logsum, block)
    grad_qkv_head = own_share(grad_qkv_head)
    branch = add_over_line(
        [add_over_cores(*part) for part in branch_parts],
        starts=(grad_attended, grad_head, grad_qkv_head),
    )
    result = (middle + branch).astype(bf16)

    grad_gate_w = over_groups(gate_term)
    grad_mid_group = lax.all_gather(after(grad_mid_low, gate_term), TENSOR, axis=0, tiled=True)
    grad_up_w = over_groups(after(up_term, grad_head))
    grad_down_w = over_groups(after(down_term, grad_head))

    def to_owners(part, start=()):
        columns = part.shape[1]
        parts = after(part.astype(bf16), start).reshape(share_count * group_count, -1, columns)
        own = scatter_groups(parts).astype(bf16)
        own = lax.all_to_all(own.reshape(tensor_count, -1, columns), TENSOR, 0, 0)
        return own.astype(f32)

    attended_group = jnp.swapaxes(attended_group, 1, 2).reshape(features_here, group_rows)
    out_term = contract(grad_mid_group, attended_group, 0, 1)
    norm_two_part = norm_two_part[0]
    norm_high = norm_two_part.astype(bf16).astype(f32)
    norm_columns = jnp.stack([norm_high, norm_two_part - norm_high], axis=1)
    grad_qkv_rows = grad_qkv_head.reshape(group_count, tensor_count, 3, head_dim, rows)
    grad_qkv_rows = lax.all_to_all(grad_qkv_rows, "p", 0, 0)
    grad_qkv_rows = after(grad_qkv_rows, out_term)
    out_sum = to_owners(
        jnp.concatenate([out_term, jnp.pad(norm_columns, ((0, 0), (0, 126)))], axis=1),
        grad_qkv_rows,
    )
    grad_out_w = out_sum[:, :, :features_here].transpose(1, 0, 2).reshape(-1, width)
    grad_norm_two = jnp.sum(out_sum[:, :, features_here : features_here + 2], axis=(0, 2))
    spots = [spot for step in range(line_count) for spot in chunk_places(step)]
    grad_qkv_low, keep, send = back_to_norm(
        grad_qkv_rows, cosine, sine, qkv_arrays, qkv_table, qkv_starts,
        jnp.stack(spots).astype(jnp.int32),
    )
    weighted_parts = [add_over_cores(keep[step], send[step]) for step in range(line_count)]
    qkv_term = contract(unit_group, after(grad_qkv_low, weighted_parts[1]), 0, 1).astype(bf16)
    weighted_one = add_over_line(weighted_parts, fills=(qkv_term,))
    factor_one = lax.rsqrt(jnp.mean(x * x, axis=-1, keepdims=True) + epsilon)
    grad_tokens = (
        grad_middle
        + factor_one * weighted_one
        - x * factor_one**3 * jnp.mean(weighted_one * x, axis=-1, keepdims=True)
    )
    qkv_sum = to_owners(qkv_term).reshape(tensor_count, weight_rows, 3, features_here)
    qkv_sum = qkv_sum.transpose(1, 2, 0, 3).reshape(weight_rows, 3 * width)
    grad_qkv = gain_one * qkv_sum
    grad_norm_one = jnp.sum(attn_qkv.astype(f32) * qkv_sum, axis=1)
    grad_mlp = jnp.concatenate([grad_gate_w, grad_up_w, grad_down_w], axis=1).astype(f32)
    return (result, grad_tokens, grad_qkv, grad_out_w, grad_mlp, grad_norm_one, grad_norm_two)


def solution(mesh):
    seq_count, fsdp_count = mesh.shape["seq"], mesh.shape["fsdp"]
    groups = seq_count // 2
    heads_here = HEADS // (2 * fsdp_count)
    dealt = min(groups, heads_here)
    fine = Mesh(mesh.devices.reshape(groups // dealt, dealt, 2, fsdp_count), ALL)
    by_rows, by_items = P(ALL, None), P(ALL)
    in_specs = (by_rows, by_rows, by_rows, by_rows, by_items, by_items, by_rows)
    out_specs = (by_rows, by_rows, by_rows, by_rows, by_rows, by_items, by_items)
    return jax.shard_map(shards, mesh=fine, in_specs=in_specs, out_specs=out_specs, check_vma=False)
```

```python
import functools

import jax
import jax.numpy as jnp
from jax import lax
from jax.experimental import pallas as pl
from jax.experimental.pallas import tpu as pltpu
from jax.sharding import Mesh
from jax.sharding import PartitionSpec as P

HEADS = 32
epsilon = 1e-05
rope_base = 130000.0
f32 = jnp.float32
bf16 = jnp.bfloat16


def lasting(microseconds):
    return pl.CostEstimate(
        flops=int(microseconds * 1.1e9), bytes_accessed=1000, transcendentals=0
    )


IN_VMEM = pl.BlockSpec(memory_space=pltpu.VMEM)
IN_SMEM = pl.BlockSpec(memory_space=pltpu.SMEM)
ANYWHERE = pl.BlockSpec(memory_space=pl.ANY)
ALL = ("r", "p", "c", "z")
GROUPS = ("r", "p")
TENSOR = ("c", "z")


def contract(left, right, left_dim, right_dim):
    return lax.dot_general(
        left, right, (((left_dim,), (right_dim,)), ((), ())), preferred_element_type=f32
    )


def causal(scores):
    keys = lax.broadcasted_iota(jnp.int32, scores.shape, 0)
    queries = lax.broadcasted_iota(jnp.int32, scores.shape, 1)
    return jnp.where(keys <= queries, scores, -1e30)


def forward_kernel(qkv_ref, out_ref, logsum_ref, keys, values_t, queries_t, *, block):
    pieces, _, head_dim, rows = qkv_ref.shape
    per_block = block // rows
    count = pieces // per_block
    for piece in range(pieces):
        number, part = divmod(piece, per_block)
        span = slice(part * rows, (part + 1) * rows)
        queries_t[number, :, span] = qkv_ref[piece, 0]
        keys[number, span, :] = qkv_ref[piece, 1].T
        values_t[number, :, span] = qkv_ref[piece, 2]

    def step(i, j, carry, diagonal):
        largest, total, result = carry
        scores = contract(keys[j], queries_t[i], 1, 0)
        if diagonal:
            scores = causal(scores)
        new_largest = jnp.maximum(largest, jnp.max(scores, axis=0, keepdims=True))
        shrink = jnp.exp(largest - new_largest)
        weights = jnp.exp(scores - new_largest)
        total = total * shrink + jnp.sum(weights, axis=0, keepdims=True)
        result = result * shrink + contract(values_t[j], weights.astype(bf16), 1, 0)
        return new_largest, total, result

    def query_block(i, _):
        carry = (
            jnp.full((1, block), -1e30, f32),
            jnp.zeros((1, block), f32),
            jnp.zeros((head_dim, block), f32),
        )
        carry = lax.fori_loop(0, i, lambda j, c: step(i, j, c, False), carry)
        largest, total, result = step(i, i, carry, True)
        result = (result / total).astype(bf16)
        for part in range(per_block):
            out_ref[i * per_block + part] = result[:, part * rows : (part + 1) * rows]
        logsum_ref[i] = largest + jnp.log(total)
        return 0

    lax.fori_loop(0, count, query_block, 0)


def backward_kernel(lower, upper, last, block, scale, *refs):
    qkv_ref, grad_ref, out_ref, logsum_ref = refs[:4]
    earlier, (result_ref, sums_ref) = refs[4:-11], refs[-11:-9]
    keys, queries, values, grads, keys_t, queries_t, grads_t, deltas, grad_queries = refs[-9:]
    pieces, _, head_dim, rows = qkv_ref.shape
    per_block = block // rows
    count = pieces // per_block
    for piece in range(lower * per_block, pieces):
        number, part = divmod(piece, per_block)
        span = slice(part * rows, (part + 1) * rows)
        queries_t[number, :, span] = qkv_ref[piece, 0]
        queries[number, span, :] = qkv_ref[piece, 0].T
        if number < upper:
            keys_t[number, :, span] = qkv_ref[piece, 1]
            keys[number, span, :] = qkv_ref[piece, 1].T
            values[number, span, :] = qkv_ref[piece, 2].T
        grad = grad_ref[piece]
        grads_t[number, :, span] = grad
        grads[number, span, :] = grad.T
        deltas[number, :, span] = jnp.sum(
            grad.astype(f32) * out_ref[piece].astype(f32), axis=0, keepdims=True
        )
    for number in range(lower, count):
        if number < upper:
            grad_queries[number] = jnp.zeros((head_dim, block), f32)
        else:
            grad_queries[number] = earlier[1][number - upper]

    def step(i, j, carry, diagonal):
        grad_key, grad_value = carry
        scores = contract(keys[j], queries_t[i], 1, 0)
        if diagonal:
            scores = causal(scores)
        probs = jnp.exp(scores - logsum_ref[i])
        grad_value = grad_value + contract(probs.astype(bf16), grads[i], 1, 0)
        grad_probs = contract(values[j], grads_t[i], 1, 0)
        grad_scores = (probs * (grad_probs - deltas[i])).astype(bf16)
        grad_key = grad_key + contract(grad_scores, queries[i], 1, 0)
        grad_queries[i] = grad_queries[i] + contract(keys_t[j], grad_scores, 1, 0)
        return grad_key, grad_value

    for j in range(lower, upper):
        zero = jnp.zeros((block, head_dim), f32)
        carry = step(j, j, (zero, zero), True)
        grad_key, grad_value = lax.fori_loop(
            j + 1, count, lambda i, c, j=j: step(i, j, c, False), carry
        )
        for part in range(per_block):
            span = slice(part * rows, (part + 1) * rows)
            result_ref[j * per_block + part, 1] = grad_key[span].T.astype(bf16)
            result_ref[j * per_block + part, 2] = grad_value[span].T.astype(bf16)
    if not last:
        for number in range(lower, count):
            sums_ref[number - lower] = grad_queries[number]
        for piece in range(lower * per_block, pieces):
            result_ref[piece, 0] = jnp.zeros((head_dim, rows), bf16)
        return
    sums_ref[0] = jnp.zeros((head_dim, block), f32)
    for piece in range(pieces):
        number, part = divmod(piece, per_block)
        span = slice(part * rows, (part + 1) * rows)
        result_ref[piece, 0] = (grad_queries[number, :, span] * scale).astype(bf16)
        if number >= upper:
            result_ref[piece, 1:] = earlier[0][piece, 1:]


def attend_forward(qkv, block):
    pieces, _, head_dim, rows = qkv.shape
    count = pieces * rows // block
    pairs = count * (count + 1) // 2 * block * block
    in_vmem = pl.BlockSpec(memory_space=pltpu.VMEM)
    by_rows = pltpu.VMEM((count, block, head_dim), bf16)
    by_features = pltpu.VMEM((count, head_dim, block), bf16)
    return pl.pallas_call(
        functools.partial(forward_kernel, block=block),
        out_shape=(
            jax.ShapeDtypeStruct((pieces, head_dim, rows), bf16),
            jax.ShapeDtypeStruct((count, 1, block), f32),
        ),
        in_specs=[in_vmem],
        out_specs=(in_vmem, in_vmem),
        scratch_shapes=[by_rows, by_features, by_features],
        compiler_params=pltpu.CompilerParams(vmem_limit_bytes=56 * 2**20),
        cost_estimate=lasting(18),
        name="attend_forward",
    )(qkv)


def attend_backward(qkv, grad, out, logsum, block, lower, upper, earlier=()):
    pieces, _, head_dim, rows = qkv.shape
    count = pieces * rows // block
    last = lower == 0
    sums = 1 if last else count - lower
    by_rows = pltpu.VMEM((count, block, head_dim), bf16)
    by_features = pltpu.VMEM((count, head_dim, block), bf16)
    return pl.pallas_call(
        functools.partial(backward_kernel, lower, upper, last, block, head_dim**-0.5),
        out_shape=(
            jax.ShapeDtypeStruct(qkv.shape, bf16),
            jax.ShapeDtypeStruct((sums, head_dim, block), f32),
        ),
        in_specs=[IN_VMEM] * (4 + len(earlier)),
        out_specs=(IN_VMEM, IN_VMEM),
        scratch_shapes=[by_rows] * 4
        + [by_features] * 3
        + [pltpu.VMEM((count, 1, block), f32), pltpu.VMEM((count, head_dim, block), f32)],
        compiler_params=pltpu.CompilerParams(vmem_limit_bytes=60 * 2**20),
        cost_estimate=lasting(18),
        name="attend_backward",
    )(qkv, grad, out, logsum, *earlier)


def start_pieces(refs, table, starts_ref, whole, semaphores):
    copies = []
    for number, (which, first, rows, *column) in enumerate(table):
        start = pl.multiple_of(starts_ref[number], rows)
        copy = pltpu.make_async_copy(
            refs[which].at[pl.ds(first, rows), pl.ds(sum(column), whole.shape[1])],
            whole.at[pl.ds(start, rows), :],
            semaphores.at[number],
        )
        copy.start()
        copies.append(copy)
    return copies


def qkv_kernel(count, table, starts_ref, x_ref, cosine_ref, sine_ref, *refs):
    pieces, (unit_ref, out_ref), (weight, weight_t, semaphores) = refs[:count], refs[-5:-3], refs[-3:]
    heads, blocks, _, head_dim, rows = out_ref.shape
    half = head_dim // 2
    copies = start_pieces(pieces, table, starts_ref, weight, semaphores)
    for number in range(blocks):
        span = slice(number * rows, (number + 1) * rows)
        x = x_ref[span].astype(f32)
        factor = lax.rsqrt(jnp.mean(x * x, axis=-1, keepdims=True) + epsilon)
        unit_ref[span] = (x * factor).astype(bf16)
    for copy in copies:
        copy.wait()
    weight_t[...] = weight[...].T
    step = 2
    for first in range(0, blocks, step):
        span = slice(first * rows, (first + step) * rows)
        made = contract(weight_t[...], unit_ref[span], 1, 1)
        cosine, sine = cosine_ref[:, span], sine_ref[:, span]
        for kind in range(3):
            for head in range(heads):
                at = (kind * heads + head) * head_dim
                upper, lower = made[at : at + half], made[at + half : at + head_dim]
                if kind < 2:
                    upper, lower = upper * cosine - lower * sine, lower * cosine + upper * sine
                upper, lower = upper.astype(bf16), lower.astype(bf16)
                if kind == 0:
                    upper, lower = upper * bf16(head_dim**-0.5), lower * bf16(head_dim**-0.5)
                for part in range(step):
                    lanes = slice(part * rows, (part + 1) * rows)
                    out_ref[head, first + part, kind, :half] = upper[:, lanes]
                    out_ref[head, first + part, kind, half:] = lower[:, lanes]


def project(x_group, cosine, sine, pieces, table, starts, heads, head_dim, rows):
    tokens, width = x_group.shape
    columns = pieces[0].shape[1]
    return pl.pallas_call(
        functools.partial(qkv_kernel, len(pieces), table),
        out_shape=(
            jax.ShapeDtypeStruct((tokens, width), bf16),
            jax.ShapeDtypeStruct((heads, tokens // rows, 3, head_dim, rows), bf16),
        ),
        in_specs=[IN_SMEM] + [IN_VMEM] * 3 + [ANYWHERE] * len(pieces),
        out_specs=(IN_VMEM, IN_VMEM),
        scratch_shapes=[
            pltpu.VMEM((width, columns), bf16),
            pltpu.VMEM((columns, width), bf16),
            pltpu.SemaphoreType.DMA((len(table),)),
        ],
        compiler_params=pltpu.CompilerParams(vmem_limit_bytes=48 * 2**20),
        cost_estimate=lasting(10),
        name="project",
    )(starts, x_group, cosine, sine, *pieces)


def mid_kernel(count, table, groups, starts_ref, x_ref, attended_ref, *refs):
    pieces, (mid_ref, normed_ref, gain_ref) = refs[:count], refs[-6:-3]
    weight, attended, semaphores = refs[-3:]
    copies = start_pieces(pieces, table, starts_ref, weight, semaphores)
    _, head_dim, rows = attended_ref.shape
    width = x_ref.shape[1]
    tensor = HEADS // groups
    pair = 128 // head_dim
    for first in range(0, HEADS, pair):
        features = jnp.concatenate(
            [
                attended_ref[head % groups * tensor + head // groups]
                for head in range(first, first + pair)
            ]
        )
        attended[:, first * head_dim : (first + pair) * head_dim] = features.T
    for copy in copies:
        copy.wait()
    cut = min(512, width)
    for start in range(0, width, cut):
        span = slice(start, start + cut)
        gain_ref[:, span] = weight[span, width:].astype(f32).T[:1]
        mid_ref[:, span] = x_ref[:, span].astype(f32) + contract(
            attended[...], weight[span, :width], 1, 1
        )
    mid = mid_ref[...]
    factor = lax.rsqrt(jnp.mean(mid * mid, axis=-1, keepdims=True) + epsilon)
    normed_ref[...] = (mid * factor * gain_ref[...]).astype(bf16)


def finish_attention(x, attended, pieces, table, starts, groups):
    rows, width = x.shape
    return pl.pallas_call(
        functools.partial(mid_kernel, len(pieces), table, groups),
        out_shape=(
            jax.ShapeDtypeStruct((rows, width), f32),
            jax.ShapeDtypeStruct((rows, width), bf16),
            jax.ShapeDtypeStruct((1, width), f32),
        ),
        in_specs=[IN_SMEM] + [IN_VMEM] * 2 + [ANYWHERE] * len(pieces),
        out_specs=(IN_VMEM,) * 3,
        scratch_shapes=[
            pltpu.VMEM((width, pieces[0].shape[1]), bf16),
            pltpu.VMEM((rows, width), bf16),
            pltpu.SemaphoreType.DMA((len(table),)),
        ],
        compiler_params=pltpu.CompilerParams(vmem_limit_bytes=48 * 2**20),
        cost_estimate=lasting(9),
        name="finish_attention",
    )(starts, x, attended, *pieces)


def grad_mid_kernel(count, table, groups, starts_ref, mid_ref, grad_ref, cotangent_ref, gain_ref, *refs):
    pieces, (grad_mid_ref, low_ref, gain_part_ref, out_ref) = refs[:count], refs[-6:-2]
    weight, semaphores = refs[-2:]
    copies = start_pieces(pieces, table, starts_ref, weight, semaphores)
    _, head_dim, rows = out_ref.shape
    width = mid_ref.shape[1]
    tensor = HEADS // groups
    pair = 128 // head_dim
    mid, grad = mid_ref[...], grad_ref[...]
    factor = lax.rsqrt(jnp.mean(mid * mid, axis=-1, keepdims=True) + epsilon)
    weighted = grad * gain_ref[...]
    inner = jnp.mean(weighted * mid, axis=-1, keepdims=True)
    grad_mid = (
        cotangent_ref[...].astype(f32) + factor * weighted - mid * (factor * factor * factor * inner)
    )
    grad_mid_ref[...] = grad_mid
    low_ref[...] = grad_mid.astype(bf16)
    gain_part_ref[...] = jnp.sum(grad * (mid * factor), axis=0, keepdims=True)
    for copy in copies:
        copy.wait()
    cut = min(512, width)
    for start in range(0, width, cut):
        made = contract(low_ref[...], weight[:, start : start + cut], 1, 0).astype(bf16)
        for at in range(0, cut, pair * head_dim):
            features = made[:, at : at + pair * head_dim].T
            for part in range(pair):
                head = (start + at) // head_dim + part
                out_ref[head % groups * tensor + head // groups] = features[
                    part * head_dim : (part + 1) * head_dim
                ]


def back_to_attention(mid, grad, cotangent, gain, pieces, table, starts, groups, head_dim):
    rows, width = mid.shape
    return pl.pallas_call(
        functools.partial(grad_mid_kernel, len(pieces), table, groups),
        out_shape=(
            jax.ShapeDtypeStruct((rows, width), f32),
            jax.ShapeDtypeStruct((rows, width), bf16),
            jax.ShapeDtypeStruct((1, width), f32),
            jax.ShapeDtypeStruct((HEADS, head_dim, rows), bf16),
        ),
        in_specs=[IN_SMEM] + [IN_VMEM] * 4 + [ANYWHERE] * len(pieces),
        out_specs=(IN_VMEM,) * 4,
        scratch_shapes=[
            pltpu.VMEM((width, width), bf16),
            pltpu.SemaphoreType.DMA((len(table),)),
        ],
        compiler_params=pltpu.CompilerParams(vmem_limit_bytes=48 * 2**20),
        cost_estimate=lasting(6),
        name="back_to_attention",
    )(starts, mid, grad, cotangent, gain, *pieces)


def turn_back_kernel(grad_ref, cosine_ref, sine_ref, unit_ref, by_tokens_ref, out_ref, low):
    heads, blocks, _, head_dim, rows = grad_ref.shape
    half = head_dim // 2
    for block in range(blocks):
        span = slice(block * rows, (block + 1) * rows)
        cosine, sine = cosine_ref[:, span], sine_ref[:, span]
        for kind in range(3):
            for head in range(heads):
                at = (kind * heads + head) * head_dim
                grad = grad_ref[head, block, kind]
                if kind < 2:
                    grad = grad.astype(f32)
                    upper, lower = grad[:half], grad[half:]
                    grad = jnp.concatenate(
                        [upper * cosine + lower * sine, lower * cosine - upper * sine]
                    ).astype(bf16)
                low[at : at + head_dim, span] = grad
        by_tokens_ref[block] = low[:, span].T
    width = out_ref.shape[0]
    cut = min(512, width)
    for start in range(0, width, cut):
        out_ref[start : start + cut] = contract(
            unit_ref[:, start : start + cut], low[...], 0, 1
        ).astype(bf16)


def turn_back(grad, cosine, sine, unit_group):
    heads, blocks, _, head_dim, rows = grad.shape
    columns = 3 * heads * head_dim
    return pl.pallas_call(
        turn_back_kernel,
        out_shape=(
            jax.ShapeDtypeStruct((blocks, rows, columns), bf16),
            jax.ShapeDtypeStruct((unit_group.shape[1], columns), bf16),
        ),
        in_specs=[IN_VMEM] * 4,
        out_specs=(IN_VMEM,) * 2,
        scratch_shapes=[pltpu.VMEM((columns, blocks * rows), bf16)],
        compiler_params=pltpu.CompilerParams(vmem_limit_bytes=48 * 2**20),
        cost_estimate=lasting(8),
        name="turn_back",
    )(grad, cosine, sine, unit_group)


def norm_kernel(count, table, starts_ref, spots_ref, by_tokens_ref, *refs):
    pieces, outs, (weight, semaphores) = refs[:count], refs[count:-2], refs[-2:]
    copies = start_pieces(pieces, table, starts_ref, weight, semaphores)
    rows = by_tokens_ref.shape[1]
    steps = len(outs) // 2
    for copy in copies:
        copy.wait()
    width = weight.shape[0]
    cut = min(1024, width)
    for step in range(steps):
        tokens = jnp.concatenate(
            [by_tokens_ref[spots_ref[2 * step]], by_tokens_ref[spots_ref[2 * step + 1]]]
        )
        for start in range(0, width, cut):
            part = contract(tokens, weight[start : start + cut], 1, 1)
            outs[step][:, start : start + cut] = part[:rows]
            outs[steps + step][:, start : start + cut] = part[rows:].astype(bf16)


def back_to_norm(by_tokens, pieces, table, starts, spots, width):
    _, rows, columns = by_tokens.shape
    steps = spots.shape[0] // 2
    made = pl.pallas_call(
        functools.partial(norm_kernel, len(pieces), table),
        out_shape=(jax.ShapeDtypeStruct((rows, width), f32),) * steps
        + (jax.ShapeDtypeStruct((rows, width), bf16),) * steps,
        in_specs=[IN_SMEM] * 2 + [IN_VMEM] + [ANYWHERE] * len(pieces),
        out_specs=(IN_VMEM,) * (2 * steps),
        scratch_shapes=[
            pltpu.VMEM((width, columns), bf16),
            pltpu.SemaphoreType.DMA((len(table),)),
        ],
        compiler_params=pltpu.CompilerParams(vmem_limit_bytes=48 * 2**20),
        cost_estimate=lasting(7),
        name="back_to_norm",
    )(starts, spots, by_tokens, *pieces)
    return made[:steps], made[steps:]


def weight_sums_kernel(
    sums_ref, out_sums_ref, weight_ref, gain_ref, qkv_ref, out_ref, one_ref, two_ref
):
    parts, rows, _ = sums_ref.shape
    kinds = 3
    width = out_ref.shape[1]
    features = width // parts
    gain = gain_ref[...]
    one = jnp.zeros((rows, 128), f32)
    two = jnp.zeros((rows, 128), f32)
    for part in range(parts):
        for kind in range(kinds):
            total = sums_ref[part, :, kind * features : (kind + 1) * features].astype(f32)
            at = slice(kind * width + part * features, kind * width + (part + 1) * features)
            qkv_ref[:, at] = gain * total
            product = total * weight_ref[:, at].astype(f32)
            for lanes in range(0, features, 128):
                one = one + product[:, lanes : lanes + 128]
        out_ref[:, part * features : (part + 1) * features] = out_sums_ref[
            part, :, :features
        ].astype(f32)
        two = two + out_sums_ref[part, :, features:].astype(f32)
    one_ref[...] = jnp.sum(one, axis=1, keepdims=True)
    two_ref[...] = jnp.sum(two, axis=1, keepdims=True)


def weight_sums(sums, out_sums, attn_qkv, gain):
    parts, rows, columns = sums.shape
    width = parts * columns // 3
    qkv, out, one, two = pl.pallas_call(
        weight_sums_kernel,
        out_shape=(
            jax.ShapeDtypeStruct((rows, 3 * width), f32),
            jax.ShapeDtypeStruct((rows, width), f32),
            jax.ShapeDtypeStruct((rows, 1), f32),
            jax.ShapeDtypeStruct((rows, 1), f32),
        ),
        in_specs=[IN_VMEM] * 4,
        out_specs=(IN_VMEM,) * 4,
        compiler_params=pltpu.CompilerParams(vmem_limit_bytes=32 * 2**20),
        cost_estimate=lasting(3),
        name="weight_sums",
    )(sums, out_sums, attn_qkv, gain)
    return qkv, out, one[:, 0], two[:, 0]


def out_product_kernel(spots_ref, attended_ref, gain_ref, *refs):
    blocks, (out_ref, grads, attended) = refs[:-3], refs[-3:]
    heads, _, head_dim, rows = attended_ref.shape
    width = grads.shape[1]
    for number, block in enumerate(blocks):
        grads[pl.ds(pl.multiple_of(spots_ref[number] * rows, rows), rows), :] = block[...]
        for head in range(heads):
            attended[
                head * head_dim : (head + 1) * head_dim, number * rows : (number + 1) * rows
            ] = attended_ref[head, number]
    columns = heads * head_dim
    out_ref[:, :columns] = contract(grads[...], attended[...], 0, 1).astype(bf16)
    gain = jnp.broadcast_to(gain_ref[...], (128, width)).T
    high = gain.astype(bf16).astype(f32)
    lanes = lax.broadcasted_iota(jnp.int32, gain.shape, 1)
    gain = jnp.where(lanes == 0, high, jnp.where(lanes == 1, gain - high, 0.0))
    out_ref[:, columns:] = gain.astype(bf16)


def out_product(blocks, spots, attended, gain):
    rows, width = blocks[0].shape
    heads, count, head_dim, _ = attended.shape
    return pl.pallas_call(
        out_product_kernel,
        out_shape=jax.ShapeDtypeStruct((width, heads * head_dim + 128), bf16),
        in_specs=[IN_SMEM] + [IN_VMEM] * (2 + len(blocks)),
        out_specs=IN_VMEM,
        scratch_shapes=[
            pltpu.VMEM((count * rows, width), bf16),
            pltpu.VMEM((heads * head_dim, count * rows), bf16),
        ],
        compiler_params=pltpu.CompilerParams(vmem_limit_bytes=48 * 2**20),
        cost_estimate=lasting(5),
        name="out_product",
    )(spots, attended, gain, *blocks)


def units_kernel(counts, tables, own_ref, other_ref, grad_own_ref, grad_other_ref, *refs):
    starts_refs, refs = refs[:3], refs[3:]
    pieces = (refs[: counts[0]], refs[counts[0] : sum(counts[:2])], refs[sum(counts[:2]) : sum(counts)])
    outs, weights, semaphores = refs[-15:-6], refs[-6:-3], refs[-3:]
    act_ref, grad_gate_ref, grad_up_ref, normed_ref, grads_ref = outs[:5]
    keep_ref, send_ref, branch_keep_ref, branch_send_ref = outs[5:]
    rows, width = own_ref.shape
    copies = [
        start_pieces(*each) for each in zip(pieces, tables, starts_refs, weights, semaphores)
    ]
    gate_w, up_w, down_w = weights

    def arrived(which):
        for copy in copies[which]:
            copy.wait()

    normed_ref[0, :rows] = own_ref[...]
    normed_ref[0, rows:] = other_ref[...]
    grads_ref[0, :rows] = grad_own_ref[...]
    grads_ref[0, rows:] = grad_other_ref[...]
    arrived(0)
    gate = contract(normed_ref[0], gate_w[...], 1, 1)
    sigmoid = 1.0 / (1.0 + jnp.exp(-gate))
    silu = gate * sigmoid
    arrived(1)
    up = contract(normed_ref[0], up_w[...], 1, 1)
    act_ref[0] = (silu * up).astype(bf16)
    arrived(2)
    grad_act = contract(grads_ref[0], down_w[...], 1, 1)
    grad_gate_ref[0] = (grad_act * up * sigmoid * (1.0 + gate * (1.0 - sigmoid))).astype(bf16)
    grad_up_ref[0] = (grad_act * silu).astype(bf16)
    cut = min(512, width)
    for start in range(0, width, cut):
        span = slice(start, start + cut)
        part = contract(grad_gate_ref[0], gate_w[:, span], 1, 0)
        part = part + contract(grad_up_ref[0], up_w[:, span], 1, 0)
        keep_ref[:, span] = part[:rows]
        send_ref[:, span] = part[rows:].astype(bf16)
    for start in range(0, width, cut):
        span = slice(start, start + cut)
        part = contract(act_ref[0], down_w[:, span], 1, 0)
        branch_keep_ref[:, span] = part[:rows]
        branch_send_ref[:, span] = part[rows:].astype(bf16)


def units_chunk(step, count, own, other, grad_own, grad_other, weights, held):
    rows, width = own.shape
    arrays = [array for pieces, _, _ in weights for array in pieces]
    counts = tuple(len(pieces) for pieces, _, _ in weights)
    tables = tuple(table for _, table, _ in weights)
    units = sum(entry[2] for entry in tables[0])
    whole = pl.BlockSpec((rows, width), lambda i: (0, 0))
    kept_units = pl.BlockSpec((1, 2 * rows, units), lambda i: (step, 0, 0))
    kept_rows = pl.BlockSpec((1, 2 * rows, width), lambda i: (step, 0, 0))
    by_units = jax.ShapeDtypeStruct((count, 2 * rows, units), bf16)
    by_rows = jax.ShapeDtypeStruct((count, 2 * rows, width), bf16)
    sums = (jax.ShapeDtypeStruct((rows, width), f32), jax.ShapeDtypeStruct((rows, width), bf16))
    return pl.pallas_call(
        functools.partial(units_kernel, counts, tables),
        grid=(1,),
        out_shape=(by_units,) * 3 + (by_rows,) * 2 + sums * 2,
        in_specs=[whole] * 4 + [IN_SMEM] * 3 + [ANYWHERE] * (len(arrays) + len(held)),
        out_specs=(kept_units,) * 3 + (kept_rows,) * 2 + (whole,) * 4,
        scratch_shapes=[pltpu.VMEM((units, width), bf16)] * 3
        + [pltpu.SemaphoreType.DMA((len(table),)) for table in tables],
        input_output_aliases={7 + len(arrays) + i: i for i in range(len(held))},
        compiler_params=pltpu.CompilerParams(vmem_limit_bytes=56 * 2**20),
        cost_estimate=lasting(13),
        name="units_chunk",
    )(own, other, grad_own, grad_other, *[starts for _, _, starts in weights], *arrays, *held)


def transposed_product_kernel(left_ref, right_ref, *refs):
    refs[-1][...] = contract(left_ref[...], right_ref[...], 0, 0).astype(bf16)


def transposed_product(left, right, held=(), place=0, count=1):
    depth, units = left.shape
    width = right.shape[1]
    cut = min(256, units)
    return pl.pallas_call(
        transposed_product_kernel,
        grid=(units // cut,),
        out_shape=jax.ShapeDtypeStruct((units, count * width), bf16),
        in_specs=[
            pl.BlockSpec((depth, cut), lambda i: (0, i)),
            pl.BlockSpec((depth, width), lambda i: (0, 0)),
        ]
        + [ANYWHERE] * len(held),
        out_specs=pl.BlockSpec((cut, width), lambda i: (i, place)),
        input_output_aliases={2 + i: 0 for i in range(len(held))},
        compiler_params=pltpu.CompilerParams(vmem_limit_bytes=48 * 2**20),
        cost_estimate=lasting(9),
        name="transposed_product",
    )(left, right, *held)


def rotary_tables(positions, head_dim):
    half_dim = head_dim // 2
    frequency = rope_base ** (-(jnp.arange(half_dim, dtype=f32) * 2.0) / head_dim)
    angles = positions.astype(f32)[None, :] * frequency[:, None]
    return jnp.cos(angles), jnp.sin(angles)


def together(*arrays):
    return lax.optimization_barrier(arrays)


def after(array, *others):
    return lax.optimization_barrier((array, *others))[0]


def swap_cores(array):
    return lax.ppermute(array, "c", [(0, 1), (1, 0)])


def from_next(array):
    count = lax.axis_size("z")
    return lax.ppermute(array, "z", [(i, (i - 1) % count) for i in range(count)])


def from_flipped(array, bit):
    return lax.ppermute(array, "p", [(i, i ^ bit) for i in range(4)])


def square_groups():
    return lax.axis_size("p") == 4 and lax.axis_size("r") == 1


def gather_chunks(block):
    count = lax.axis_size("z")
    chunks = []
    for step in range(count):
        later = from_next(block) if step < count - 1 else None
        chunks.append((block, swap_cores(block)))
        block = later
    return chunks


def add_over_cores(keep, send):
    return keep + swap_cores(send.astype(bf16)).astype(f32)


def near_pieces(block):
    if not square_groups():
        return lax.all_gather(block, GROUPS, axis=0)
    return block, from_flipped(block, 1), from_flipped(block, 2)


def group_pieces(near):
    if not square_groups():
        return [(near[group], group, 0) for group in range(near.shape[0])]
    block, beside, across = near
    half = block.shape[0] // 2
    place = lax.axis_index("p")
    top, low = from_flipped(beside[:half], 2), from_flipped(across[half:], 1)
    return [
        (block, place, 0), (beside, place ^ 1, 0), (across, place ^ 2, 0),
        (top, place ^ 3, 0), (low, place ^ 3, half),
    ]


def placed(pieces, rows):
    table = tuple((which, 0, piece[0].shape[0]) for which, piece in enumerate(pieces))
    starts = [jnp.int32(group) * rows + first for _, group, first in pieces]
    return [array for array, _, _ in pieces], table, jnp.stack(starts).astype(jnp.int32)


def group_parts(whole):
    parts = whole.reshape(lax.axis_size("r") * lax.axis_size("p"), -1, whole.shape[1])
    if not square_groups():
        return parts
    place = lax.axis_index("p")
    return [lax.dynamic_index_in_dim(parts, place ^ bits, 0, keepdims=False) for bits in range(4)]


def scatter_first(parts):
    if not square_groups():
        return ()
    _, beside, across, corner = parts
    half = corner.shape[0] // 2
    return (
        from_flipped(jnp.concatenate([corner[:half], beside[:half]]), 1),
        from_flipped(jnp.concatenate([corner[half:], across[half:]]), 2),
    )


def scatter_second(parts, first):
    if not square_groups():
        flat = parts.reshape(-1, parts.shape[-1])
        return lax.psum_scatter(flat, GROUPS, scatter_dimension=0, tiled=True)
    own, beside, across, corner = parts
    half = corner.shape[0] // 2
    from_beside, from_across = (array.astype(f32) for array in first)
    beside_low = (beside[half:].astype(f32) + from_across[:half]).astype(bf16)
    across_top = (across[:half].astype(f32) + from_beside[:half]).astype(bf16)
    total_low = from_across[half:] + from_flipped(beside_low, 1).astype(f32)
    total_top = from_beside[half:] + from_flipped(across_top, 2).astype(f32)
    return (own.astype(f32) + jnp.concatenate([total_top, total_low])).astype(bf16)


def to_owners(own):
    count = lax.axis_size(TENSOR)
    return lax.all_to_all(own.reshape(count, -1, own.shape[1]), TENSOR, 0, 0)


def shards(tokens, attn_qkv, attn_out_t, mlp_weight, norm1, norm2, cotangent):
    rows, width = tokens.shape
    group_count, share_count = lax.axis_size("p"), lax.axis_size("r")
    line_count = lax.axis_size("z")
    tensor_count = lax.axis_size("c") * line_count
    head_dim = width // HEADS
    heads_here = HEADS // tensor_count
    group_rows = rows * tensor_count
    features_here = heads_here * head_dim
    weight_rows = attn_qkv.shape[0]
    share, place, core = lax.axis_index("r"), lax.axis_index("z"), lax.axis_index("c")
    block = min(1024, group_rows)
    x = tokens.astype(f32)
    gain_one = norm1.astype(f32)[:, None]
    device_index = (share * group_count + lax.axis_index("p")) * tensor_count

    def chunk_places(step):
        along = lax.rem(place + step, line_count)
        return core * line_count + along, (1 - core) * line_count + along

    x_group = lax.all_gather(tokens, TENSOR, axis=0, tiled=True)
    scaled_qkv = (attn_qkv.astype(f32) * gain_one).astype(bf16)
    qkv_cut = scaled_qkv.reshape(weight_rows, 3, tensor_count, features_here).transpose(2, 0, 1, 3)
    qkv_cut = qkv_cut.reshape(tensor_count, weight_rows, 3 * features_here)
    gain_columns = jnp.pad(norm2[:, None], ((0, 0), (0, 127)))
    out_near = near_pieces(jnp.concatenate([attn_out_t, gain_columns], axis=1))
    gate_near = near_pieces(mlp_weight[:, :width])
    unit_rows = mlp_weight.shape[0]
    qkv_part = lax.all_to_all(qkv_cut, TENSOR, 0, 0).reshape(-1, 3 * features_here)
    qkv_part, out_near, gate_near = together(qkv_part, out_near, gate_near)
    qkv_rows = qkv_part.shape[0]
    qkv_arrays, qkv_table, qkv_starts = placed(group_pieces(near_pieces(qkv_part)), qkv_rows)
    out_pieces = group_pieces(out_near)
    out_plane = jnp.concatenate([array for array, _, _ in out_pieces])
    qkv_arrays, x_group, gate_near, out_plane = together(
        qkv_arrays, x_group, gate_near, out_plane
    )

    positions = device_index * rows + jnp.arange(group_rows)
    cosine, sine = rotary_tables(positions, head_dim)
    unit_group, stacked = project(
        x_group, cosine, sine, qkv_arrays, qkv_table, qkv_starts, heads_here, head_dim, rows
    )
    gate_weight = placed(group_pieces(gate_near), unit_rows)
    stacked, gate_arrays, later = together(stacked, gate_weight[0], from_next(out_plane))
    gate_weight = (gate_arrays, *gate_weight[1:])
    out_ring = [out_plane, later]
    swapped = [swap_cores(array) for array in after(out_ring, stacked)]
    qkv = lax.all_to_all(stacked, "p", 0, 0)
    qkv, later, swapped = together(qkv, from_next(out_ring[-1]), swapped)
    qkv = qkv.reshape(-1, 3, head_dim, rows)
    out_ring.append(later)
    rest_whole = lax.all_gather(
        after(mlp_weight[:, width:], x_group), GROUPS, axis=0, tiled=True
    )
    up_weight, down_weight = (
        ([rest_whole], ((0, 0, rest_whole.shape[0], column),), jnp.zeros((1,), jnp.int32))
        for column in (0, width)
    )

    def over_shares(array):
        return lax.all_gather(array, "r", axis=0, tiled=True) if share_count > 1 else array

    def own_share(array):
        if share_count == 1:
            return array
        pieces = group_count * tensor_count
        return lax.dynamic_slice_in_dim(array, share * pieces, pieces, 0)

    qkv = over_shares(qkv)
    rest = [out_ring[-1]]
    for _ in range(line_count - 3):
        rest.append(from_next(rest[-1]))
    swapped.append(swap_cores(out_ring[-1]))
    attended, logsum = attend_forward(qkv, block)
    attended, rest, swapped = together(attended, rest[1:], swapped)
    out_ring += rest
    swapped += [swap_cores(array) for array in rest]
    attended_head = own_share(attended)

    out_table, out_starts = [], []
    for which in range(2 * line_count):
        side = core if which < line_count else 1 - core
        along = lax.rem(place + which % line_count, line_count)
        first = 0
        for array, group, offset in out_pieces:
            out_table.append((which, first, array.shape[0]))
            spot = (jnp.int32(group) * 2 + side) * line_count + along
            out_starts.append(spot * weight_rows + offset)
            first += array.shape[0]
    out_table, out_starts = tuple(out_table), jnp.stack(out_starts).astype(jnp.int32)

    attended_local = lax.all_to_all(attended_head, ("p", "c", "z"), 0, 0)
    later = from_next(after(cotangent, attended))
    attended_local, swapped = together(attended_local, swapped)
    out_weight = (out_ring + swapped, out_table, out_starts)
    grad_out_ring = [cotangent, later, from_next(after(later, attended_local))]
    middle, normed_two, gain_two = finish_attention(
        tokens, attended_local, *out_weight, HEADS // tensor_count
    )
    normed_two, grad_out_ring = together(normed_two, grad_out_ring)
    attended_group = attended_head.reshape(group_count, tensor_count, head_dim, rows)
    attended_group = lax.all_to_all(after(attended_group, normed_two), "p", 0, 0)

    held, branch_parts = (), []
    normed, grad_out, came, total = normed_two, grad_out_ring[0], (), None
    for step in range(line_count):
        later = from_next(normed) if step < line_count - 1 else ()
        if step < line_count - 3:
            grad_out_ring.append(from_next(grad_out_ring[-1]))
        if step >= 2:
            came = from_next(total.astype(bf16))
        *held, keep, send, branch_keep, branch_send = units_chunk(
            step, line_count, normed, swap_cores(normed), grad_out, swap_cores(grad_out),
            (gate_weight, up_weight, down_weight), held,
        )
        branch_parts.append((branch_keep, branch_send))
        if step == 0:
            later, attended_group, keep, send = together(later, attended_group, keep, send)
        else:
            later, came, keep, send = together(later, came, keep, send)
        keep, grad_out_ring = together(keep, grad_out_ring)
        part = add_over_cores(keep, send)
        normed = later
        if step < line_count - 1:
            grad_out = grad_out_ring[step + 1]
        if step == 0:
            own_part = part
        else:
            total = part if step == 1 else came.astype(f32) + part
    activation, gate_grads, up_grads, normed_group, grad_out_group = (
        array.reshape(group_rows, -1) for array in held
    )

    def over_groups(part):
        return lax.psum_scatter(part, GROUPS, scatter_dimension=0, tiled=True)

    gate_term = transposed_product(after(gate_grads, total), normed_group)
    came, gate_term = together(from_next(total.astype(bf16)), gate_term)
    grad_normed = came.astype(f32) + own_part
    grad_middle, grad_mid_low, norm_two_part, grad_attended = back_to_attention(
        middle, grad_normed, cotangent, gain_two, *out_weight,
        HEADS // tensor_count, head_dim,
    )
    grad_head = lax.all_to_all(grad_attended, ("p", "c", "z"), 0, 0)
    up_grads, activation = after((up_grads, activation), grad_attended)
    up_term = transposed_product(up_grads, normed_group)
    down_term = transposed_product(activation, grad_out_group)
    grad_head, up_term, down_term = together(grad_head, up_term, down_term)

    grad_head = over_shares(grad_head)
    count = qkv.shape[0] * rows // block
    backward = functools.partial(attend_backward, qkv, grad_head, attended, logsum, block)
    later_keys = backward(count // 2, count)
    grad_mid_ring = [grad_mid_low, from_next(after(grad_mid_low, grad_head))]
    branch_came = [swap_cores(part[1]) for part in after(branch_parts, grad_head)]
    later_keys, grad_mid_ring, branch_came = together(later_keys, grad_mid_ring, branch_came)

    def branch_sum(came, step):
        return came + branch_parts[step][0] + branch_came[step].astype(f32)

    grad_qkv_head = backward(0, count // 2, later_keys)[0]
    for _ in range(line_count - 3):
        grad_mid_ring.append(from_next(grad_mid_ring[-1]))
    came = from_next(after(branch_sum(0.0, 1 % line_count).astype(bf16), later_keys))
    mid_swapped = [swap_cores(array) for array in grad_mid_ring[:2]]
    grad_qkv_head, grad_mid_ring, came, mid_swapped = together(
        grad_qkv_head, grad_mid_ring, came, mid_swapped
    )
    grad_qkv_head = own_share(grad_qkv_head)
    grad_gate_w, grad_up_w = over_groups(gate_term), over_groups(up_term)

    spots = jnp.stack([spot for step in range(line_count) for spot in chunk_places(step)])
    spots = spots.astype(jnp.int32)
    grad_qkv_rows = grad_qkv_head.reshape(group_count, tensor_count, 3, head_dim, rows)
    grad_qkv_rows = lax.all_to_all(grad_qkv_rows, "p", 0, 0)
    mid_swapped += [swap_cores(array) for array in grad_mid_ring[2:]]
    grad_mid_ring.append(from_next(grad_mid_ring[-1]))
    for step in range(2, line_count - 1):
        came = from_next(branch_sum(came.astype(f32), step).astype(bf16))
    grad_qkv_rows, grad_mid_ring, came, mid_swapped = together(
        grad_qkv_rows, grad_mid_ring, came, mid_swapped
    )
    branch_last = branch_sum(came.astype(f32), line_count - 1) if line_count > 2 else came
    branch_last = from_next(branch_last.astype(bf16))
    mid_swapped.append(swap_cores(grad_mid_ring[-1]))
    grad_qkv_low, qkv_term = turn_back(grad_qkv_rows, cosine, sine, unit_group)
    qkv_parts = group_parts(qkv_term)
    qkv_first = scatter_first(qkv_parts)
    keep, send = back_to_norm(
        after(grad_qkv_low, qkv_parts), qkv_arrays, qkv_table, qkv_starts, spots, width
    )
    keep, send, branch_last, mid_swapped = together(keep, send, branch_last, mid_swapped)
    total = add_over_cores(keep[1 % line_count], send[1 % line_count])
    came = from_next(total.astype(bf16))
    swapped = [swap_cores(send[step]) for step in range(2, line_count)]
    grad_mid_blocks = [
        part for pair in zip(grad_mid_ring, mid_swapped, strict=True) for part in pair
    ]
    out_term = out_product(grad_mid_blocks, spots, attended_group, norm_two_part)
    came, swapped, qkv_first, out_term = together(came, swapped, qkv_first, out_term)
    total = came.astype(f32) + keep[2 % line_count] + swapped[0].astype(f32)
    came = from_next(total.astype(bf16))
    out_parts = group_parts(out_term)
    out_first = scatter_first(out_parts)
    qkv_own = scatter_second(qkv_parts, qkv_first)
    came, qkv_own, out_first = together(came, qkv_own, out_first)
    qkv_sums = to_owners(qkv_own)
    grad_down_w = over_groups(after(down_term, qkv_own))
    for step in range(3, line_count):
        total = came.astype(f32) + keep[step] + swapped[step - 2].astype(f32)
        came = from_next(total.astype(bf16))
    swapped = swap_cores(after(send[0], qkv_own))
    out_own = scatter_second(out_parts, out_first)
    came, swapped, out_own = together(came, swapped, out_own)
    weighted_one = came.astype(f32) + keep[0] + swapped.astype(f32)
    out_sums = to_owners(after(out_own, qkv_sums))
    grad_mlp = jnp.concatenate([grad_gate_w, grad_up_w, grad_down_w], axis=1).astype(f32)
    result = (middle + branch_sum(branch_last.astype(f32), 0)).astype(bf16)
    factor_one = lax.rsqrt(jnp.mean(x * x, axis=-1, keepdims=True) + epsilon)
    grad_tokens = (
        grad_middle
        + factor_one * weighted_one
        - x * factor_one**3 * jnp.mean(weighted_one * x, axis=-1, keepdims=True)
    )
    grad_qkv, grad_out_w, grad_norm_one, grad_norm_two = weight_sums(
        qkv_sums, out_sums, attn_qkv, gain_one
    )
    return (result, grad_tokens, grad_qkv, grad_out_w, grad_mlp, grad_norm_one, grad_norm_two)


def solution(mesh):
    seq_count, fsdp_count = mesh.shape["seq"], mesh.shape["fsdp"]
    groups = seq_count // 2
    heads_here = HEADS // (2 * fsdp_count)
    dealt = min(groups, heads_here)
    fine = Mesh(mesh.devices.reshape(groups // dealt, dealt, 2, fsdp_count), ALL)
    by_rows, by_items = P(ALL, None), P(ALL)
    in_specs = (by_rows, by_rows, by_rows, by_rows, by_items, by_items, by_rows)
    out_specs = (by_rows, by_rows, by_rows, by_rows, by_rows, by_items, by_items)
    return jax.shard_map(shards, mesh=fine, in_specs=in_specs, out_specs=out_specs, check_vma=False)
```

```python
import functools

import jax
import jax.numpy as jnp
from jax import lax
from jax.experimental import pallas as pl
from jax.experimental.pallas import tpu as pltpu
from jax.sharding import Mesh
from jax.sharding import PartitionSpec as P

HEADS = 32
epsilon = 1e-05
rope_base = 130000.0
f32 = jnp.float32
bf16 = jnp.bfloat16


def lasting(microseconds):
    return pl.CostEstimate(
        flops=int(microseconds * 1.1e9), bytes_accessed=1000, transcendentals=0
    )


IN_VMEM = pl.BlockSpec(memory_space=pltpu.VMEM)
IN_SMEM = pl.BlockSpec(memory_space=pltpu.SMEM)
ANYWHERE = pl.BlockSpec(memory_space=pl.ANY)
ALL = ("r", "p", "c", "z")
GROUPS = ("r", "p")
TENSOR = ("c", "z")


def contract(left, right, left_dim, right_dim):
    return lax.dot_general(
        left, right, (((left_dim,), (right_dim,)), ((), ())), preferred_element_type=f32
    )


def causal(scores):
    keys = lax.broadcasted_iota(jnp.int32, scores.shape, 0)
    queries = lax.broadcasted_iota(jnp.int32, scores.shape, 1)
    return jnp.where(keys <= queries, scores, -1e30)


def forward_kernel(qkv_ref, out_ref, logsum_ref, keys, values_t, queries_t, *, block):
    pieces, _, head_dim, rows = qkv_ref.shape
    per_block = block // rows
    count = pieces // per_block
    for piece in range(pieces):
        number, part = divmod(piece, per_block)
        span = slice(part * rows, (part + 1) * rows)
        queries_t[number, :, span] = qkv_ref[piece, 0]
        keys[number, span, :] = qkv_ref[piece, 1].T
        values_t[number, :, span] = qkv_ref[piece, 2]

    def step(i, j, carry, diagonal):
        largest, total, result = carry
        scores = contract(keys[j], queries_t[i], 1, 0)
        if diagonal:
            scores = causal(scores)
        new_largest = jnp.maximum(largest, jnp.max(scores, axis=0, keepdims=True))
        shrink = jnp.exp(largest - new_largest)
        weights = jnp.exp(scores - new_largest)
        total = total * shrink + jnp.sum(weights, axis=0, keepdims=True)
        result = result * shrink + contract(values_t[j], weights.astype(bf16), 1, 0)
        return new_largest, total, result

    def query_block(i, _):
        carry = (
            jnp.full((1, block), -1e30, f32),
            jnp.zeros((1, block), f32),
            jnp.zeros((head_dim, block), f32),
        )
        carry = lax.fori_loop(0, i, lambda j, c: step(i, j, c, False), carry)
        largest, total, result = step(i, i, carry, True)
        result = (result / total).astype(bf16)
        for part in range(per_block):
            out_ref[i * per_block + part] = result[:, part * rows : (part + 1) * rows]
        logsum_ref[i] = largest + jnp.log(total)
        return 0

    lax.fori_loop(0, count, query_block, 0)


def backward_kernel(lower, upper, last, block, scale, *refs):
    qkv_ref, grad_ref, out_ref, logsum_ref = refs[:4]
    earlier, (result_ref, sums_ref) = refs[4:-11], refs[-11:-9]
    keys, queries, values, grads, keys_t, queries_t, grads_t, deltas, grad_queries = refs[-9:]
    pieces, _, head_dim, rows = qkv_ref.shape
    per_block = block // rows
    count = pieces // per_block
    for piece in range(lower * per_block, pieces):
        number, part = divmod(piece, per_block)
        span = slice(part * rows, (part + 1) * rows)
        queries_t[number, :, span] = qkv_ref[piece, 0]
        queries[number, span, :] = qkv_ref[piece, 0].T
        if number < upper:
            keys_t[number, :, span] = qkv_ref[piece, 1]
            keys[number, span, :] = qkv_ref[piece, 1].T
            values[number, span, :] = qkv_ref[piece, 2].T
        grad = grad_ref[piece]
        grads_t[number, :, span] = grad
        grads[number, span, :] = grad.T
        deltas[number, :, span] = jnp.sum(
            grad.astype(f32) * out_ref[piece].astype(f32), axis=0, keepdims=True
        )
    for number in range(lower, count):
        if number < upper:
            grad_queries[number] = jnp.zeros((head_dim, block), f32)
        else:
            grad_queries[number] = earlier[1][number - upper]

    def step(i, j, carry, diagonal):
        grad_key, grad_value = carry
        scores = contract(keys[j], queries_t[i], 1, 0)
        if diagonal:
            scores = causal(scores)
        probs = jnp.exp(scores - logsum_ref[i])
        grad_value = grad_value + contract(probs.astype(bf16), grads[i], 1, 0)
        grad_probs = contract(values[j], grads_t[i], 1, 0)
        grad_scores = (probs * (grad_probs - deltas[i])).astype(bf16)
        grad_key = grad_key + contract(grad_scores, queries[i], 1, 0)
        grad_queries[i] = grad_queries[i] + contract(keys_t[j], grad_scores, 1, 0)
        return grad_key, grad_value

    for j in range(lower, upper):
        zero = jnp.zeros((block, head_dim), f32)
        carry = step(j, j, (zero, zero), True)
        grad_key, grad_value = lax.fori_loop(
            j + 1, count, lambda i, c, j=j: step(i, j, c, False), carry
        )
        for part in range(per_block):
            span = slice(part * rows, (part + 1) * rows)
            result_ref[j * per_block + part, 1] = grad_key[span].T.astype(bf16)
            result_ref[j * per_block + part, 2] = grad_value[span].T.astype(bf16)
    if not last:
        for number in range(lower, count):
            sums_ref[number - lower] = grad_queries[number]
        for piece in range(lower * per_block, pieces):
            result_ref[piece, 0] = jnp.zeros((head_dim, rows), bf16)
        return
    sums_ref[0] = jnp.zeros((head_dim, block), f32)
    for piece in range(pieces):
        number, part = divmod(piece, per_block)
        span = slice(part * rows, (part + 1) * rows)
        result_ref[piece, 0] = (grad_queries[number, :, span] * scale).astype(bf16)
        if number >= upper:
            result_ref[piece, 1:] = earlier[0][piece, 1:]


def attend_forward(qkv, block):
    pieces, _, head_dim, rows = qkv.shape
    count = pieces * rows // block
    pairs = count * (count + 1) // 2 * block * block
    in_vmem = pl.BlockSpec(memory_space=pltpu.VMEM)
    by_rows = pltpu.VMEM((count, block, head_dim), bf16)
    by_features = pltpu.VMEM((count, head_dim, block), bf16)
    return pl.pallas_call(
        functools.partial(forward_kernel, block=block),
        out_shape=(
            jax.ShapeDtypeStruct((pieces, head_dim, rows), bf16),
            jax.ShapeDtypeStruct((count, 1, block), f32),
        ),
        in_specs=[in_vmem],
        out_specs=(in_vmem, in_vmem),
        scratch_shapes=[by_rows, by_features, by_features],
        compiler_params=pltpu.CompilerParams(vmem_limit_bytes=56 * 2**20),
        cost_estimate=lasting(18),
        name="attend_forward",
    )(qkv)


def attend_backward(qkv, grad, out, logsum, block, lower, upper, earlier=()):
    pieces, _, head_dim, rows = qkv.shape
    count = pieces * rows // block
    last = lower == 0
    sums = 1 if last else count - lower
    by_rows = pltpu.VMEM((count, block, head_dim), bf16)
    by_features = pltpu.VMEM((count, head_dim, block), bf16)
    return pl.pallas_call(
        functools.partial(backward_kernel, lower, upper, last, block, head_dim**-0.5),
        out_shape=(
            jax.ShapeDtypeStruct(qkv.shape, bf16),
            jax.ShapeDtypeStruct((sums, head_dim, block), f32),
        ),
        in_specs=[IN_VMEM] * (4 + len(earlier)),
        out_specs=(IN_VMEM, IN_VMEM),
        scratch_shapes=[by_rows] * 4
        + [by_features] * 3
        + [pltpu.VMEM((count, 1, block), f32), pltpu.VMEM((count, head_dim, block), f32)],
        compiler_params=pltpu.CompilerParams(vmem_limit_bytes=60 * 2**20),
        cost_estimate=lasting(18),
        name="attend_backward",
    )(qkv, grad, out, logsum, *earlier)


def start_pieces(refs, table, starts_ref, whole, semaphores):
    copies = []
    for number, (which, first, rows, *column) in enumerate(table):
        start = pl.multiple_of(starts_ref[number], rows)
        copy = pltpu.make_async_copy(
            refs[which].at[pl.ds(first, rows), pl.ds(sum(column), whole.shape[1])],
            whole.at[pl.ds(start, rows), :],
            semaphores.at[number],
        )
        copy.start()
        copies.append(copy)
    return copies


def qkv_kernel(count, table, starts_ref, x_ref, cosine_ref, sine_ref, *refs):
    pieces, (unit_ref, out_ref), (weight, weight_t, semaphores) = refs[:count], refs[-5:-3], refs[-3:]
    heads, blocks, _, head_dim, rows = out_ref.shape
    half = head_dim // 2
    copies = start_pieces(pieces, table, starts_ref, weight, semaphores)
    for number in range(blocks):
        span = slice(number * rows, (number + 1) * rows)
        x = x_ref[span].astype(f32)
        factor = lax.rsqrt(jnp.mean(x * x, axis=-1, keepdims=True) + epsilon)
        unit_ref[span] = (x * factor).astype(bf16)
    for copy in copies:
        copy.wait()
    weight_t[...] = weight[...].T
    step = 2
    for first in range(0, blocks, step):
        span = slice(first * rows, (first + step) * rows)
        made = contract(weight_t[...], unit_ref[span], 1, 1)
        cosine, sine = cosine_ref[:, span], sine_ref[:, span]
        for kind in range(3):
            for head in range(heads):
                at = (kind * heads + head) * head_dim
                upper, lower = made[at : at + half], made[at + half : at + head_dim]
                if kind < 2:
                    upper, lower = upper * cosine - lower * sine, lower * cosine + upper * sine
                upper, lower = upper.astype(bf16), lower.astype(bf16)
                if kind == 0:
                    upper, lower = upper * bf16(head_dim**-0.5), lower * bf16(head_dim**-0.5)
                for part in range(step):
                    lanes = slice(part * rows, (part + 1) * rows)
                    out_ref[head, first + part, kind, :half] = upper[:, lanes]
                    out_ref[head, first + part, kind, half:] = lower[:, lanes]


def project(x_group, cosine, sine, pieces, table, starts, heads, head_dim, rows):
    tokens, width = x_group.shape
    columns = pieces[0].shape[1]
    return pl.pallas_call(
        functools.partial(qkv_kernel, len(pieces), table),
        out_shape=(
            jax.ShapeDtypeStruct((tokens, width), bf16),
            jax.ShapeDtypeStruct((heads, tokens // rows, 3, head_dim, rows), bf16),
        ),
        in_specs=[IN_SMEM] + [IN_VMEM] * 3 + [ANYWHERE] * len(pieces),
        out_specs=(IN_VMEM, IN_VMEM),
        scratch_shapes=[
            pltpu.VMEM((width, columns), bf16),
            pltpu.VMEM((columns, width), bf16),
            pltpu.SemaphoreType.DMA((len(table),)),
        ],
        compiler_params=pltpu.CompilerParams(vmem_limit_bytes=48 * 2**20),
        cost_estimate=lasting(10),
        name="project",
    )(starts, x_group, cosine, sine, *pieces)


def mid_kernel(count, table, groups, starts_ref, x_ref, attended_ref, *refs):
    pieces, (mid_ref, normed_ref, gain_ref) = refs[:count], refs[-6:-3]
    weight, attended, semaphores = refs[-3:]
    copies = start_pieces(pieces, table, starts_ref, weight, semaphores)
    _, head_dim, rows = attended_ref.shape
    width = x_ref.shape[1]
    tensor = HEADS // groups
    pair = 128 // head_dim
    for first in range(0, HEADS, pair):
        features = jnp.concatenate(
            [
                attended_ref[head % groups * tensor + head // groups]
                for head in range(first, first + pair)
            ]
        )
        attended[:, first * head_dim : (first + pair) * head_dim] = features.T
    for copy in copies:
        copy.wait()
    cut = min(512, width)
    for start in range(0, width, cut):
        span = slice(start, start + cut)
        gain_ref[:, span] = weight[span, width:].astype(f32).T[:1]
        mid_ref[:, span] = x_ref[:, span].astype(f32) + contract(
            attended[...], weight[span, :width], 1, 1
        )
    mid = mid_ref[...]
    factor = lax.rsqrt(jnp.mean(mid * mid, axis=-1, keepdims=True) + epsilon)
    normed_ref[...] = (mid * factor * gain_ref[...]).astype(bf16)


def finish_attention(x, attended, pieces, table, starts, groups):
    rows, width = x.shape
    return pl.pallas_call(
        functools.partial(mid_kernel, len(pieces), table, groups),
        out_shape=(
            jax.ShapeDtypeStruct((rows, width), f32),
            jax.ShapeDtypeStruct((rows, width), bf16),
            jax.ShapeDtypeStruct((1, width), f32),
        ),
        in_specs=[IN_SMEM] + [IN_VMEM] * 2 + [ANYWHERE] * len(pieces),
        out_specs=(IN_VMEM,) * 3,
        scratch_shapes=[
            pltpu.VMEM((width, pieces[0].shape[1]), bf16),
            pltpu.VMEM((rows, width), bf16),
            pltpu.SemaphoreType.DMA((len(table),)),
        ],
        compiler_params=pltpu.CompilerParams(vmem_limit_bytes=48 * 2**20),
        cost_estimate=lasting(9),
        name="finish_attention",
    )(starts, x, attended, *pieces)


def grad_mid_kernel(count, table, groups, starts_ref, mid_ref, grad_ref, cotangent_ref, gain_ref, *refs):
    pieces, (grad_mid_ref, low_ref, gain_part_ref, out_ref) = refs[:count], refs[-6:-2]
    weight, semaphores = refs[-2:]
    copies = start_pieces(pieces, table, starts_ref, weight, semaphores)
    _, head_dim, rows = out_ref.shape
    width = mid_ref.shape[1]
    tensor = HEADS // groups
    pair = 128 // head_dim
    mid, grad = mid_ref[...], grad_ref[...]
    factor = lax.rsqrt(jnp.mean(mid * mid, axis=-1, keepdims=True) + epsilon)
    weighted = grad * gain_ref[...]
    inner = jnp.mean(weighted * mid, axis=-1, keepdims=True)
    grad_mid = (
        cotangent_ref[...].astype(f32) + factor * weighted - mid * (factor * factor * factor * inner)
    )
    grad_mid_ref[...] = grad_mid
    low_ref[...] = grad_mid.astype(bf16)
    gain_part_ref[...] = jnp.sum(grad * (mid * factor), axis=0, keepdims=True)
    for copy in copies:
        copy.wait()
    cut = min(512, width)
    for start in range(0, width, cut):
        made = contract(low_ref[...], weight[:, start : start + cut], 1, 0).astype(bf16)
        for at in range(0, cut, pair * head_dim):
            features = made[:, at : at + pair * head_dim].T
            for part in range(pair):
                head = (start + at) // head_dim + part
                out_ref[head % groups * tensor + head // groups] = features[
                    part * head_dim : (part + 1) * head_dim
                ]


def back_to_attention(mid, grad, cotangent, gain, pieces, table, starts, groups, head_dim):
    rows, width = mid.shape
    return pl.pallas_call(
        functools.partial(grad_mid_kernel, len(pieces), table, groups),
        out_shape=(
            jax.ShapeDtypeStruct((rows, width), f32),
            jax.ShapeDtypeStruct((rows, width), bf16),
            jax.ShapeDtypeStruct((1, width), f32),
            jax.ShapeDtypeStruct((HEADS, head_dim, rows), bf16),
        ),
        in_specs=[IN_SMEM] + [IN_VMEM] * 4 + [ANYWHERE] * len(pieces),
        out_specs=(IN_VMEM,) * 4,
        scratch_shapes=[
            pltpu.VMEM((width, width), bf16),
            pltpu.SemaphoreType.DMA((len(table),)),
        ],
        compiler_params=pltpu.CompilerParams(vmem_limit_bytes=48 * 2**20),
        cost_estimate=lasting(6),
        name="back_to_attention",
    )(starts, mid, grad, cotangent, gain, *pieces)


def write_parts(place_ref, count, rows_of, outs):
    if len(outs) == 1:
        for group in range(count):
            block = rows_of(group)
            outs[0][group * block.shape[0] : (group + 1) * block.shape[0]] = block
        return
    to_beside, to_across, beside_low, across_top, own = outs
    half = own.shape[0] // 2
    block = rows_of(place_ref[0] ^ 3)
    to_beside[:half] = block[:half]
    to_across[:half] = block[half:]
    block = rows_of(place_ref[0] ^ 1)
    to_beside[half:] = block[:half]
    beside_low[...] = block[half:]
    block = rows_of(place_ref[0] ^ 2)
    to_across[half:] = block[half:]
    across_top[...] = block[:half]
    own[...] = rows_of(place_ref[0])


def part_shapes(rows, columns, square):
    if not square:
        return [jax.ShapeDtypeStruct((rows, columns), bf16)]
    own = rows // 4
    return [
        jax.ShapeDtypeStruct((each, columns), bf16) for each in (own, own, own // 2, own // 2, own)
    ]


def turn_back_kernel(count, place_ref, grad_ref, cosine_ref, sine_ref, unit_ref, by_tokens_ref, *refs):
    outs, low = refs[:-1], refs[-1]
    heads, blocks, _, head_dim, rows = grad_ref.shape
    half = head_dim // 2
    for block in range(blocks):
        span = slice(block * rows, (block + 1) * rows)
        cosine, sine = cosine_ref[:, span], sine_ref[:, span]
        for kind in range(3):
            for head in range(heads):
                at = (kind * heads + head) * head_dim
                grad = grad_ref[head, block, kind]
                if kind < 2:
                    grad = grad.astype(f32)
                    upper, lower = grad[:half], grad[half:]
                    grad = jnp.concatenate(
                        [upper * cosine + lower * sine, lower * cosine - upper * sine]
                    ).astype(bf16)
                low[at : at + head_dim, span] = grad
        by_tokens_ref[block] = low[:, span].T
    each = unit_ref.shape[1] // count

    def rows_of(group):
        start = group * each if isinstance(group, int) else pl.multiple_of(group * each, each)
        return contract(unit_ref[:, pl.ds(start, each)], low[...], 0, 1).astype(bf16)

    write_parts(place_ref, count, rows_of, outs)


def turn_back(grad, cosine, sine, unit_group, place, count, square):
    heads, blocks, _, head_dim, rows = grad.shape
    columns = 3 * heads * head_dim
    shapes = part_shapes(unit_group.shape[1], columns, square)
    by_tokens, *parts = pl.pallas_call(
        functools.partial(turn_back_kernel, count),
        out_shape=[jax.ShapeDtypeStruct((blocks, rows, columns), bf16), *shapes],
        in_specs=[IN_SMEM] + [IN_VMEM] * 4,
        out_specs=[IN_VMEM] * (1 + len(shapes)),
        scratch_shapes=[pltpu.VMEM((columns, blocks * rows), bf16)],
        compiler_params=pltpu.CompilerParams(vmem_limit_bytes=48 * 2**20),
        cost_estimate=lasting(8),
        name="turn_back",
    )(place, grad, cosine, sine, unit_group)
    return by_tokens, parts


def norm_kernel(count, table, starts_ref, spots_ref, by_tokens_ref, *refs):
    pieces, outs, (weight, semaphores) = refs[:count], refs[count:-2], refs[-2:]
    copies = start_pieces(pieces, table, starts_ref, weight, semaphores)
    rows = by_tokens_ref.shape[1]
    steps = len(outs) - 1
    for copy in copies:
        copy.wait()
    width = weight.shape[0]
    cut = min(1024, width)
    for step in range(steps):
        tokens = jnp.concatenate(
            [by_tokens_ref[spots_ref[2 * step]], by_tokens_ref[spots_ref[2 * step + 1]]]
        )
        for start in range(0, width, cut):
            part = contract(tokens, weight[start : start + cut], 1, 1)
            outs[step][:, start : start + cut] = part[:rows]
            outs[steps][step, :, start : start + cut] = part[rows:].astype(bf16)


def back_to_norm(by_tokens, pieces, table, starts, spots, width):
    _, rows, columns = by_tokens.shape
    steps = spots.shape[0] // 2
    made = pl.pallas_call(
        functools.partial(norm_kernel, len(pieces), table),
        out_shape=(jax.ShapeDtypeStruct((rows, width), f32),) * steps
        + (jax.ShapeDtypeStruct((steps, rows, width), bf16),),
        in_specs=[IN_SMEM] * 2 + [IN_VMEM] + [ANYWHERE] * len(pieces),
        out_specs=(IN_VMEM,) * (steps + 1),
        scratch_shapes=[
            pltpu.VMEM((width, columns), bf16),
            pltpu.SemaphoreType.DMA((len(table),)),
        ],
        compiler_params=pltpu.CompilerParams(vmem_limit_bytes=48 * 2**20),
        cost_estimate=lasting(7),
        name="back_to_norm",
    )(starts, spots, by_tokens, *pieces)
    return made[:steps], made[steps]


def weight_sums_kernel(
    sums_ref, out_sums_ref, weight_ref, gain_ref, qkv_ref, out_ref, one_ref, two_ref
):
    parts, rows, _ = sums_ref.shape
    kinds = 3
    width = out_ref.shape[1]
    features = width // parts
    gain = gain_ref[...]
    one = jnp.zeros((rows, 128), f32)
    two = jnp.zeros((rows, 128), f32)
    for part in range(parts):
        for kind in range(kinds):
            total = sums_ref[part, :, kind * features : (kind + 1) * features].astype(f32)
            at = slice(kind * width + part * features, kind * width + (part + 1) * features)
            qkv_ref[:, at] = gain * total
            product = total * weight_ref[:, at].astype(f32)
            for lanes in range(0, features, 128):
                one = one + product[:, lanes : lanes + 128]
        out_ref[:, part * features : (part + 1) * features] = out_sums_ref[
            part, :, :features
        ].astype(f32)
        two = two + out_sums_ref[part, :, features:].astype(f32)
    one_ref[...] = jnp.sum(one, axis=1, keepdims=True)
    two_ref[...] = jnp.sum(two, axis=1, keepdims=True)


def weight_sums(sums, out_sums, attn_qkv, gain):
    parts, rows, columns = sums.shape
    width = parts * columns // 3
    qkv, out, one, two = pl.pallas_call(
        weight_sums_kernel,
        out_shape=(
            jax.ShapeDtypeStruct((rows, 3 * width), f32),
            jax.ShapeDtypeStruct((rows, width), f32),
            jax.ShapeDtypeStruct((rows, 1), f32),
            jax.ShapeDtypeStruct((rows, 1), f32),
        ),
        in_specs=[IN_VMEM] * 4,
        out_specs=(IN_VMEM,) * 4,
        compiler_params=pltpu.CompilerParams(vmem_limit_bytes=32 * 2**20),
        cost_estimate=lasting(3),
        name="weight_sums",
    )(sums, out_sums, attn_qkv, gain)
    return qkv, out, one[:, 0], two[:, 0]


def out_product_kernel(spots_ref, attended_ref, gain_ref, *refs):
    blocks, (out_ref, grads, attended) = refs[:-3], refs[-3:]
    heads, _, head_dim, rows = attended_ref.shape
    width = grads.shape[1]
    for number, block in enumerate(blocks):
        grads[pl.ds(pl.multiple_of(spots_ref[number] * rows, rows), rows), :] = block[...]
        for head in range(heads):
            attended[
                head * head_dim : (head + 1) * head_dim, number * rows : (number + 1) * rows
            ] = attended_ref[head, number]
    columns = heads * head_dim
    out_ref[:, :columns] = contract(grads[...], attended[...], 0, 1).astype(bf16)
    gain = jnp.broadcast_to(gain_ref[...], (128, width)).T
    high = gain.astype(bf16).astype(f32)
    lanes = lax.broadcasted_iota(jnp.int32, gain.shape, 1)
    gain = jnp.where(lanes == 0, high, jnp.where(lanes == 1, gain - high, 0.0))
    out_ref[:, columns:] = gain.astype(bf16)


def out_product(blocks, spots, attended, gain):
    rows, width = blocks[0].shape
    heads, count, head_dim, _ = attended.shape
    return pl.pallas_call(
        out_product_kernel,
        out_shape=jax.ShapeDtypeStruct((width, heads * head_dim + 128), bf16),
        in_specs=[IN_SMEM] + [IN_VMEM] * (2 + len(blocks)),
        out_specs=IN_VMEM,
        scratch_shapes=[
            pltpu.VMEM((count * rows, width), bf16),
            pltpu.VMEM((heads * head_dim, count * rows), bf16),
        ],
        compiler_params=pltpu.CompilerParams(vmem_limit_bytes=48 * 2**20),
        cost_estimate=lasting(5),
        name="out_product",
    )(spots, attended, gain, *blocks)


def units_kernel(counts, tables, own_ref, other_ref, grad_own_ref, grad_other_ref, *refs):
    starts_refs, refs = refs[:3], refs[3:]
    pieces = (refs[: counts[0]], refs[counts[0] : sum(counts[:2])], refs[sum(counts[:2]) : sum(counts)])
    outs, weights, semaphores = refs[-15:-6], refs[-6:-3], refs[-3:]
    act_ref, grad_gate_ref, grad_up_ref, normed_ref, grads_ref = outs[:5]
    branch_keep_ref, branch_send_ref, keep_ref, send_ref = outs[5:]
    rows, width = own_ref.shape
    copies = [
        start_pieces(*each) for each in zip(pieces, tables, starts_refs, weights, semaphores)
    ]
    gate_w, up_w, down_w = weights

    def arrived(which):
        for copy in copies[which]:
            copy.wait()

    normed_ref[0, :rows] = own_ref[...]
    normed_ref[0, rows:] = other_ref[...]
    grads_ref[0, :rows] = grad_own_ref[...]
    grads_ref[0, rows:] = grad_other_ref[...]
    arrived(0)
    gate = contract(normed_ref[0], gate_w[...], 1, 1)
    sigmoid = 1.0 / (1.0 + jnp.exp(-gate))
    silu = gate * sigmoid
    arrived(1)
    up = contract(normed_ref[0], up_w[...], 1, 1)
    act_ref[0] = (silu * up).astype(bf16)
    arrived(2)
    grad_act = contract(grads_ref[0], down_w[...], 1, 1)
    grad_gate_ref[0] = (grad_act * up * sigmoid * (1.0 + gate * (1.0 - sigmoid))).astype(bf16)
    grad_up_ref[0] = (grad_act * silu).astype(bf16)
    cut = min(512, width)
    for start in range(0, width, cut):
        span = slice(start, start + cut)
        part = contract(grad_gate_ref[0], gate_w[:, span], 1, 0)
        part = part + contract(grad_up_ref[0], up_w[:, span], 1, 0)
        keep_ref[:, span] = part[:rows]
        send_ref[:, span] = part[rows:].astype(bf16)
    for start in range(0, width, cut):
        span = slice(start, start + cut)
        part = contract(act_ref[0], down_w[:, span], 1, 0)
        branch_keep_ref[0, :, span] = part[:rows]
        branch_send_ref[0, :, span] = part[rows:].astype(bf16)


def units_chunk(step, count, own, other, grad_own, grad_other, weights, held):
    rows, width = own.shape
    arrays = [array for pieces, _, _ in weights for array in pieces]
    counts = tuple(len(pieces) for pieces, _, _ in weights)
    tables = tuple(table for _, table, _ in weights)
    units = sum(entry[2] for entry in tables[0])
    whole = pl.BlockSpec((rows, width), lambda i: (0, 0))
    kept_units = pl.BlockSpec((1, 2 * rows, units), lambda i: (step, 0, 0))
    kept_rows = pl.BlockSpec((1, 2 * rows, width), lambda i: (step, 0, 0))
    by_units = jax.ShapeDtypeStruct((count, 2 * rows, units), bf16)
    by_rows = jax.ShapeDtypeStruct((count, 2 * rows, width), bf16)
    sums = tuple(jax.ShapeDtypeStruct((rows, width), kind) for kind in (f32, bf16))
    kept_branch = pl.BlockSpec((1, rows, width), lambda i: (step, 0, 0))
    branch = tuple(jax.ShapeDtypeStruct((count, rows, width), kind) for kind in (f32, bf16))
    return pl.pallas_call(
        functools.partial(units_kernel, counts, tables),
        grid=(1,),
        out_shape=(by_units,) * 3 + (by_rows,) * 2 + branch + sums,
        in_specs=[whole] * 4 + [IN_SMEM] * 3 + [ANYWHERE] * (len(arrays) + len(held)),
        out_specs=(kept_units,) * 3 + (kept_rows,) * 2 + (kept_branch,) * 2 + (whole,) * 2,
        scratch_shapes=[pltpu.VMEM((units, width), bf16)] * 3
        + [pltpu.SemaphoreType.DMA((len(table),)) for table in tables],
        input_output_aliases={7 + len(arrays) + i: i for i in range(len(held))},
        compiler_params=pltpu.CompilerParams(vmem_limit_bytes=56 * 2**20),
        cost_estimate=lasting(13),
        name="units_chunk",
    )(own, other, grad_own, grad_other, *[starts for _, _, starts in weights], *arrays, *held)


def transposed_product_kernel(left_ref, right_ref, *refs):
    refs[-1][...] = contract(left_ref[...], right_ref[...], 0, 0).astype(bf16)


def transposed_product(left, right, held=(), place=0, count=1):
    depth, units = left.shape
    width = right.shape[1]
    cut = min(256, units)
    return pl.pallas_call(
        transposed_product_kernel,
        grid=(units // cut,),
        out_shape=jax.ShapeDtypeStruct((units, count * width), bf16),
        in_specs=[
            pl.BlockSpec((depth, cut), lambda i: (0, i)),
            pl.BlockSpec((depth, width), lambda i: (0, 0)),
        ]
        + [ANYWHERE] * len(held),
        out_specs=pl.BlockSpec((cut, width), lambda i: (i, place)),
        input_output_aliases={2 + i: 0 for i in range(len(held))},
        compiler_params=pltpu.CompilerParams(vmem_limit_bytes=48 * 2**20),
        cost_estimate=lasting(9),
        name="transposed_product",
    )(left, right, *held)


def product_parts_kernel(count, place_ref, left_ref, right_ref, *outs):
    each = left_ref.shape[1] // count

    def rows_of(group):
        start = group * each if isinstance(group, int) else pl.multiple_of(group * each, each)
        return contract(left_ref[:, pl.ds(start, each)], right_ref[...], 0, 0).astype(bf16)

    write_parts(place_ref, count, rows_of, outs)


def product_parts(left, right, place, count, square):
    shapes = part_shapes(left.shape[1], right.shape[1], square)
    return pl.pallas_call(
        functools.partial(product_parts_kernel, count),
        out_shape=shapes,
        in_specs=[IN_SMEM] + [IN_VMEM] * 2,
        out_specs=[IN_VMEM] * len(shapes),
        compiler_params=pltpu.CompilerParams(vmem_limit_bytes=48 * 2**20),
        cost_estimate=lasting(10),
        name="product_parts",
    )(place, left, right)


def rotary_tables(positions, head_dim):
    half_dim = head_dim // 2
    frequency = rope_base ** (-(jnp.arange(half_dim, dtype=f32) * 2.0) / head_dim)
    angles = positions.astype(f32)[None, :] * frequency[:, None]
    return jnp.cos(angles), jnp.sin(angles)


def together(*arrays):
    return lax.optimization_barrier(arrays)


def after(array, *others):
    return lax.optimization_barrier((array, *others))[0]


def swap_cores(array):
    return lax.ppermute(array, "c", [(0, 1), (1, 0)])


def from_next(array):
    count = lax.axis_size("z")
    return lax.ppermute(array, "z", [(i, (i - 1) % count) for i in range(count)])


def from_flipped(array, bit):
    return lax.ppermute(array, "p", [(i, i ^ bit) for i in range(4)])


def square_groups():
    return lax.axis_size("p") == 4 and lax.axis_size("r") == 1


def gather_chunks(block):
    count = lax.axis_size("z")
    chunks = []
    for step in range(count):
        later = from_next(block) if step < count - 1 else None
        chunks.append((block, swap_cores(block)))
        block = later
    return chunks


def add_over_cores(keep, send):
    return keep + swap_cores(send.astype(bf16)).astype(f32)


def near_pieces(block):
    if not square_groups():
        return lax.all_gather(block, GROUPS, axis=0)
    return block, from_flipped(block, 1), from_flipped(block, 2)


def group_pieces(near):
    if not square_groups():
        return [(near[group], group, 0) for group in range(near.shape[0])]
    block, beside, across = near
    half = block.shape[0] // 2
    place = lax.axis_index("p")
    top, low = from_flipped(beside[:half], 2), from_flipped(across[half:], 1)
    return [
        (block, place, 0), (beside, place ^ 1, 0), (across, place ^ 2, 0),
        (top, place ^ 3, 0), (low, place ^ 3, half),
    ]


def placed(pieces, rows):
    table = tuple((which, 0, piece[0].shape[0]) for which, piece in enumerate(pieces))
    starts = [jnp.int32(group) * rows + first for _, group, first in pieces]
    return [array for array, _, _ in pieces], table, jnp.stack(starts).astype(jnp.int32)


def group_parts(whole):
    if not square_groups():
        return [whole]
    parts = whole.reshape(4, -1, whole.shape[1])
    place = lax.axis_index("p")
    own, beside, across, corner = (
        lax.dynamic_index_in_dim(parts, place ^ bits, 0, keepdims=False) for bits in range(4)
    )
    half = own.shape[0] // 2
    return [
        jnp.concatenate([corner[:half], beside[:half]]),
        jnp.concatenate([corner[half:], across[half:]]),
        beside[half:], across[:half], own,
    ]


def scatter_first(parts):
    if not square_groups():
        return ()
    return from_flipped(parts[0], 1), from_flipped(parts[1], 2)


def scatter_second(parts, first):
    if not square_groups():
        own = lax.psum_scatter(parts[0], GROUPS, scatter_dimension=0, tiled=True)
        return own.astype(f32)
    _, _, beside_low, across_top, own = parts
    half = own.shape[0] // 2
    from_beside, from_across = (array.astype(f32) for array in first)
    beside_low = (beside_low.astype(f32) + from_across[:half]).astype(bf16)
    across_top = (across_top.astype(f32) + from_beside[:half]).astype(bf16)
    total_low = from_across[half:] + from_flipped(beside_low, 1).astype(f32)
    total_top = from_beside[half:] + from_flipped(across_top, 2).astype(f32)
    return own.astype(f32) + jnp.concatenate([total_top, total_low])


def to_owners(own):
    count = lax.axis_size(TENSOR)
    return lax.all_to_all(own.astype(bf16).reshape(count, -1, own.shape[1]), TENSOR, 0, 0)


def shards(tokens, attn_qkv, attn_out_t, mlp_weight, norm1, norm2, cotangent):
    rows, width = tokens.shape
    group_count, share_count = lax.axis_size("p"), lax.axis_size("r")
    line_count = lax.axis_size("z")
    tensor_count = lax.axis_size("c") * line_count
    head_dim = width // HEADS
    heads_here = HEADS // tensor_count
    group_rows = rows * tensor_count
    features_here = heads_here * head_dim
    weight_rows = attn_qkv.shape[0]
    share, place, core = lax.axis_index("r"), lax.axis_index("z"), lax.axis_index("c")
    block = min(1024, group_rows)
    x = tokens.astype(f32)
    gain_one = norm1.astype(f32)[:, None]
    device_index = (share * group_count + lax.axis_index("p")) * tensor_count

    def chunk_places(step):
        along = lax.rem(place + step, line_count)
        return core * line_count + along, (1 - core) * line_count + along

    x_group = lax.all_gather(tokens, TENSOR, axis=0, tiled=True)
    scaled_qkv = (attn_qkv.astype(f32) * gain_one).astype(bf16)
    qkv_cut = scaled_qkv.reshape(weight_rows, 3, tensor_count, features_here).transpose(2, 0, 1, 3)
    qkv_cut = qkv_cut.reshape(tensor_count, weight_rows, 3 * features_here)
    gain_columns = jnp.pad(norm2[:, None], ((0, 0), (0, 127)))
    out_near = near_pieces(jnp.concatenate([attn_out_t, gain_columns], axis=1))
    gate_near = near_pieces(mlp_weight[:, :width])
    unit_rows = mlp_weight.shape[0]
    qkv_part = lax.all_to_all(qkv_cut, TENSOR, 0, 0).reshape(-1, 3 * features_here)
    qkv_part, out_near, gate_near = together(qkv_part, out_near, gate_near)
    qkv_rows = qkv_part.shape[0]
    qkv_arrays, qkv_table, qkv_starts = placed(group_pieces(near_pieces(qkv_part)), qkv_rows)
    out_pieces = group_pieces(out_near)
    out_plane = jnp.concatenate([array for array, _, _ in out_pieces])
    qkv_arrays, x_group, gate_near, out_plane = together(
        qkv_arrays, x_group, gate_near, out_plane
    )

    positions = device_index * rows + jnp.arange(group_rows)
    cosine, sine = rotary_tables(positions, head_dim)
    unit_group, stacked = project(
        x_group, cosine, sine, qkv_arrays, qkv_table, qkv_starts, heads_here, head_dim, rows
    )
    gate_weight = placed(group_pieces(gate_near), unit_rows)
    stacked, gate_arrays, later = together(stacked, gate_weight[0], from_next(out_plane))
    gate_weight = (gate_arrays, *gate_weight[1:])
    out_ring = [out_plane, later]
    swapped = [swap_cores(array) for array in after(out_ring, stacked)]
    qkv = lax.all_to_all(stacked, "p", 0, 0)
    qkv, later, swapped = together(qkv, from_next(out_ring[-1]), swapped)
    qkv = qkv.reshape(-1, 3, head_dim, rows)
    out_ring.append(later)
    rest_whole = lax.all_gather(
        after(mlp_weight[:, width:], qkv_arrays), GROUPS, axis=0, tiled=True
    )
    up_weight, down_weight = (
        ([rest_whole], ((0, 0, rest_whole.shape[0], column),), jnp.zeros((1,), jnp.int32))
        for column in (0, width)
    )

    def over_shares(array):
        return lax.all_gather(array, "r", axis=0, tiled=True) if share_count > 1 else array

    def own_share(array):
        if share_count == 1:
            return array
        pieces = group_count * tensor_count
        return lax.dynamic_slice_in_dim(array, share * pieces, pieces, 0)

    qkv = over_shares(qkv)
    rest = [out_ring[-1]]
    for _ in range(line_count - 3):
        rest.append(from_next(rest[-1]))
    swapped.append(swap_cores(out_ring[-1]))
    attended, logsum = attend_forward(qkv, block)
    attended, rest, swapped = together(attended, rest[1:], swapped)
    out_ring += rest
    swapped += [swap_cores(array) for array in rest]
    attended_head = own_share(attended)

    out_table, out_starts = [], []
    for which in range(2 * line_count):
        side = core if which < line_count else 1 - core
        along = lax.rem(place + which % line_count, line_count)
        first = 0
        for array, group, offset in out_pieces:
            out_table.append((which, first, array.shape[0]))
            spot = (jnp.int32(group) * 2 + side) * line_count + along
            out_starts.append(spot * weight_rows + offset)
            first += array.shape[0]
    out_table, out_starts = tuple(out_table), jnp.stack(out_starts).astype(jnp.int32)

    attended_local = lax.all_to_all(attended_head, ("p", "c", "z"), 0, 0)
    later = from_next(after(cotangent, attended))
    attended_local, swapped = together(attended_local, swapped)
    out_weight = (out_ring + swapped, out_table, out_starts)
    grad_out_ring = [cotangent, later, from_next(after(later, attended_local))]
    middle, normed_two, gain_two = finish_attention(
        tokens, attended_local, *out_weight, HEADS // tensor_count
    )
    normed_two, grad_out_ring = together(normed_two, grad_out_ring)
    attended_group = attended_head.reshape(group_count, tensor_count, head_dim, rows)
    attended_group = lax.all_to_all(after(attended_group, normed_two), "p", 0, 0)

    held = ()
    normed, grad_out, came, total = normed_two, grad_out_ring[0], (), None
    for step in range(line_count):
        later = from_next(normed) if step < line_count - 1 else ()
        if step < line_count - 3:
            grad_out_ring.append(from_next(grad_out_ring[-1]))
        if step >= 2:
            came = from_next(total.astype(bf16))
        *held, keep, send = units_chunk(
            step, line_count, normed, swap_cores(normed), grad_out, swap_cores(grad_out),
            (gate_weight, up_weight, down_weight), held,
        )
        if step == 0:
            later, attended_group, keep, send = together(later, attended_group, keep, send)
        else:
            later, came, keep, send = together(later, came, keep, send)
        keep, grad_out_ring = together(keep, grad_out_ring)
        part = add_over_cores(keep, send)
        normed = later
        if step < line_count - 1:
            grad_out = grad_out_ring[step + 1]
        if step == 0:
            own_part = part
        else:
            total = part if step == 1 else came.astype(f32) + part
    activation, gate_grads, up_grads, normed_group, grad_out_group = (
        array.reshape(group_rows, -1) for array in held[:5]
    )
    branch_keep, branch_send = held[5:]

    def over_groups(part):
        return lax.psum_scatter(part, GROUPS, scatter_dimension=0, tiled=True)

    gate_term = transposed_product(after(gate_grads, total), normed_group)
    came, gate_term = together(from_next(total.astype(bf16)), gate_term)
    grad_normed = came.astype(f32) + own_part
    grad_middle, grad_mid_low, norm_two_part, grad_attended = back_to_attention(
        middle, grad_normed, cotangent, gain_two, *out_weight,
        HEADS // tensor_count, head_dim,
    )
    grad_head = lax.all_to_all(grad_attended, ("p", "c", "z"), 0, 0)
    up_term = transposed_product(after(up_grads, grad_attended), normed_group)
    group_place = lax.axis_index("p").astype(jnp.int32)[None]
    group_all = share_count * group_count
    branch_came = swap_cores(after(branch_send, grad_attended))
    grad_head, up_term, branch_came = together(grad_head, up_term, branch_came)

    def branch_sum(came, step):
        return came + branch_keep[step] + branch_came[step].astype(f32)

    grad_head = over_shares(grad_head)
    grad_gate_w, grad_up_w = over_groups(gate_term), over_groups(up_term)
    count = qkv.shape[0] * rows // block
    backward = functools.partial(attend_backward, qkv, grad_head, attended, logsum, block)
    later_keys = backward(count // 2, count)
    grad_mid_ring = [grad_mid_low, from_next(after(grad_mid_low, grad_head))]
    mid_swapped = [swap_cores(after(grad_mid_low, grad_head))]
    later_keys, grad_mid_ring, mid_swapped = together(later_keys, grad_mid_ring, mid_swapped)
    grad_qkv_head = backward(0, count // 2, later_keys)[0]
    mid_swapped += [swap_cores(array) for array in grad_mid_ring[1:]]
    for _ in range(line_count - 3):
        grad_mid_ring.append(from_next(grad_mid_ring[-1]))
    came = from_next(after(branch_sum(0.0, 1 % line_count).astype(bf16), later_keys))
    grad_qkv_head, grad_mid_ring, came, mid_swapped, grad_gate_w = together(
        grad_qkv_head, grad_mid_ring, came, mid_swapped, grad_gate_w
    )
    grad_qkv_head = own_share(grad_qkv_head)

    spots = jnp.stack([spot for step in range(line_count) for spot in chunk_places(step)])
    spots = spots.astype(jnp.int32)
    grad_qkv_rows = grad_qkv_head.reshape(group_count, tensor_count, 3, head_dim, rows)
    grad_qkv_rows = lax.all_to_all(grad_qkv_rows, "p", 0, 0)
    mid_swapped += [swap_cores(array) for array in grad_mid_ring[2:]]
    grad_mid_ring.append(from_next(grad_mid_ring[-1]))
    for step in range(2, line_count - 1):
        came = from_next(branch_sum(came.astype(f32), step).astype(bf16))
    grad_qkv_rows, mid_swapped = together(grad_qkv_rows, mid_swapped)
    grad_qkv_low, qkv_parts = turn_back(
        grad_qkv_rows, cosine, sine, unit_group, group_place, group_all, square_groups()
    )
    grad_qkv_low, qkv_parts, grad_mid_ring, came = together(
        grad_qkv_low, qkv_parts, grad_mid_ring, came
    )
    qkv_first = scatter_first(qkv_parts)
    branch_last = branch_sum(came.astype(f32), line_count - 1) if line_count > 2 else came
    branch_last = from_next(branch_last.astype(bf16))
    keep, send = back_to_norm(
        grad_qkv_low, qkv_arrays, qkv_table, qkv_starts, spots, width
    )
    keep, send, branch_last, qkv_first = together(keep, send, branch_last, qkv_first)
    swapped = swap_cores(send)
    total = keep[1 % line_count] + swapped[1 % line_count].astype(f32)
    came = from_next(total.astype(bf16))
    mid_swapped.append(swap_cores(after(grad_mid_ring[-1], total)))
    grad_mid_blocks = [
        part for pair in zip(grad_mid_ring, mid_swapped, strict=True) for part in pair
    ]
    out_term = out_product(grad_mid_blocks, spots, attended_group, norm_two_part)
    down_parts = product_parts(
        after(activation, total), grad_out_group, group_place, group_all, square_groups()
    )
    qkv_own = scatter_second(qkv_parts, after(qkv_first, total)).astype(bf16)
    came, qkv_own, out_term, down_parts, grad_up_w = together(
        came, qkv_own, out_term, down_parts, grad_up_w
    )
    qkv_sums = to_owners(qkv_own)
    total = came.astype(f32) + keep[2 % line_count] + swapped[2 % line_count].astype(f32)
    came = from_next(total.astype(bf16))
    out_parts = group_parts(out_term)
    out_first = scatter_first(out_parts)
    down_first = scatter_first(down_parts)
    came, out_first = together(came, out_first)
    for step in range(3, line_count):
        total = came.astype(f32) + keep[step] + swapped[step].astype(f32)
        came = from_next(total.astype(bf16))
    out_own = scatter_second(out_parts, out_first)
    came, down_first, out_own, qkv_sums = together(came, down_first, out_own, qkv_sums)
    out_sums = to_owners(out_own)
    weighted_one = came.astype(f32) + keep[0] + swapped[0].astype(f32)
    grad_down_w = scatter_second(down_parts, down_first)
    grad_mlp = jnp.concatenate(
        [grad_gate_w.astype(f32), grad_up_w.astype(f32), grad_down_w.astype(f32)], axis=1
    )
    result = (middle + branch_sum(branch_last.astype(f32), 0)).astype(bf16)
    factor_one = lax.rsqrt(jnp.mean(x * x, axis=-1, keepdims=True) + epsilon)
    grad_tokens = (
        grad_middle
        + factor_one * weighted_one
        - x * factor_one**3 * jnp.mean(weighted_one * x, axis=-1, keepdims=True)
    )
    grad_qkv, grad_out_w, grad_norm_one, grad_norm_two = weight_sums(
        qkv_sums, out_sums, attn_qkv, gain_one
    )
    return (result, grad_tokens, grad_qkv, grad_out_w, grad_mlp, grad_norm_one, grad_norm_two)


def solution(mesh):
    seq_count, fsdp_count = mesh.shape["seq"], mesh.shape["fsdp"]
    groups = seq_count // 2
    heads_here = HEADS // (2 * fsdp_count)
    dealt = min(groups, heads_here)
    fine = Mesh(mesh.devices.reshape(groups // dealt, dealt, 2, fsdp_count), ALL)
    by_rows, by_items = P(ALL, None), P(ALL)
    in_specs = (by_rows, by_rows, by_rows, by_rows, by_items, by_items, by_rows)
    out_specs = (by_rows, by_rows, by_rows, by_rows, by_rows, by_items, by_items)
    return jax.shard_map(shards, mesh=fine, in_specs=in_specs, out_specs=out_specs, check_vma=False)
```

```python
import functools

import jax
import jax.numpy as jnp
from jax import lax
from jax.experimental import pallas as pl
from jax.experimental.pallas import tpu as pltpu
from jax.sharding import Mesh
from jax.sharding import PartitionSpec as P

HEADS = 32
epsilon = 1e-05
rope_base = 130000.0
f32 = jnp.float32
bf16 = jnp.bfloat16


def lasting(microseconds):
    return pl.CostEstimate(
        flops=int(microseconds * 1.1e9), bytes_accessed=1000, transcendentals=0
    )


IN_VMEM = pl.BlockSpec(memory_space=pltpu.VMEM)
IN_SMEM = pl.BlockSpec(memory_space=pltpu.SMEM)
ANYWHERE = pl.BlockSpec(memory_space=pl.ANY)
ALL = ("r", "p", "c", "z")
GROUPS = ("r", "p")
TENSOR = ("c", "z")


def contract(left, right, left_dim, right_dim):
    return lax.dot_general(
        left, right, (((left_dim,), (right_dim,)), ((), ())), preferred_element_type=f32
    )


def causal(scores):
    keys = lax.broadcasted_iota(jnp.int32, scores.shape, 0)
    queries = lax.broadcasted_iota(jnp.int32, scores.shape, 1)
    return jnp.where(keys <= queries, scores, -1e30)


def repeat(first, last, step, carry):
    if not isinstance(last, int) or last - first > 4:
        return lax.fori_loop(first, last, step, carry)
    for number in range(first, last):
        carry = step(number, carry)
    return carry


def forward_kernel(qkv_ref, out_ref, logsum_ref, keys, values_t, queries_t, *, block):
    pieces, _, head_dim, rows = qkv_ref.shape
    per_block = block // rows
    count = pieces // per_block
    for piece in range(pieces):
        number, part = divmod(piece, per_block)
        span = slice(part * rows, (part + 1) * rows)
        queries_t[number, :, span] = qkv_ref[piece, 0]
        keys[number, span, :] = qkv_ref[piece, 1].T
        values_t[number, :, span] = qkv_ref[piece, 2]

    def step(i, j, carry, diagonal):
        largest, total, result = carry
        scores = contract(keys[j], queries_t[i], 1, 0)
        if diagonal:
            scores = causal(scores)
        new_largest = jnp.maximum(largest, jnp.max(scores, axis=0, keepdims=True))
        shrink = jnp.exp(largest - new_largest)
        weights = jnp.exp(scores - new_largest)
        total = total * shrink + jnp.sum(weights, axis=0, keepdims=True)
        result = result * shrink + contract(values_t[j], weights.astype(bf16), 1, 0)
        return new_largest, total, result

    def query_block(i, _):
        carry = (
            jnp.full((1, block), -1e30, f32),
            jnp.zeros((1, block), f32),
            jnp.zeros((head_dim, block), f32),
        )
        carry = repeat(0, i, lambda j, c: step(i, j, c, False), carry)
        largest, total, result = step(i, i, carry, True)
        result = (result / total).astype(bf16)
        for part in range(per_block):
            out_ref[i * per_block + part] = result[:, part * rows : (part + 1) * rows]
        logsum_ref[i] = largest + jnp.log(total)
        return 0

    repeat(0, count, query_block, 0)


def backward_kernel(lower, upper, last, block, scale, *refs):
    qkv_ref, grad_ref, out_ref, logsum_ref = refs[:4]
    earlier, (result_ref, sums_ref) = refs[4:-11], refs[-11:-9]
    keys, queries, values, grads, keys_t, queries_t, grads_t, deltas, grad_queries = refs[-9:]
    pieces, _, head_dim, rows = qkv_ref.shape
    per_block = block // rows
    count = pieces // per_block
    for piece in range(lower * per_block, pieces):
        number, part = divmod(piece, per_block)
        span = slice(part * rows, (part + 1) * rows)
        queries_t[number, :, span] = qkv_ref[piece, 0]
        queries[number, span, :] = qkv_ref[piece, 0].T
        if number < upper:
            keys_t[number, :, span] = qkv_ref[piece, 1]
            keys[number, span, :] = qkv_ref[piece, 1].T
            values[number, span, :] = qkv_ref[piece, 2].T
        grad = grad_ref[piece]
        grads_t[number, :, span] = grad
        grads[number, span, :] = grad.T
        deltas[number, :, span] = jnp.sum(
            grad.astype(f32) * out_ref[piece].astype(f32), axis=0, keepdims=True
        )
    for number in range(lower, count):
        if number < upper:
            grad_queries[number] = jnp.zeros((head_dim, block), f32)
        else:
            grad_queries[number] = earlier[1][number - upper]

    def step(i, j, carry, diagonal):
        grad_key, grad_value = carry
        scores = contract(keys[j], queries_t[i], 1, 0)
        if diagonal:
            scores = causal(scores)
        probs = jnp.exp(scores - logsum_ref[i])
        grad_value = grad_value + contract(probs.astype(bf16), grads[i], 1, 0)
        grad_probs = contract(values[j], grads_t[i], 1, 0)
        grad_scores = (probs * (grad_probs - deltas[i])).astype(bf16)
        grad_key = grad_key + contract(grad_scores, queries[i], 1, 0)
        grad_queries[i] = grad_queries[i] + contract(keys_t[j], grad_scores, 1, 0)
        return grad_key, grad_value

    for j in range(lower, upper):
        zero = jnp.zeros((block, head_dim), f32)
        carry = step(j, j, (zero, zero), True)
        grad_key, grad_value = repeat(
            j + 1, count, lambda i, c, j=j: step(i, j, c, False), carry
        )
        for part in range(per_block):
            span = slice(part * rows, (part + 1) * rows)
            result_ref[j * per_block + part, 1] = grad_key[span].T.astype(bf16)
            result_ref[j * per_block + part, 2] = grad_value[span].T.astype(bf16)
    if not last:
        for number in range(lower, count):
            sums_ref[number - lower] = grad_queries[number]
        for piece in range(lower * per_block, pieces):
            result_ref[piece, 0] = jnp.zeros((head_dim, rows), bf16)
        return
    sums_ref[0] = jnp.zeros((head_dim, block), f32)
    for piece in range(pieces):
        number, part = divmod(piece, per_block)
        span = slice(part * rows, (part + 1) * rows)
        result_ref[piece, 0] = (grad_queries[number, :, span] * scale).astype(bf16)
        if number >= upper:
            result_ref[piece, 1:] = earlier[0][piece, 1:]


def attend_forward(qkv, block):
    pieces, _, head_dim, rows = qkv.shape
    count = pieces * rows // block
    pairs = count * (count + 1) // 2 * block * block
    in_vmem = pl.BlockSpec(memory_space=pltpu.VMEM)
    by_rows = pltpu.VMEM((count, block, head_dim), bf16)
    by_features = pltpu.VMEM((count, head_dim, block), bf16)
    return pl.pallas_call(
        functools.partial(forward_kernel, block=block),
        out_shape=(
            jax.ShapeDtypeStruct((pieces, head_dim, rows), bf16),
            jax.ShapeDtypeStruct((count, 1, block), f32),
        ),
        in_specs=[in_vmem],
        out_specs=(in_vmem, in_vmem),
        scratch_shapes=[by_rows, by_features, by_features],
        compiler_params=pltpu.CompilerParams(vmem_limit_bytes=56 * 2**20),
        cost_estimate=lasting(18),
        name="attend_forward",
    )(qkv)


def attend_backward(qkv, grad, out, logsum, block, lower, upper, earlier=()):
    pieces, _, head_dim, rows = qkv.shape
    count = pieces * rows // block
    last = lower == 0
    sums = 1 if last else count - lower
    by_rows = pltpu.VMEM((count, block, head_dim), bf16)
    by_features = pltpu.VMEM((count, head_dim, block), bf16)
    return pl.pallas_call(
        functools.partial(backward_kernel, lower, upper, last, block, head_dim**-0.5),
        out_shape=(
            jax.ShapeDtypeStruct(qkv.shape, bf16),
            jax.ShapeDtypeStruct((sums, head_dim, block), f32),
        ),
        in_specs=[IN_VMEM] * (4 + len(earlier)),
        out_specs=(IN_VMEM, IN_VMEM),
        scratch_shapes=[by_rows] * 4
        + [by_features] * 3
        + [pltpu.VMEM((count, 1, block), f32), pltpu.VMEM((count, head_dim, block), f32)],
        compiler_params=pltpu.CompilerParams(vmem_limit_bytes=60 * 2**20),
        cost_estimate=lasting(18),
        name="attend_backward",
    )(qkv, grad, out, logsum, *earlier)


def start_pieces(refs, table, starts_ref, whole, semaphores):
    copies = []
    for number, (which, first, rows, *column) in enumerate(table):
        start = pl.multiple_of(starts_ref[number], rows)
        copy = pltpu.make_async_copy(
            refs[which].at[pl.ds(first, rows), pl.ds(sum(column), whole.shape[1])],
            whole.at[pl.ds(start, rows), :],
            semaphores.at[number],
        )
        copy.start()
        copies.append(copy)
    return copies


def qkv_kernel(count, table, starts_ref, x_ref, cosine_ref, sine_ref, *refs):
    pieces, (unit_ref, out_ref), (weight, weight_t, semaphores) = refs[:count], refs[-5:-3], refs[-3:]
    heads, blocks, _, head_dim, rows = out_ref.shape
    half = head_dim // 2
    copies = start_pieces(pieces, table, starts_ref, weight, semaphores)
    for number in range(blocks):
        span = slice(number * rows, (number + 1) * rows)
        x = x_ref[span].astype(f32)
        factor = lax.rsqrt(jnp.mean(x * x, axis=-1, keepdims=True) + epsilon)
        unit_ref[span] = (x * factor).astype(bf16)
    for copy in copies:
        copy.wait()
    weight_t[...] = weight[...].T
    step = 2
    for first in range(0, blocks, step):
        span = slice(first * rows, (first + step) * rows)
        made = contract(weight_t[...], unit_ref[span], 1, 1)
        cosine, sine = cosine_ref[:, span], sine_ref[:, span]
        for kind in range(3):
            for head in range(heads):
                at = (kind * heads + head) * head_dim
                upper, lower = made[at : at + half], made[at + half : at + head_dim]
                if kind < 2:
                    upper, lower = upper * cosine - lower * sine, lower * cosine + upper * sine
                upper, lower = upper.astype(bf16), lower.astype(bf16)
                if kind == 0:
                    upper, lower = upper * bf16(head_dim**-0.5), lower * bf16(head_dim**-0.5)
                for part in range(step):
                    lanes = slice(part * rows, (part + 1) * rows)
                    out_ref[head, first + part, kind, :half] = upper[:, lanes]
                    out_ref[head, first + part, kind, half:] = lower[:, lanes]


def project(x_group, cosine, sine, pieces, table, starts, heads, head_dim, rows):
    tokens, width = x_group.shape
    columns = pieces[0].shape[1]
    return pl.pallas_call(
        functools.partial(qkv_kernel, len(pieces), table),
        out_shape=(
            jax.ShapeDtypeStruct((tokens, width), bf16),
            jax.ShapeDtypeStruct((heads, tokens // rows, 3, head_dim, rows), bf16),
        ),
        in_specs=[IN_SMEM] + [IN_VMEM] * 3 + [ANYWHERE] * len(pieces),
        out_specs=(IN_VMEM, IN_VMEM),
        scratch_shapes=[
            pltpu.VMEM((width, columns), bf16),
            pltpu.VMEM((columns, width), bf16),
            pltpu.SemaphoreType.DMA((len(table),)),
        ],
        compiler_params=pltpu.CompilerParams(vmem_limit_bytes=48 * 2**20),
        cost_estimate=lasting(10),
        name="project",
    )(starts, x_group, cosine, sine, *pieces)


def mid_kernel(count, table, groups, starts_ref, x_ref, attended_ref, *refs):
    pieces, (mid_ref, normed_ref, gain_ref) = refs[:count], refs[-6:-3]
    weight, attended, semaphores = refs[-3:]
    copies = start_pieces(pieces, table, starts_ref, weight, semaphores)
    _, head_dim, rows = attended_ref.shape
    width = x_ref.shape[1]
    tensor = HEADS // groups
    pair = 128 // head_dim
    for first in range(0, HEADS, pair):
        features = jnp.concatenate(
            [
                attended_ref[head % groups * tensor + head // groups]
                for head in range(first, first + pair)
            ]
        )
        attended[:, first * head_dim : (first + pair) * head_dim] = features.T
    for copy in copies:
        copy.wait()
    cut = min(512, width)
    for start in range(0, width, cut):
        span = slice(start, start + cut)
        gain_ref[:, span] = weight[span, width:].astype(f32).T[:1]
        mid_ref[:, span] = x_ref[:, span].astype(f32) + contract(
            attended[...], weight[span, :width], 1, 1
        )
    mid = mid_ref[...]
    factor = lax.rsqrt(jnp.mean(mid * mid, axis=-1, keepdims=True) + epsilon)
    normed_ref[...] = (mid * factor * gain_ref[...]).astype(bf16)


def finish_attention(x, attended, pieces, table, starts, groups):
    rows, width = x.shape
    return pl.pallas_call(
        functools.partial(mid_kernel, len(pieces), table, groups),
        out_shape=(
            jax.ShapeDtypeStruct((rows, width), f32),
            jax.ShapeDtypeStruct((rows, width), bf16),
            jax.ShapeDtypeStruct((1, width), f32),
        ),
        in_specs=[IN_SMEM] + [IN_VMEM] * 2 + [ANYWHERE] * len(pieces),
        out_specs=(IN_VMEM,) * 3,
        scratch_shapes=[
            pltpu.VMEM((width, pieces[0].shape[1]), bf16),
            pltpu.VMEM((rows, width), bf16),
            pltpu.SemaphoreType.DMA((len(table),)),
        ],
        compiler_params=pltpu.CompilerParams(vmem_limit_bytes=48 * 2**20),
        cost_estimate=lasting(9),
        name="finish_attention",
    )(starts, x, attended, *pieces)


def grad_mid_kernel(count, table, groups, starts_ref, mid_ref, grad_ref, cotangent_ref, gain_ref, *refs):
    pieces, (grad_mid_ref, low_ref, gain_part_ref, out_ref) = refs[:count], refs[-6:-2]
    weight, semaphores = refs[-2:]
    copies = start_pieces(pieces, table, starts_ref, weight, semaphores)
    _, head_dim, rows = out_ref.shape
    width = mid_ref.shape[1]
    tensor = HEADS // groups
    pair = 128 // head_dim
    mid, grad = mid_ref[...], grad_ref[...]
    factor = lax.rsqrt(jnp.mean(mid * mid, axis=-1, keepdims=True) + epsilon)
    weighted = grad * gain_ref[...]
    inner = jnp.mean(weighted * mid, axis=-1, keepdims=True)
    grad_mid = (
        cotangent_ref[...].astype(f32) + factor * weighted - mid * (factor * factor * factor * inner)
    )
    grad_mid_ref[...] = grad_mid
    low_ref[...] = grad_mid.astype(bf16)
    gain_part_ref[...] = jnp.sum(grad * (mid * factor), axis=0, keepdims=True)
    for copy in copies:
        copy.wait()
    cut = min(512, width)
    for start in range(0, width, cut):
        made = contract(low_ref[...], weight[:, start : start + cut], 1, 0).astype(bf16)
        for at in range(0, cut, pair * head_dim):
            features = made[:, at : at + pair * head_dim].T
            for part in range(pair):
                head = (start + at) // head_dim + part
                out_ref[head % groups * tensor + head // groups] = features[
                    part * head_dim : (part + 1) * head_dim
                ]


def back_to_attention(mid, grad, cotangent, gain, pieces, table, starts, groups, head_dim):
    rows, width = mid.shape
    return pl.pallas_call(
        functools.partial(grad_mid_kernel, len(pieces), table, groups),
        out_shape=(
            jax.ShapeDtypeStruct((rows, width), f32),
            jax.ShapeDtypeStruct((rows, width), bf16),
            jax.ShapeDtypeStruct((1, width), f32),
            jax.ShapeDtypeStruct((HEADS, head_dim, rows), bf16),
        ),
        in_specs=[IN_SMEM] + [IN_VMEM] * 4 + [ANYWHERE] * len(pieces),
        out_specs=(IN_VMEM,) * 4,
        scratch_shapes=[
            pltpu.VMEM((width, width), bf16),
            pltpu.SemaphoreType.DMA((len(table),)),
        ],
        compiler_params=pltpu.CompilerParams(vmem_limit_bytes=48 * 2**20),
        cost_estimate=lasting(6),
        name="back_to_attention",
    )(starts, mid, grad, cotangent, gain, *pieces)


def write_parts(place_ref, count, rows_of, outs):
    if len(outs) == 1:
        for group in range(count):
            block = rows_of(group)
            outs[0][group * block.shape[0] : (group + 1) * block.shape[0]] = block
        return
    to_beside, to_across, beside_low, across_top, own = outs
    half = own.shape[0] // 2
    block = rows_of(place_ref[0] ^ 3)
    to_beside[:half] = block[:half]
    to_across[:half] = block[half:]
    block = rows_of(place_ref[0] ^ 1)
    to_beside[half:] = block[:half]
    beside_low[...] = block[half:]
    block = rows_of(place_ref[0] ^ 2)
    to_across[half:] = block[half:]
    across_top[...] = block[:half]
    own[...] = rows_of(place_ref[0])


def part_shapes(rows, columns, square):
    if not square:
        return [jax.ShapeDtypeStruct((rows, columns), bf16)]
    own = rows // 4
    return [
        jax.ShapeDtypeStruct((each, columns), bf16) for each in (own, own, own // 2, own // 2, own)
    ]


def turn_back_kernel(count, place_ref, grad_ref, cosine_ref, sine_ref, unit_ref, by_tokens_ref, *refs):
    outs, low = refs[:-1], refs[-1]
    heads, blocks, _, head_dim, rows = grad_ref.shape
    half = head_dim // 2
    for block in range(blocks):
        span = slice(block * rows, (block + 1) * rows)
        cosine, sine = cosine_ref[:, span], sine_ref[:, span]
        for kind in range(3):
            for head in range(heads):
                at = (kind * heads + head) * head_dim
                grad = grad_ref[head, block, kind]
                if kind < 2:
                    grad = grad.astype(f32)
                    upper, lower = grad[:half], grad[half:]
                    grad = jnp.concatenate(
                        [upper * cosine + lower * sine, lower * cosine - upper * sine]
                    ).astype(bf16)
                low[at : at + head_dim, span] = grad
        by_tokens_ref[block] = low[:, span].T
    each = unit_ref.shape[1] // count

    def rows_of(group):
        start = group * each if isinstance(group, int) else pl.multiple_of(group * each, each)
        return contract(unit_ref[:, pl.ds(start, each)], low[...], 0, 1).astype(bf16)

    write_parts(place_ref, count, rows_of, outs)


def turn_back(grad, cosine, sine, unit_group, place, count, square):
    heads, blocks, _, head_dim, rows = grad.shape
    columns = 3 * heads * head_dim
    shapes = part_shapes(unit_group.shape[1], columns, square)
    by_tokens, *parts = pl.pallas_call(
        functools.partial(turn_back_kernel, count),
        out_shape=[jax.ShapeDtypeStruct((blocks, rows, columns), bf16), *shapes],
        in_specs=[IN_SMEM] + [IN_VMEM] * 4,
        out_specs=[IN_VMEM] * (1 + len(shapes)),
        scratch_shapes=[pltpu.VMEM((columns, blocks * rows), bf16)],
        compiler_params=pltpu.CompilerParams(vmem_limit_bytes=48 * 2**20),
        cost_estimate=lasting(8),
        name="turn_back",
    )(place, grad, cosine, sine, unit_group)
    return by_tokens, parts


def norm_kernel(count, table, starts_ref, spots_ref, by_tokens_ref, *refs):
    pieces, outs, (weight, semaphores) = refs[:count], refs[count:-2], refs[-2:]
    copies = start_pieces(pieces, table, starts_ref, weight, semaphores)
    rows = by_tokens_ref.shape[1]
    steps = len(outs) - 1
    for copy in copies:
        copy.wait()
    width = weight.shape[0]
    cut = min(1024, width)
    for step in range(steps):
        tokens = jnp.concatenate(
            [by_tokens_ref[spots_ref[2 * step]], by_tokens_ref[spots_ref[2 * step + 1]]]
        )
        for start in range(0, width, cut):
            part = contract(tokens, weight[start : start + cut], 1, 1)
            outs[step][:, start : start + cut] = part[:rows]
            outs[steps][step, :, start : start + cut] = part[rows:].astype(bf16)


def back_to_norm(by_tokens, pieces, table, starts, spots, width):
    _, rows, columns = by_tokens.shape
    steps = spots.shape[0] // 2
    made = pl.pallas_call(
        functools.partial(norm_kernel, len(pieces), table),
        out_shape=(jax.ShapeDtypeStruct((rows, width), f32),) * steps
        + (jax.ShapeDtypeStruct((steps, rows, width), bf16),),
        in_specs=[IN_SMEM] * 2 + [IN_VMEM] + [ANYWHERE] * len(pieces),
        out_specs=(IN_VMEM,) * (steps + 1),
        scratch_shapes=[
            pltpu.VMEM((width, columns), bf16),
            pltpu.SemaphoreType.DMA((len(table),)),
        ],
        compiler_params=pltpu.CompilerParams(vmem_limit_bytes=48 * 2**20),
        cost_estimate=lasting(7),
        name="back_to_norm",
    )(starts, spots, by_tokens, *pieces)
    return made[:steps], made[steps]


def weight_sums_kernel(
    sums_ref, out_sums_ref, weight_ref, gain_ref, qkv_ref, out_ref, one_ref, two_ref
):
    parts, rows, _ = sums_ref.shape
    kinds = 3
    width = out_ref.shape[1]
    features = width // parts
    gain = gain_ref[...]
    one = jnp.zeros((rows, 128), f32)
    two = jnp.zeros((rows, 128), f32)
    for part in range(parts):
        for kind in range(kinds):
            total = sums_ref[part, :, kind * features : (kind + 1) * features].astype(f32)
            at = slice(kind * width + part * features, kind * width + (part + 1) * features)
            qkv_ref[:, at] = gain * total
            product = total * weight_ref[:, at].astype(f32)
            for lanes in range(0, features, 128):
                one = one + product[:, lanes : lanes + 128]
        out_ref[:, part * features : (part + 1) * features] = out_sums_ref[
            part, :, :features
        ].astype(f32)
        two = two + out_sums_ref[part, :, features:].astype(f32)
    one_ref[...] = jnp.sum(one, axis=1, keepdims=True)
    two_ref[...] = jnp.sum(two, axis=1, keepdims=True)


def weight_sums(sums, out_sums, attn_qkv, gain):
    parts, rows, columns = sums.shape
    width = parts * columns // 3
    qkv, out, one, two = pl.pallas_call(
        weight_sums_kernel,
        out_shape=(
            jax.ShapeDtypeStruct((rows, 3 * width), f32),
            jax.ShapeDtypeStruct((rows, width), f32),
            jax.ShapeDtypeStruct((rows, 1), f32),
            jax.ShapeDtypeStruct((rows, 1), f32),
        ),
        in_specs=[IN_VMEM] * 4,
        out_specs=(IN_VMEM,) * 4,
        compiler_params=pltpu.CompilerParams(vmem_limit_bytes=32 * 2**20),
        cost_estimate=lasting(3),
        name="weight_sums",
    )(sums, out_sums, attn_qkv, gain)
    return qkv, out, one[:, 0], two[:, 0]


def out_product_kernel(spots_ref, attended_ref, gain_ref, *refs):
    blocks, (out_ref, grads, attended) = refs[:-3], refs[-3:]
    heads, _, head_dim, rows = attended_ref.shape
    width = grads.shape[1]
    for number, block in enumerate(blocks):
        grads[pl.ds(pl.multiple_of(spots_ref[number] * rows, rows), rows), :] = block[...]
        for head in range(heads):
            attended[
                head * head_dim : (head + 1) * head_dim, number * rows : (number + 1) * rows
            ] = attended_ref[head, number]
    columns = heads * head_dim
    out_ref[:, :columns] = contract(grads[...], attended[...], 0, 1).astype(bf16)
    gain = jnp.broadcast_to(gain_ref[...], (128, width)).T
    high = gain.astype(bf16).astype(f32)
    lanes = lax.broadcasted_iota(jnp.int32, gain.shape, 1)
    gain = jnp.where(lanes == 0, high, jnp.where(lanes == 1, gain - high, 0.0))
    out_ref[:, columns:] = gain.astype(bf16)


def out_product(blocks, spots, attended, gain):
    rows, width = blocks[0].shape
    heads, count, head_dim, _ = attended.shape
    return pl.pallas_call(
        out_product_kernel,
        out_shape=jax.ShapeDtypeStruct((width, heads * head_dim + 128), bf16),
        in_specs=[IN_SMEM] + [IN_VMEM] * (2 + len(blocks)),
        out_specs=IN_VMEM,
        scratch_shapes=[
            pltpu.VMEM((count * rows, width), bf16),
            pltpu.VMEM((heads * head_dim, count * rows), bf16),
        ],
        compiler_params=pltpu.CompilerParams(vmem_limit_bytes=48 * 2**20),
        cost_estimate=lasting(5),
        name="out_product",
    )(spots, attended, gain, *blocks)


def units_kernel(counts, tables, own_ref, other_ref, grad_own_ref, grad_other_ref, *refs):
    starts_refs, refs = refs[:3], refs[3:]
    pieces = (refs[: counts[0]], refs[counts[0] : sum(counts[:2])], refs[sum(counts[:2]) : sum(counts)])
    outs, weights, semaphores = refs[-15:-6], refs[-6:-3], refs[-3:]
    act_ref, grad_gate_ref, grad_up_ref, normed_ref, grads_ref = outs[:5]
    branch_keep_ref, branch_send_ref, keep_ref, send_ref = outs[5:]
    rows, width = own_ref.shape
    copies = [
        start_pieces(*each) for each in zip(pieces, tables, starts_refs, weights, semaphores)
    ]
    gate_w, up_w, down_w = weights

    def arrived(which):
        for copy in copies[which]:
            copy.wait()

    normed_ref[0, :rows] = own_ref[...]
    normed_ref[0, rows:] = other_ref[...]
    grads_ref[0, :rows] = grad_own_ref[...]
    grads_ref[0, rows:] = grad_other_ref[...]
    arrived(0)
    gate = contract(normed_ref[0], gate_w[...], 1, 1)
    sigmoid = 1.0 / (1.0 + jnp.exp(-gate))
    silu = gate * sigmoid
    arrived(1)
    up = contract(normed_ref[0], up_w[...], 1, 1)
    act_ref[0] = (silu * up).astype(bf16)
    arrived(2)
    grad_act = contract(grads_ref[0], down_w[...], 1, 1)
    grad_gate_ref[0] = (grad_act * up * sigmoid * (1.0 + gate * (1.0 - sigmoid))).astype(bf16)
    grad_up_ref[0] = (grad_act * silu).astype(bf16)
    cut = min(512, width)
    for start in range(0, width, cut):
        span = slice(start, start + cut)
        part = contract(grad_gate_ref[0], gate_w[:, span], 1, 0)
        part = part + contract(grad_up_ref[0], up_w[:, span], 1, 0)
        keep_ref[:, span] = part[:rows]
        send_ref[:, span] = part[rows:].astype(bf16)
    for start in range(0, width, cut):
        span = slice(start, start + cut)
        part = contract(act_ref[0], down_w[:, span], 1, 0)
        branch_keep_ref[0, :, span] = part[:rows]
        branch_send_ref[0, :, span] = part[rows:].astype(bf16)


def units_chunk(step, count, own, other, grad_own, grad_other, weights, held):
    rows, width = own.shape
    arrays = [array for pieces, _, _ in weights for array in pieces]
    counts = tuple(len(pieces) for pieces, _, _ in weights)
    tables = tuple(table for _, table, _ in weights)
    units = sum(entry[2] for entry in tables[0])
    whole = pl.BlockSpec((rows, width), lambda i: (0, 0))
    kept_units = pl.BlockSpec((1, 2 * rows, units), lambda i: (step, 0, 0))
    kept_rows = pl.BlockSpec((1, 2 * rows, width), lambda i: (step, 0, 0))
    by_units = jax.ShapeDtypeStruct((count, 2 * rows, units), bf16)
    by_rows = jax.ShapeDtypeStruct((count, 2 * rows, width), bf16)
    sums = tuple(jax.ShapeDtypeStruct((rows, width), kind) for kind in (f32, bf16))
    kept_branch = pl.BlockSpec((1, rows, width), lambda i: (step, 0, 0))
    branch = tuple(jax.ShapeDtypeStruct((count, rows, width), kind) for kind in (f32, bf16))
    return pl.pallas_call(
        functools.partial(units_kernel, counts, tables),
        grid=(1,),
        out_shape=(by_units,) * 3 + (by_rows,) * 2 + branch + sums,
        in_specs=[whole] * 4 + [IN_SMEM] * 3 + [ANYWHERE] * (len(arrays) + len(held)),
        out_specs=(kept_units,) * 3 + (kept_rows,) * 2 + (kept_branch,) * 2 + (whole,) * 2,
        scratch_shapes=[pltpu.VMEM((units, width), bf16)] * 3
        + [pltpu.SemaphoreType.DMA((len(table),)) for table in tables],
        input_output_aliases={7 + len(arrays) + i: i for i in range(len(held))},
        compiler_params=pltpu.CompilerParams(vmem_limit_bytes=56 * 2**20),
        cost_estimate=lasting(13),
        name="units_chunk",
    )(own, other, grad_own, grad_other, *[starts for _, _, starts in weights], *arrays, *held)


def transposed_product_kernel(left_ref, right_ref, *refs):
    refs[-1][...] = contract(left_ref[...], right_ref[...], 0, 0).astype(bf16)


def transposed_product(left, right, held=(), place=0, count=1):
    depth, units = left.shape
    width = right.shape[1]
    cut = min(256, units)
    return pl.pallas_call(
        transposed_product_kernel,
        grid=(units // cut,),
        out_shape=jax.ShapeDtypeStruct((units, count * width), bf16),
        in_specs=[
            pl.BlockSpec((depth, cut), lambda i: (0, i)),
            pl.BlockSpec((depth, width), lambda i: (0, 0)),
        ]
        + [ANYWHERE] * len(held),
        out_specs=pl.BlockSpec((cut, width), lambda i: (i, place)),
        input_output_aliases={2 + i: 0 for i in range(len(held))},
        compiler_params=pltpu.CompilerParams(vmem_limit_bytes=48 * 2**20),
        cost_estimate=lasting(9),
        name="transposed_product",
    )(left, right, *held)


def product_parts_kernel(count, place_ref, left_ref, right_ref, *outs):
    each = left_ref.shape[1] // count

    def rows_of(group):
        start = group * each if isinstance(group, int) else pl.multiple_of(group * each, each)
        return contract(left_ref[:, pl.ds(start, each)], right_ref[...], 0, 0).astype(bf16)

    write_parts(place_ref, count, rows_of, outs)


def product_parts(left, right, place, count, square):
    shapes = part_shapes(left.shape[1], right.shape[1], square)
    return pl.pallas_call(
        functools.partial(product_parts_kernel, count),
        out_shape=shapes,
        in_specs=[IN_SMEM] + [IN_VMEM] * 2,
        out_specs=[IN_VMEM] * len(shapes),
        compiler_params=pltpu.CompilerParams(vmem_limit_bytes=48 * 2**20),
        cost_estimate=lasting(10),
        name="product_parts",
    )(place, left, right)


def rotary_tables(positions, head_dim):
    half_dim = head_dim // 2
    frequency = rope_base ** (-(jnp.arange(half_dim, dtype=f32) * 2.0) / head_dim)
    angles = positions.astype(f32)[None, :] * frequency[:, None]
    return jnp.cos(angles), jnp.sin(angles)


def together(*arrays):
    return lax.optimization_barrier(arrays)


def after(array, *others):
    return lax.optimization_barrier((array, *others))[0]


def swap_cores(array):
    return lax.ppermute(array, "c", [(0, 1), (1, 0)])


def from_next(array):
    count = lax.axis_size("z")
    return lax.ppermute(array, "z", [(i, (i - 1) % count) for i in range(count)])


def from_flipped(array, bit):
    return lax.ppermute(array, "p", [(i, i ^ bit) for i in range(4)])


def square_groups():
    return lax.axis_size("p") == 4 and lax.axis_size("r") == 1


def gather_chunks(block):
    count = lax.axis_size("z")
    chunks = []
    for step in range(count):
        later = from_next(block) if step < count - 1 else None
        chunks.append((block, swap_cores(block)))
        block = later
    return chunks


def add_over_cores(keep, send):
    return keep + swap_cores(send.astype(bf16)).astype(f32)


def near_pieces(block):
    if not square_groups():
        return lax.all_gather(block, GROUPS, axis=0)
    return block, from_flipped(block, 1), from_flipped(block, 2)


def group_pieces(near):
    if not square_groups():
        return [(near[group], group, 0) for group in range(near.shape[0])]
    block, beside, across = near
    half = block.shape[0] // 2
    place = lax.axis_index("p")
    top, low = from_flipped(beside[:half], 2), from_flipped(across[half:], 1)
    return [
        (block, place, 0), (beside, place ^ 1, 0), (across, place ^ 2, 0),
        (top, place ^ 3, 0), (low, place ^ 3, half),
    ]


def placed(pieces, rows):
    table = tuple((which, 0, piece[0].shape[0]) for which, piece in enumerate(pieces))
    starts = [jnp.int32(group) * rows + first for _, group, first in pieces]
    return [array for array, _, _ in pieces], table, jnp.stack(starts).astype(jnp.int32)


def group_parts(whole):
    if not square_groups():
        return [whole]
    parts = whole.reshape(4, -1, whole.shape[1])
    place = lax.axis_index("p")
    own, beside, across, corner = (
        lax.dynamic_index_in_dim(parts, place ^ bits, 0, keepdims=False) for bits in range(4)
    )
    half = own.shape[0] // 2
    return [
        jnp.concatenate([corner[:half], beside[:half]]),
        jnp.concatenate([corner[half:], across[half:]]),
        beside[half:], across[:half], own,
    ]


def scatter_first(parts):
    if not square_groups():
        return ()
    return from_flipped(parts[0], 1), from_flipped(parts[1], 2)


def scatter_second(parts, first):
    if not square_groups():
        own = lax.psum_scatter(parts[0], GROUPS, scatter_dimension=0, tiled=True)
        return own.astype(f32)
    _, _, beside_low, across_top, own = parts
    half = own.shape[0] // 2
    from_beside, from_across = (array.astype(f32) for array in first)
    beside_low = (beside_low.astype(f32) + from_across[:half]).astype(bf16)
    across_top = (across_top.astype(f32) + from_beside[:half]).astype(bf16)
    total_low = from_across[half:] + from_flipped(beside_low, 1).astype(f32)
    total_top = from_beside[half:] + from_flipped(across_top, 2).astype(f32)
    return own.astype(f32) + jnp.concatenate([total_top, total_low])


def to_owners(own):
    count = lax.axis_size(TENSOR)
    return lax.all_to_all(own.astype(bf16).reshape(count, -1, own.shape[1]), TENSOR, 0, 0)


def shards(tokens, attn_qkv, attn_out_t, mlp_weight, norm1, norm2, cotangent):
    rows, width = tokens.shape
    group_count, share_count = lax.axis_size("p"), lax.axis_size("r")
    line_count = lax.axis_size("z")
    tensor_count = lax.axis_size("c") * line_count
    head_dim = width // HEADS
    heads_here = HEADS // tensor_count
    group_rows = rows * tensor_count
    features_here = heads_here * head_dim
    weight_rows = attn_qkv.shape[0]
    share, place, core = lax.axis_index("r"), lax.axis_index("z"), lax.axis_index("c")
    block = min(1024, group_rows)
    x = tokens.astype(f32)
    gain_one = norm1.astype(f32)[:, None]
    device_index = (share * group_count + lax.axis_index("p")) * tensor_count

    def chunk_places(step):
        along = lax.rem(place + step, line_count)
        return core * line_count + along, (1 - core) * line_count + along

    x_group = lax.all_gather(tokens, TENSOR, axis=0, tiled=True)
    scaled_qkv = (attn_qkv.astype(f32) * gain_one).astype(bf16)
    qkv_cut = scaled_qkv.reshape(weight_rows, 3, tensor_count, features_here).transpose(2, 0, 1, 3)
    qkv_cut = qkv_cut.reshape(tensor_count, weight_rows, 3 * features_here)
    gain_columns = jnp.pad(norm2[:, None], ((0, 0), (0, 127)))
    out_near = near_pieces(jnp.concatenate([attn_out_t, gain_columns], axis=1))
    gate_near = near_pieces(mlp_weight[:, :width])
    unit_rows = mlp_weight.shape[0]
    qkv_part = lax.all_to_all(qkv_cut, TENSOR, 0, 0).reshape(-1, 3 * features_here)
    qkv_part, out_near, gate_near = together(qkv_part, out_near, gate_near)
    qkv_rows = qkv_part.shape[0]
    qkv_arrays, qkv_table, qkv_starts = placed(group_pieces(near_pieces(qkv_part)), qkv_rows)
    out_pieces = group_pieces(out_near)
    out_plane = jnp.concatenate([array for array, _, _ in out_pieces])
    qkv_arrays, x_group, gate_near, out_plane = together(
        qkv_arrays, x_group, gate_near, out_plane
    )

    positions = device_index * rows + jnp.arange(group_rows)
    cosine, sine = rotary_tables(positions, head_dim)
    unit_group, stacked = project(
        x_group, cosine, sine, qkv_arrays, qkv_table, qkv_starts, heads_here, head_dim, rows
    )
    gate_weight = placed(group_pieces(gate_near), unit_rows)
    stacked, gate_arrays, later = together(stacked, gate_weight[0], from_next(out_plane))
    gate_weight = (gate_arrays, *gate_weight[1:])
    out_ring = [out_plane, later]
    swapped = [swap_cores(array) for array in after(out_ring, stacked)]
    qkv = lax.all_to_all(stacked, "p", 0, 0)
    qkv, later, swapped = together(qkv, from_next(out_ring[-1]), swapped)
    qkv = qkv.reshape(-1, 3, head_dim, rows)
    out_ring.append(later)
    rest_whole = lax.all_gather(
        after(mlp_weight[:, width:], qkv_arrays), GROUPS, axis=0, tiled=True
    )
    up_weight, down_weight = (
        ([rest_whole], ((0, 0, rest_whole.shape[0], column),), jnp.zeros((1,), jnp.int32))
        for column in (0, width)
    )

    def over_shares(array):
        return lax.all_gather(array, "r", axis=0, tiled=True) if share_count > 1 else array

    def own_share(array):
        if share_count == 1:
            return array
        pieces = group_count * tensor_count
        return lax.dynamic_slice_in_dim(array, share * pieces, pieces, 0)

    qkv = over_shares(qkv)
    rest = [out_ring[-1]]
    for _ in range(line_count - 3):
        rest.append(from_next(rest[-1]))
    swapped.append(swap_cores(out_ring[-1]))
    attended, logsum = attend_forward(qkv, block)
    attended, rest, swapped = together(attended, rest[1:], swapped)
    out_ring += rest
    swapped += [swap_cores(array) for array in rest]
    attended_head = own_share(attended)

    out_table, out_starts = [], []
    for which in range(2 * line_count):
        side = core if which < line_count else 1 - core
        along = lax.rem(place + which % line_count, line_count)
        first = 0
        for array, group, offset in out_pieces:
            out_table.append((which, first, array.shape[0]))
            spot = (jnp.int32(group) * 2 + side) * line_count + along
            out_starts.append(spot * weight_rows + offset)
            first += array.shape[0]
    out_table, out_starts = tuple(out_table), jnp.stack(out_starts).astype(jnp.int32)

    attended_local = lax.all_to_all(attended_head, ("p", "c", "z"), 0, 0)
    later = from_next(after(cotangent, attended))
    attended_local, swapped = together(attended_local, swapped)
    out_weight = (out_ring + swapped, out_table, out_starts)
    grad_out_ring = [cotangent, later, from_next(after(later, attended_local))]
    middle, normed_two, gain_two = finish_attention(
        tokens, attended_local, *out_weight, HEADS // tensor_count
    )
    normed_two, grad_out_ring = together(normed_two, grad_out_ring)
    attended_group = attended_head.reshape(group_count, tensor_count, head_dim, rows)
    attended_group = lax.all_to_all(after(attended_group, normed_two), "p", 0, 0)

    held = ()
    normed, grad_out, came, total = normed_two, grad_out_ring[0], (), None
    for step in range(line_count):
        later = from_next(normed) if step < line_count - 1 else ()
        if step < line_count - 3:
            grad_out_ring.append(from_next(grad_out_ring[-1]))
        if step >= 2:
            came = from_next(total.astype(bf16))
        *held, keep, send = units_chunk(
            step, line_count, normed, swap_cores(normed), grad_out, swap_cores(grad_out),
            (gate_weight, up_weight, down_weight), held,
        )
        if step == 0:
            later, attended_group, keep, send = together(later, attended_group, keep, send)
        else:
            later, came, keep, send = together(later, came, keep, send)
        keep, grad_out_ring = together(keep, grad_out_ring)
        part = add_over_cores(keep, send)
        normed = later
        if step < line_count - 1:
            grad_out = grad_out_ring[step + 1]
        if step == 0:
            own_part = part
        else:
            total = part if step == 1 else came.astype(f32) + part
    activation, gate_grads, up_grads, normed_group, grad_out_group = (
        array.reshape(group_rows, -1) for array in held[:5]
    )
    branch_keep, branch_send = held[5:]

    def over_groups(part):
        return lax.psum_scatter(part, GROUPS, scatter_dimension=0, tiled=True)

    gate_term = transposed_product(after(gate_grads, total), normed_group)
    came, gate_term = together(from_next(total.astype(bf16)), gate_term)
    grad_normed = came.astype(f32) + own_part
    grad_middle, grad_mid_low, norm_two_part, grad_attended = back_to_attention(
        middle, grad_normed, cotangent, gain_two, *out_weight,
        HEADS // tensor_count, head_dim,
    )
    grad_head = lax.all_to_all(grad_attended, ("p", "c", "z"), 0, 0)
    up_term = transposed_product(after(up_grads, grad_attended), normed_group)
    group_place = lax.axis_index("p").astype(jnp.int32)[None]
    group_all = share_count * group_count
    branch_came = swap_cores(after(branch_send, grad_attended))
    grad_head, up_term, branch_came = together(grad_head, up_term, branch_came)

    def branch_sum(came, step):
        return came + branch_keep[step] + branch_came[step].astype(f32)

    grad_head = over_shares(grad_head)
    grad_gate_w, grad_up_w = over_groups(gate_term), over_groups(up_term)
    count = qkv.shape[0] * rows // block
    backward = functools.partial(attend_backward, qkv, grad_head, attended, logsum, block)
    later_keys = backward(count // 2, count)
    grad_mid_ring = [grad_mid_low, from_next(after(grad_mid_low, grad_head))]
    mid_swapped = [swap_cores(after(grad_mid_low, grad_head))]
    later_keys, grad_mid_ring, mid_swapped = together(later_keys, grad_mid_ring, mid_swapped)
    grad_qkv_head = backward(0, count // 2, later_keys)[0]
    mid_swapped += [swap_cores(array) for array in grad_mid_ring[1:]]
    for _ in range(line_count - 3):
        grad_mid_ring.append(from_next(grad_mid_ring[-1]))
    came = from_next(after(branch_sum(0.0, 1 % line_count).astype(bf16), later_keys))
    grad_qkv_head, grad_mid_ring, came, mid_swapped, grad_gate_w = together(
        grad_qkv_head, grad_mid_ring, came, mid_swapped, grad_gate_w
    )
    grad_qkv_head = own_share(grad_qkv_head)

    spots = jnp.stack([spot for step in range(line_count) for spot in chunk_places(step)])
    spots = spots.astype(jnp.int32)
    grad_qkv_rows = grad_qkv_head.reshape(group_count, tensor_count, 3, head_dim, rows)
    grad_qkv_rows = lax.all_to_all(grad_qkv_rows, "p", 0, 0)
    mid_swapped += [swap_cores(array) for array in grad_mid_ring[2:]]
    grad_mid_ring.append(from_next(grad_mid_ring[-1]))
    for step in range(2, line_count - 1):
        came = from_next(branch_sum(came.astype(f32), step).astype(bf16))
    grad_qkv_rows, mid_swapped = together(grad_qkv_rows, mid_swapped)
    grad_qkv_low, qkv_parts = turn_back(
        grad_qkv_rows, cosine, sine, unit_group, group_place, group_all, square_groups()
    )
    grad_qkv_low, qkv_parts, grad_mid_ring, came = together(
        grad_qkv_low, qkv_parts, grad_mid_ring, came
    )
    qkv_first = scatter_first(qkv_parts)
    branch_last = branch_sum(came.astype(f32), line_count - 1) if line_count > 2 else came
    branch_last = from_next(branch_last.astype(bf16))
    keep, send = back_to_norm(
        grad_qkv_low, qkv_arrays, qkv_table, qkv_starts, spots, width
    )
    keep, send, branch_last, qkv_first = together(keep, send, branch_last, qkv_first)
    swapped = swap_cores(send)
    total = keep[1 % line_count] + swapped[1 % line_count].astype(f32)
    came = from_next(total.astype(bf16))
    mid_swapped.append(swap_cores(after(grad_mid_ring[-1], total)))
    grad_mid_blocks = [
        part for pair in zip(grad_mid_ring, mid_swapped, strict=True) for part in pair
    ]
    out_term = out_product(grad_mid_blocks, spots, attended_group, norm_two_part)
    down_parts = product_parts(
        after(activation, total), grad_out_group, group_place, group_all, square_groups()
    )
    qkv_own = scatter_second(qkv_parts, after(qkv_first, total)).astype(bf16)
    came, qkv_own, out_term, down_parts, grad_up_w = together(
        came, qkv_own, out_term, down_parts, grad_up_w
    )
    qkv_sums = to_owners(qkv_own)
    total = came.astype(f32) + keep[2 % line_count] + swapped[2 % line_count].astype(f32)
    came = from_next(total.astype(bf16))
    out_parts = group_parts(out_term)
    out_first = scatter_first(out_parts)
    down_first = scatter_first(down_parts)
    came, out_first = together(came, out_first)
    for step in range(3, line_count):
        total = came.astype(f32) + keep[step] + swapped[step].astype(f32)
        came = from_next(total.astype(bf16))
    out_own = scatter_second(out_parts, out_first)
    came, down_first, out_own, qkv_sums = together(came, down_first, out_own, qkv_sums)
    out_sums = to_owners(out_own)
    weighted_one = came.astype(f32) + keep[0] + swapped[0].astype(f32)
    grad_down_w = scatter_second(down_parts, down_first)
    grad_mlp = jnp.concatenate(
        [grad_gate_w.astype(f32), grad_up_w.astype(f32), grad_down_w.astype(f32)], axis=1
    )
    result = (middle + branch_sum(branch_last.astype(f32), 0)).astype(bf16)
    factor_one = lax.rsqrt(jnp.mean(x * x, axis=-1, keepdims=True) + epsilon)
    grad_tokens = (
        grad_middle
        + factor_one * weighted_one
        - x * factor_one**3 * jnp.mean(weighted_one * x, axis=-1, keepdims=True)
    )
    grad_qkv, grad_out_w, grad_norm_one, grad_norm_two = weight_sums(
        qkv_sums, out_sums, attn_qkv, gain_one
    )
    return (result, grad_tokens, grad_qkv, grad_out_w, grad_mlp, grad_norm_one, grad_norm_two)


def solution(mesh):
    seq_count, fsdp_count = mesh.shape["seq"], mesh.shape["fsdp"]
    groups = seq_count // 2
    heads_here = HEADS // (2 * fsdp_count)
    dealt = min(groups, heads_here)
    fine = Mesh(mesh.devices.reshape(groups // dealt, dealt, 2, fsdp_count), ALL)
    by_rows, by_items = P(ALL, None), P(ALL)
    in_specs = (by_rows, by_rows, by_rows, by_rows, by_items, by_items, by_rows)
    out_specs = (by_rows, by_rows, by_rows, by_rows, by_rows, by_items, by_items)
    return jax.shard_map(shards, mesh=fine, in_specs=in_specs, out_specs=out_specs, check_vma=False)
```
